512 devices in a mesh: slide: 16 (over z_lo, core), seq: 32 (over y, x, z_hi).
Axes of the slice: x: 4, y: 4, z: 16 (z_hi: 2, z_lo: 8; z = z_hi * 8 + z_lo), core: 2. Of those that a mesh axis runs over, the one named last changes fastest.
Arguments:
- ctx_in: bfloat16 [16, 6144, 1536], P('slide', 'seq'), may hold values from -6 to 6
- resid: bfloat16 [16, 6144, 1536], P('slide', 'seq'), may hold values from -6 to 6
- enc_out_w: bfloat16 [1536, 1536], P(None, 'seq'), may hold values from -0.15625 to 0.15625
- slide_proj: bfloat16 [1536, 768], P(None, 'seq'), may hold values from -0.15625 to 0.15625
- qkv_w: bfloat16 [768, 2304], P(None, 'seq'), may hold values from -0.75 to 0.75
- tissue: int32 [16, 32, 192], P('slide', 'seq'), may hold values from 0 to 191, each once within a row
- kept_count: int32 [16, 32], P('slide'), may hold values from 64 to 192, as said below
- dilation: int32 [16, 2], P('slide'), may hold values from 4 to 64, as said below
Outputs:
- slide_out: bfloat16 [16, 6144, 768], P('slide', 'seq')
The draws below stay inside these ranges and needn't reach their ends.
Inputs may be any that keep to these rules, and one draw needn't show every extreme that they name: `kept_count`: for every slide the counts sum to 4096, and for every block b the counts of blocks 0 to b together exceed (b + 1) * 128 by 0 to 64, by 0 for the last block. `dilation`: column 0 is a local segment length from a quarter of 64 to 64; column 1 is a rate of 4, 8 or 16.
All inputs are finite; a program needn't handle non-finite values.
Results may differ from the reference program's by a relative error of at most 0.009.
Values may be sent and summed in bfloat16 or wider, within the bound.
No kernel may reach another device: no remote copies, remote signals or barrier semaphores. Data moves between devices by JAX's collectives and lax.ppermute only.
A program may use at most 64 MiB of HBM per device.

```python
import math
import jax
import jax.numpy as jnp
from jax import lax

D_ENC = 1536
D = 768
HEADS = 16
HEAD_DIM = 48
KEPT_DEV = 128
HALF = 64
TILE_DEV = 192
RATE_MIN = 4
SLIDES = 16
SEQ_LEN = 4096
TILES = 6144
N_SEQ = 32


def draw_kept_count(key, part):
    key = jax.random.fold_in(key, 11)
    pick_key, spill_key = jax.random.split(key)
    spill_rows = jax.random.randint(spill_key, (SLIDES, N_SEQ), 0, HALF + 1)
    peak_rank = jax.random.randint(pick_key, (SLIDES, 1), 0, N_SEQ - 1)
    rank_ids = jnp.arange(N_SEQ, dtype=jnp.int32)[None, :]
    spill_rows = jnp.where(rank_ids == peak_rank, HALF, spill_rows)
    spill_rows = jnp.where((rank_ids == peak_rank - 1) | (rank_ids == peak_rank + 1), 0, spill_rows)
    spill_rows = jnp.where(rank_ids == N_SEQ - 1, 0, spill_rows)
    before = jnp.concatenate([jnp.zeros((SLIDES, 1), jnp.int32), spill_rows[:, :-1]], axis=1)
    return (KEPT_DEV + spill_rows - before).astype(jnp.int32)


def draw_dilation(key, part):
    key = jax.random.fold_in(key, 23)
    span_key, rate_key, order_key = jax.random.split(key, 3)
    spans = jax.random.randint(span_key, (SLIDES,), HALF // 4, HALF + 1)
    powers = jax.random.randint(rate_key, (SLIDES,), 0, 3)
    order_slides = jax.random.permutation(order_key, SLIDES)
    spans = spans.at[order_slides[0]].set(HALF).at[order_slides[1]].set(HALF // 4)
    powers = powers.at[order_slides[0]].set(0).at[order_slides[1]].set(2)
    rates = jnp.where(powers == 0, 4, jnp.where(powers == 1, 8, 16))
    return jnp.stack([spans, rates], axis=1).astype(jnp.int32)


def draw_qkv_w(key, part):
    key = jax.random.fold_in(key, 37)
    first_key, second_key, third_key = jax.random.split(key, 3)
    key_part = jax.random.normal(first_key, (D, D), jnp.float32) / math.sqrt(D)
    query_part = jax.random.normal(second_key, (D, D), jnp.float32) / math.sqrt(D)
    value_part = jax.random.normal(third_key, (D, D), jnp.float32) / math.sqrt(D)
    joined = jnp.concatenate([query_part, key_part, value_part], axis=1)
    return jnp.clip(joined, -0.75, 0.75).astype(jnp.bfloat16)


def level_of(own_key, extent, pieces, smallest, top_value):
    level, own = 1.0, jax.random.fold_in(own_key, 6)
    for axis_at, blocks in pieces:
        draws = jnp.exp(jax.random.uniform(jax.random.fold_in(own, axis_at), (blocks,), jnp.float32, smallest / len(pieces), top_value / len(pieces)))
        level = level * jnp.repeat(draws, extent[axis_at] // blocks).reshape([-1 if axis == axis_at else 1 for axis in range(len(extent))])
    return level


def scatter_about(rng, shape, width, limit, cuts=(), held_as=jnp.bfloat16):
    level = level_of(rng, shape, cuts, -0.22, 0.18) if cuts else 1.0
    drawn = jax.random.normal(rng, shape, jnp.float32) * width * level
    return jnp.minimum(jnp.maximum(drawn, -limit), limit).astype(held_as)


def setup_inputs(seed: int = 0) -> dict:
    key_of = jax.random.split(jax.random.key(seed), 9)
    return {
        "ctx_in": scatter_about(key_of[0], (SLIDES, TILES, D_ENC), 1.0, 6.0, ((0, 16), (1, 32))),
        "resid": scatter_about(key_of[1], (SLIDES, TILES, D_ENC), 1.0, 6.0, ((0, 16), (1, 32))),
        "enc_out_w": scatter_about(key_of[2], (D_ENC, D_ENC), D_ENC ** -0.5, 0.15625, ((1, 32),)),
        "slide_proj": scatter_about(key_of[3], (D_ENC, D), D_ENC ** -0.5, 0.15625, ((1, 32),)),
        "qkv_w": draw_qkv_w(jax.random.fold_in(key_of[8], 71), 0),
        "tissue": jax.vmap(lambda own: jax.random.permutation(own, TILE_DEV))(jax.random.split(key_of[5], SLIDES * N_SEQ)).reshape((SLIDES, N_SEQ, TILE_DEV)).astype(jnp.int32),
        "kept_count": draw_kept_count(jax.random.fold_in(key_of[8], 71), 0),
        "dilation": draw_dilation(jax.random.fold_in(key_of[8], 71), 0),
    }


NORM_EPS = 1e-06
BIG_NEGATIVE = -1e+30

def norm_rows(values):
    center = values - lax.optimization_barrier(jnp.mean(values, axis=-1, keepdims=True))
    spread = lax.optimization_barrier(jnp.mean(center * center, axis=-1, keepdims=True))
    return center * lax.rsqrt(spread + NORM_EPS)

def dilated_slide_attention(blended_output, segment_length, dilation_rate):
    score_scale = HEAD_DIM ** (-0.5)
    queries = blended_output[:, :D].reshape(SEQ_LEN, HEADS, HEAD_DIM).astype(jnp.float32)
    keys_all = blended_output[:, D:2 * D].reshape(SEQ_LEN, HEADS, HEAD_DIM).astype(jnp.float32)
    values_all = blended_output[:, 2 * D:].reshape(SEQ_LEN, HEADS, HEAD_DIM).astype(jnp.float32)
    positions = jnp.arange(SEQ_LEN, dtype=jnp.int32)
    head_numbers = jnp.arange(HEADS, dtype=jnp.int32)
    padding = jnp.zeros((HALF, HEADS, HEAD_DIM), jnp.float32)
    keys_wide = jnp.concatenate([padding, keys_all, padding], axis=0)
    values_wide = jnp.concatenate([padding, values_all, padding], axis=0)
    window_ids = jnp.arange(KEPT_DEV + 2 * HALF, dtype=jnp.int32)
    block_rows = jnp.arange(KEPT_DEV, dtype=jnp.int32)

    def local_block(block_index):
        first_pos = block_index * KEPT_DEV
        query_blk = lax.dynamic_slice_in_dim(queries, first_pos, KEPT_DEV, 0)
        key_blk = lax.dynamic_slice_in_dim(keys_wide, first_pos, KEPT_DEV + 2 * HALF, 0)
        value_blk = lax.dynamic_slice_in_dim(values_wide, first_pos, KEPT_DEV + 2 * HALF, 0)
        query_pos = first_pos + block_rows
        key_pos = first_pos - HALF + window_ids
        key_ok = (key_pos >= 0) & (key_pos < SEQ_LEN)
        allowed = ((query_pos // segment_length)[:, None] == (key_pos // segment_length)[None, :]) & key_ok[None, :]
        scores = jnp.einsum('qhd,khd->qhk', query_blk, key_blk) * score_scale
        local_best = lax.optimization_barrier(jnp.max(jnp.where(allowed[:, None, :], scores, BIG_NEGATIVE), axis=-1))
        weights = jnp.where(allowed[:, None, :], jnp.exp(scores - local_best[..., None]), 0.0)
        local_total = lax.optimization_barrier(jnp.sum(weights, axis=-1))
        rounded = lax.optimization_barrier(weights.astype(jnp.bfloat16)).astype(jnp.float32)
        summed = jnp.einsum('qhk,khd->qhd', rounded, value_blk)
        return (local_best, local_total, summed)
    local_best, local_total, local_sum = lax.map(local_block, jnp.arange(N_SEQ, dtype=jnp.int32))
    local_best = local_best.reshape(SEQ_LEN, HEADS)
    local_total = local_total.reshape(SEQ_LEN, HEADS)
    local_sum = local_sum.reshape(SEQ_LEN, HEADS, HEAD_DIM)
    place_total = SEQ_LEN // RATE_MIN
    leading_offset = jnp.mod(head_numbers, dilation_rate)
    lattice_rows = leading_offset[None, :] + dilation_rate * jnp.arange(place_total, dtype=jnp.int32)[:, None]
    grid_ok = lattice_rows < SEQ_LEN
    grid_safe = jnp.broadcast_to(jnp.minimum(lattice_rows, SEQ_LEN - 1)[:, :, None], (place_total, HEADS, HEAD_DIM))
    grid_q = jnp.take_along_axis(queries, grid_safe, axis=0)
    grid_k = jnp.take_along_axis(keys_all, grid_safe, axis=0)
    grid_v = jnp.take_along_axis(values_all, grid_safe, axis=0)
    scores_g = jnp.einsum('ahd,bhd->ahb', grid_q, grid_k) * score_scale
    usable = grid_ok[:, :, None] & jnp.transpose(grid_ok)[None, :, :]
    glob_best = lax.optimization_barrier(jnp.max(jnp.where(usable, scores_g, BIG_NEGATIVE), axis=-1))
    weights_g = jnp.where(usable, jnp.exp(scores_g - glob_best[..., None]), 0.0)
    glob_total = lax.optimization_barrier(jnp.sum(weights_g, axis=-1))
    glob_sum = jnp.einsum('ahb,bhd->ahd', weights_g, grid_v, precision=lax.Precision.HIGHEST)
    shift_amount = positions[:, None] - leading_offset[None, :]
    inside_lattice = (shift_amount >= 0) & (jnp.mod(shift_amount, dilation_rate) == 0)
    lattice_slot = jnp.clip(shift_amount // dilation_rate, 0, place_total - 1).astype(jnp.int32)
    row_best = jnp.where(inside_lattice, jnp.take_along_axis(glob_best, lattice_slot, axis=0), BIG_NEGATIVE)
    row_total = jnp.where(inside_lattice, jnp.take_along_axis(glob_total, lattice_slot, axis=0), 0.0)
    slot_wide = jnp.broadcast_to(lattice_slot[:, :, None], (SEQ_LEN, HEADS, HEAD_DIM))
    row_sum = jnp.where(inside_lattice[:, :, None], jnp.take_along_axis(glob_sum, slot_wide, axis=0), 0.0)
    joint_best = jnp.maximum(local_best, row_best)
    near_factor = jnp.exp(local_best - joint_best)
    far_factor = jnp.exp(row_best - joint_best)
    numerator = near_factor[..., None] * local_sum + far_factor[..., None] * row_sum
    denominator = near_factor * local_total + far_factor * row_total
    return (numerator / denominator[..., None]).reshape(SEQ_LEN, D).astype(jnp.bfloat16)

def slide_forward(ctx_slide, resid_slide, enc_out_w, slide_proj, qkv_w, tissue_slide, count_slide, dilation_slide):
    counts = count_slide.astype(jnp.int32)
    starts = (jnp.cumsum(counts) - counts).astype(jnp.int32)
    place_numbers = jnp.arange(TILE_DEV, dtype=jnp.int32)
    block_ids = jnp.arange(N_SEQ, dtype=jnp.int32)
    kept_mask = place_numbers[None, :] < counts[:, None]
    positions = jnp.where(kept_mask, starts[:, None] + place_numbers[None, :], SEQ_LEN).astype(jnp.int32)
    tile_ids = (block_ids[:, None] * TILE_DEV + tissue_slide).astype(jnp.int32)
    seq_tile = jnp.zeros((SEQ_LEN,), jnp.int32).at[positions.reshape(-1)].set(tile_ids.reshape(-1), mode='drop')
    ctx_rows = jnp.take(ctx_slide, seq_tile, axis=0)
    resid_rows = jnp.take(resid_slide, seq_tile, axis=0)
    hidden = resid_rows.astype(jnp.float32) + jnp.dot(ctx_rows, enc_out_w, preferred_element_type=jnp.float32)
    normed = norm_rows(hidden).astype(jnp.bfloat16)
    embedded = jnp.dot(normed, slide_proj, preferred_element_type=jnp.float32).astype(jnp.bfloat16)
    blended_output = jnp.dot(embedded, qkv_w, preferred_element_type=jnp.float32).astype(jnp.bfloat16)
    attended = dilated_slide_attention(blended_output, dilation_slide[0], dilation_slide[1])
    return jnp.zeros((TILES, D), jnp.bfloat16).at[seq_tile].set(attended)

def reference(ctx_in, resid, enc_out_w, slide_proj, qkv_w, tissue, kept_count, dilation):

    def one_slide(slide_index):
        return slide_forward(ctx_in[slide_index], resid[slide_index], enc_out_w, slide_proj, qkv_w, tissue[slide_index], kept_count[slide_index], dilation[slide_index])
    return lax.map(one_slide, jnp.arange(SLIDES, dtype=jnp.int32))
```

```python
import jax
import jax.numpy as jnp
from jax import lax
from jax.sharding import Mesh, PartitionSpec as P

HEADS = 16
HEAD_DIM = 48
D = 768
HALF = 64
RATE_MIN = 4
TILE_DEV = 192
SEQ_LEN = 4096
WINDOW = 384
KEY_SLOTS = 80
QUERY_SLOTS = 48
LANES = 128
PLANE = ("y", "x")
NORM_EPS = 1e-06
BIG_NEGATIVE = -1e30
SCALE = HEAD_DIM**-0.5


def dot_nt(a, b):
    return lax.dot_general(a, b, (((1,), (1,)), ((), ())), preferred_element_type=jnp.float32)


def mirrored(x):
    z_low = lax.axis_size("zlo")
    pairs = [
        (low * 2 + high, (z_low - 1 - low) * 2 + (1 - high))
        for low in range(z_low)
        for high in range(2)
    ]
    return lax.ppermute(x, ("zlo", "zhi"), pairs)


def across(x):
    return lax.ppermute(x, "zhi", [(0, 1), (1, 0)])


def both_halves(x, high):
    other = mirrored(x)
    return jnp.where(high == 0, jnp.stack([x, other]), jnp.stack([other, x]))


def gather_weight(x, high):
    pair = both_halves(x, high).reshape(2 * x.shape[0], x.shape[1])
    plane = lax.all_gather(pair, PLANE, axis=0, tiled=True)
    return lax.all_gather(plane, "core", axis=0, tiled=False)


def on_device(ctx_in, resid, enc_out_w, slide_proj, qkv_w, tissue, kept_count, dilation):
    core = lax.axis_index("core")
    high = lax.axis_index("zhi")
    plane_id = lax.axis_index("y") * lax.axis_size("x") + lax.axis_index("x")
    block_id = plane_id * 2 + high
    seg_len, rate = dilation[0, 0], dilation[0, 1]
    counts = kept_count[0]
    starts = jnp.cumsum(counts) - counts
    pair_counts = counts.reshape(-1, 2).sum(axis=1)
    pair_starts = starts.reshape(-1, 2)[:, 0]

    def pick(table, index):
        return jnp.sum(jnp.where(jnp.arange(table.shape[0]) == index, table, 0))

    count_me, start_me = pick(counts, block_id), pick(starts, block_id)
    count_other, start_other = pick(counts, block_id + 1 - 2 * high), pick(starts, block_id + 1 - 2 * high)
    pair_start, pair_count = pick(pair_starts, plane_id), pick(pair_counts, plane_id)
    base = jnp.where(high == 0, pair_start - HALF, pair_start)

    w_own = lax.dynamic_slice_in_dim(enc_out_w, core * D, D, 0).T
    p_own = lax.dynamic_slice_in_dim(slide_proj, core * D, D, 0).T
    q_own = lax.dynamic_slice_in_dim(qkv_w, core * (D // 2), D // 2, 0).T
    w_all = gather_weight(w_own, high)
    p_all = gather_weight(p_own, high)
    q_all = gather_weight(q_own, high)

    listing = tissue[0, 0]
    own_ctx = jnp.take(ctx_in[0], listing, axis=0)
    own_res = jnp.take(resid[0], listing, axis=0)
    hidden = own_res.astype(jnp.float32) + dot_nt(own_ctx[:, :D], w_all[0]) + dot_nt(own_ctx[:, D:], w_all[1])
    center = hidden - jnp.mean(hidden, axis=-1, keepdims=True)
    spread = jnp.mean(center * center, axis=-1, keepdims=True)
    normed = (center * lax.rsqrt(spread + NORM_EPS)).astype(jnp.bfloat16)
    embedded = (dot_nt(normed[:, :D], p_all[0]) + dot_nt(normed[:, D:], p_all[1])).astype(jnp.bfloat16)

    partner = across(embedded)
    rim_from = jnp.where(high == 0, count_other - HALF, 0)
    rim = lax.dynamic_slice_in_dim(partner, rim_from, HALF, 0)
    planes = lax.axis_size("y") * lax.axis_size("x")
    halo_pairs = [(p * 2, p * 2 + 2) for p in range(planes - 1)]
    halo_pairs += [(p * 2 + 1, p * 2 - 1) for p in range(1, planes)]
    halo = lax.ppermute(rim, ("y", "x", "zhi"), halo_pairs)

    rows = jnp.arange(TILE_DEV, dtype=jnp.int32)
    rim_rows = jnp.arange(HALF, dtype=jnp.int32)
    window = jnp.arange(WINDOW, dtype=jnp.int32)
    live = rows < count_me
    place_to = jnp.concatenate(
        [
            jnp.where(live, start_me - base + rows, -1),
            jnp.where(rows < count_other, start_other - base + rows, -1),
            rim_rows + jnp.where(high == 0, 0, pair_count),
        ]
    )
    place = (window[:, None] == place_to[None, :]).astype(jnp.bfloat16)
    sources = jnp.concatenate([embedded, partner, halo], axis=0)
    spanned = jnp.dot(place, sources, preferred_element_type=jnp.float32).astype(jnp.bfloat16)

    half = D // 2
    q_rows = (
        dot_nt(q_all[0, :D], embedded[:, :half]) + dot_nt(q_all[1, :D], embedded[:, half:])
    ).astype(jnp.bfloat16).reshape(HEADS, HEAD_DIM, TILE_DEV)
    kv_rows = (
        dot_nt(q_all[0, D:], spanned[:, :half]) + dot_nt(q_all[1, D:], spanned[:, half:])
    ).astype(jnp.bfloat16)
    keys = kv_rows[:D].reshape(HEADS, HEAD_DIM, WINDOW)
    vals = kv_rows[D:].reshape(HEADS, HEAD_DIM, WINDOW)

    heads = jnp.arange(HEADS, dtype=jnp.int32)
    key_slots = jnp.arange(KEY_SLOTS, dtype=jnp.int32)
    query_slots = jnp.arange(QUERY_SLOTS, dtype=jnp.int32)
    key_phase = jnp.mod(heads - pair_start, rate)
    query_phase = jnp.mod(heads - start_me, rate)
    key_lane = pair_start - base + key_phase[:, None] + rate * key_slots[None, :]
    key_pick = (key_lane[:, :, None] == window[None, None, :]).astype(jnp.bfloat16)
    query_row = query_phase[:, None] + rate * query_slots[None, :]
    query_pick = (query_row[:, :, None] == rows[None, None, :]).astype(jnp.bfloat16)
    kv_heads = jnp.concatenate(
        [keys, vals, jnp.zeros((HEADS, LANES - 2 * HEAD_DIM, WINDOW), jnp.bfloat16)], axis=1
    )
    q_heads = jnp.concatenate(
        [q_rows, jnp.zeros((HEADS, LANES - HEAD_DIM, TILE_DEV), jnp.bfloat16)], axis=1
    )
    payload = jnp.concatenate(
        [
            jnp.einsum("hsw,hfw->hsf", key_pick, kv_heads, preferred_element_type=jnp.float32),
            jnp.einsum("hsw,hfw->hsf", query_pick, q_heads, preferred_element_type=jnp.float32),
        ],
        axis=1,
    ).astype(jnp.bfloat16)
    arrived = lax.all_to_all(payload, PLANE, 0, 0)
    far_kv = arrived[:, :KEY_SLOTS].reshape(-1, LANES)
    far_q = arrived[:, KEY_SLOTS:].reshape(-1, LANES)
    far_phase = jnp.mod(plane_id - pair_starts, rate)
    far_live = (far_phase[:, None] + rate * key_slots[None, :] < pair_counts[:, None]).reshape(-1, 1)
    far_scores = jnp.where(far_live, dot_nt(far_kv, far_q) * SCALE, BIG_NEGATIVE)
    far_best = jnp.max(far_scores, axis=0, keepdims=True)
    far_weights = jnp.where(far_live, jnp.exp(far_scores - far_best), 0.0)
    far_total = jnp.sum(far_weights, axis=0)
    far_sum = jnp.einsum(
        "kq,kd->qd", far_weights.astype(jnp.bfloat16), far_kv, preferred_element_type=jnp.float32
    )[:, HEAD_DIM : 2 * HEAD_DIM]
    far_log = far_best[0] + jnp.log(far_total)
    log_a = lax.reduce_precision(far_log, 8, 7)
    log_b = lax.reduce_precision(far_log - log_a, 8, 7)
    log_c = lax.reduce_precision(far_log - log_a - log_b, 8, 7)
    answer = jnp.concatenate(
        [
            far_sum / far_total[:, None],
            jnp.stack([log_a, log_b, log_c], axis=1),
            jnp.zeros((far_q.shape[0], LANES - HEAD_DIM - 3), jnp.float32),
        ],
        axis=1,
    ).astype(jnp.bfloat16)
    answers = lax.all_to_all(answer.reshape(-1, QUERY_SLOTS, LANES), PLANE, 0, 0)

    key_pos = base + window
    key_ok = (key_pos >= 0) & (key_pos < SEQ_LEN)
    query_pos = start_me + rows
    allowed = (key_pos // seg_len)[:, None] == (query_pos // seg_len)[None, :]
    allowed = (allowed & key_ok[:, None])[None]
    scores = jnp.einsum("hdk,hdq->hkq", keys, q_rows, preferred_element_type=jnp.float32) * SCALE
    local_best = jnp.max(jnp.where(allowed, scores, BIG_NEGATIVE), axis=1)
    weights = jnp.where(allowed, jnp.exp(scores - local_best[:, None]), 0.0)
    local_total = jnp.sum(weights, axis=1)
    local_sum = jnp.einsum(
        "hdk,hkq->hdq", vals, weights.astype(jnp.bfloat16), preferred_element_type=jnp.float32
    )

    spread_rows = jnp.einsum("hsf,hsr->hfr", answers, query_pick, preferred_element_type=jnp.float32)
    shift = rows[None, :] - query_phase[:, None]
    inside = (shift >= 0) & (jnp.mod(shift, rate) == 0)
    row_log = spread_rows[:, HEAD_DIM] + spread_rows[:, HEAD_DIM + 1] + spread_rows[:, HEAD_DIM + 2]
    row_log = jnp.where(inside, row_log, BIG_NEGATIVE)
    joint = jnp.maximum(local_best, row_log)
    near = jnp.exp(local_best - joint)
    far = jnp.exp(row_log - joint)
    below = jnp.where(live[None], near * local_total + far, 1.0)
    attended = (near[:, None] * local_sum + far[:, None] * spread_rows[:, :HEAD_DIM]) / below[:, None]
    attended = jnp.where(live[None, None], attended, 0.0).astype(jnp.bfloat16).reshape(D, TILE_DEV)
    back = (listing[None, :] == rows[:, None]).astype(jnp.bfloat16)
    return dot_nt(back, attended).astype(jnp.bfloat16)[None]


def solution(mesh):
    devices = mesh.devices.reshape(-1, 2, 4, 4, 2)
    split = Mesh(devices, ("zlo", "core", "y", "x", "zhi"))
    slide, seq = ("zlo", "core"), ("y", "x", "zhi")
    return jax.shard_map(
        on_device,
        mesh=split,
        in_specs=(
            P(slide, seq, None),
            P(slide, seq, None),
            P(None, seq),
            P(None, seq),
            P(None, seq),
            P(slide, seq, None),
            P(slide, None),
            P(slide, None),
        ),
        out_specs=P(slide, seq, None),
        check_vma=False,
    )
```

```python
import functools

import jax
import jax.numpy as jnp
from jax import lax
from jax.experimental import pallas as pl
from jax.experimental.pallas import tpu as pltpu
from jax.sharding import Mesh, PartitionSpec as P

HEADS = 16
HEAD_DIM = 48
D = 768
D_ENC = 1536
HALF = 64
TILE_DEV = 192
SEQ_LEN = 4096
WINDOW = 384
KEY_SLOTS = 80
QUERY_SLOTS = 48
LANES = 128
W_ROWS = 48
P_ROWS = 24
Q_ROWS = 72
PLANES = 16
PLANE = ("y", "x")
NORM_EPS = 1e-06
BIG_NEGATIVE = -1e30
SCALE = HEAD_DIM**-0.5
BF16 = jnp.bfloat16
F32 = jnp.float32
I32 = jnp.int32
VMEM_LIMIT = 48 * 1024 * 1024

CORE, HIGH, RATE, START_ME, COUNT_ME, START_OTHER, COUNT_OTHER, PAIR_START, PAIR_COUNT, BASE = range(10)
ALL_STARTS = 16
ALL_COUNTS = 32


def dot_nn(a, b):
    return lax.dot_general(a, b, (((1,), (0,)), ((), ())), preferred_element_type=F32)


def dot_nt(a, b):
    return lax.dot_general(a, b, (((1,), (1,)), ((), ())), preferred_element_type=F32)


def dot_tn(a, b):
    return lax.dot_general(a, b, (((0,), (0,)), ((), ())), preferred_element_type=F32)


def iota(shape, dim):
    return lax.broadcasted_iota(I32, shape, dim)


def embed_kernel(table, ctx, res, near_a, near_b, far_a, far_b, out, w, p, hidden, normed, sems):
    core, high = table[CORE], table[HIGH]
    loads = [
        pltpu.make_async_copy(near_a, w.at[core, :, high], sems.at[0]),
        pltpu.make_async_copy(near_b, w.at[1 - core, :, high], sems.at[1]),
        pltpu.make_async_copy(far_a.at[:, :W_ROWS], w.at[core, :, 1 - high], sems.at[2]),
        pltpu.make_async_copy(far_b.at[:, :W_ROWS], w.at[1 - core, :, 1 - high], sems.at[3]),
        pltpu.make_async_copy(far_a.at[:, W_ROWS:], p.at[core], sems.at[4]),
        pltpu.make_async_copy(far_b.at[:, W_ROWS:], p.at[1 - core], sems.at[5]),
    ]
    for load in loads:
        load.start()
    for load in loads[:4]:
        load.wait()
    group = 4
    width = group * 2 * W_ROWS
    total = jnp.zeros((TILE_DEV, 1), F32)
    for n in range(PLANES // group):
        columns = slice(n * width, (n + 1) * width)
        part = res[:, columns].astype(F32)
        for half in range(2):
            block = w[half, n * group : (n + 1) * group].reshape(width, D)
            part += dot_nt(ctx[:, half * D : (half + 1) * D], block)
        hidden[:, columns] = part
        total += jnp.sum(part, axis=1, keepdims=True)
    center = hidden[...] - total / D_ENC
    spread = jnp.sum(center * center, axis=1, keepdims=True) / D_ENC
    normed[...] = (center * lax.rsqrt(spread + NORM_EPS)).astype(BF16)
    for load in loads[4:]:
        load.wait()
    for n in range(2):
        rows = slice(n * PLANES // 2, (n + 1) * PLANES // 2)
        part = dot_nt(normed[:, :D], p[0, rows].reshape(D // 2, D))
        part += dot_nt(normed[:, D:], p[1, rows].reshape(D // 2, D))
        out[:, n * D // 2 : (n + 1) * D // 2] = part.astype(BF16)


def embed(table, ctx, res, near_a, near_b, far_a, far_b):
    vmem = pl.BlockSpec(memory_space=pltpu.VMEM)
    hbm = pl.BlockSpec(memory_space=pl.ANY)
    return pl.pallas_call(
        embed_kernel,
        out_shape=jax.ShapeDtypeStruct((TILE_DEV, D), BF16),
        in_specs=[pl.BlockSpec(memory_space=pltpu.SMEM), vmem, vmem, hbm, hbm, hbm, hbm],
        out_specs=vmem,
        scratch_shapes=[
            pltpu.VMEM((2, PLANES, 2, W_ROWS, D), BF16),
            pltpu.VMEM((2, PLANES, 2 * P_ROWS, D), BF16),
            pltpu.VMEM((TILE_DEV, D_ENC), F32),
            pltpu.VMEM((TILE_DEV, D_ENC), BF16),
            pltpu.SemaphoreType.DMA((6,)),
        ],
        compiler_params=pltpu.CompilerParams(vmem_limit_bytes=VMEM_LIMIT),
        cost_estimate=pl.CostEstimate(flops=1_400_000_000, bytes_accessed=9_000_000, transcendentals=0),
        name="embed_rows",
    )(table, ctx, res, near_a, near_b, far_a, far_b)


def project_kernel(table, own, partner, halo, qa, qb, payload, q_out, kv_out, spanned):
    core, rate, base = table[CORE], table[RATE], table[BASE]

    def placed(first, count, length):
        lane = iota((WINDOW, length), 1)
        hit = (iota((WINDOW, length), 0) == lane + first) & (lane < count)
        return hit.astype(BF16)

    spread = dot_nn(placed(table[START_ME] - base, table[COUNT_ME], TILE_DEV), own[...])
    spread += dot_nn(placed(table[START_OTHER] - base, table[COUNT_OTHER], TILE_DEV), partner[...])
    halo_at = jnp.where(table[HIGH] == 0, 0, table[PAIR_COUNT])
    spread += dot_nn(placed(halo_at, HALF, HALF), halo[...])
    spanned[...] = spread.astype(BF16)
    half = D // 2
    lanes_a = pl.ds(pl.multiple_of(core * half, LANES), half)
    lanes_b = pl.ds(pl.multiple_of((1 - core) * half, LANES), half)
    own_a, own_b = own[:, lanes_a], own[:, lanes_b]
    q_out[...] = (dot_nt(qa[:D], own_a) + dot_nt(qb[:D], own_b)).astype(BF16)
    span_a, span_b = spanned[:, lanes_a], spanned[:, lanes_b]
    for n in range(2):
        rows = slice((n + 1) * D, (n + 2) * D)
        kv_out[n * D : (n + 1) * D] = (dot_nt(qa[rows], span_a) + dot_nt(qb[rows], span_b)).astype(BF16)
    key_slot = iota((KEY_SLOTS, WINDOW), 0) * rate
    key_lane = iota((KEY_SLOTS, WINDOW), 1)
    query_slot = iota((QUERY_SLOTS, TILE_DEV), 0) * rate
    query_lane = iota((QUERY_SLOTS, TILE_DEV), 1)
    key_rest = jnp.zeros((LANES - 2 * HEAD_DIM, WINDOW), BF16)
    query_rest = jnp.zeros((LANES - HEAD_DIM, TILE_DEV), BF16)
    for h in range(HEADS):
        rows = slice(h * HEAD_DIM, (h + 1) * HEAD_DIM)
        key_first = table[PAIR_START] - base + ((h - table[PAIR_START]) & (rate - 1))
        key_pick = (key_lane == key_slot + key_first).astype(BF16)
        both = jnp.concatenate([kv_out[rows], kv_out[D + h * HEAD_DIM : D + (h + 1) * HEAD_DIM], key_rest], axis=0)
        payload[h, :KEY_SLOTS] = dot_nt(key_pick, both).astype(BF16)
        query_first = (h - table[START_ME]) & (rate - 1)
        query_pick = (query_lane == query_slot + query_first).astype(BF16)
        ask = jnp.concatenate([q_out[rows], query_rest], axis=0)
        payload[h, KEY_SLOTS:] = dot_nt(query_pick, ask).astype(BF16)


def project(table, own, partner, halo, qa, qb):
    vmem = pl.BlockSpec(memory_space=pltpu.VMEM)
    return pl.pallas_call(
        project_kernel,
        out_shape=(
            jax.ShapeDtypeStruct((HEADS, KEY_SLOTS + QUERY_SLOTS, LANES), BF16),
            jax.ShapeDtypeStruct((D, TILE_DEV), BF16),
            jax.ShapeDtypeStruct((2 * D, WINDOW), BF16),
        ),
        in_specs=[pl.BlockSpec(memory_space=pltpu.SMEM)] + [vmem] * 5,
        out_specs=(vmem, vmem, vmem),
        scratch_shapes=[pltpu.VMEM((WINDOW, D), BF16)],
        compiler_params=pltpu.CompilerParams(vmem_limit_bytes=VMEM_LIMIT),
        cost_estimate=pl.CostEstimate(flops=2_000_000_000, bytes_accessed=6_000_000, transcendentals=0),
        name="project_rows",
    )(table, own, partner, halo, qa, qb)


def local_kernel(q, kv, key_seg, query_seg, out_sum, out_best, out_total):
    allowed = key_seg[...] == query_seg[...]
    for h in range(HEADS):
        rows = slice(h * HEAD_DIM, (h + 1) * HEAD_DIM)
        scores = dot_tn(kv[rows], q[rows]) * SCALE
        scores = jnp.where(allowed, scores, BIG_NEGATIVE)
        best = jnp.max(scores, axis=0, keepdims=True)
        weights = jnp.exp(scores - best)
        out_best[h : h + 1] = best
        out_total[h : h + 1] = jnp.sum(weights, axis=0, keepdims=True)
        out_sum[rows] = dot_nn(kv[D + h * HEAD_DIM : D + (h + 1) * HEAD_DIM], weights.astype(BF16))


def local_branch(q, kv, key_seg, query_seg):
    vmem = pl.BlockSpec(memory_space=pltpu.VMEM)
    stat = jax.ShapeDtypeStruct((HEADS, TILE_DEV), F32)
    return pl.pallas_call(
        local_kernel,
        out_shape=(jax.ShapeDtypeStruct((D, TILE_DEV), F32), stat, stat),
        in_specs=[vmem] * 4,
        out_specs=(vmem, vmem, vmem),
        compiler_params=pltpu.CompilerParams(vmem_limit_bytes=VMEM_LIMIT),
        cost_estimate=pl.CostEstimate(flops=300_000_000, bytes_accessed=3_000_000, transcendentals=1_200_000),
        name="local_branch",
    )(q, kv, key_seg, query_seg)


def far_kernel(table, plane, arrived, answer, scores):
    rate = table[RATE]
    kv = arrived[:, :KEY_SLOTS].reshape(PLANES * KEY_SLOTS, LANES)
    group = 8
    width = group * QUERY_SLOTS
    slot = iota((KEY_SLOTS, width), 0) * rate
    for n in range(PLANES // group):
        asks = arrived[n * group : (n + 1) * group, KEY_SLOTS:].reshape(width, LANES)
        best = jnp.full((1, width), BIG_NEGATIVE, F32)
        for p in range(PLANES):
            phase = (plane[0] - table[ALL_STARTS + p]) & (rate - 1)
            piece = dot_nt(arrived[p, :KEY_SLOTS], asks) * SCALE
            piece = jnp.where(slot + phase < table[ALL_COUNTS + p], piece, BIG_NEGATIVE)
            scores[p * KEY_SLOTS : (p + 1) * KEY_SLOTS] = piece
            best = jnp.maximum(best, jnp.max(piece, axis=0, keepdims=True))
        weights = jnp.exp(scores[...] - best)
        total = jnp.sum(weights, axis=0, keepdims=True)
        summed = dot_tn(kv, weights.astype(BF16))
        shared = summed[HEAD_DIM : 2 * HEAD_DIM] / total
        log_all = best + jnp.log(total)
        log_a = log_all.astype(BF16).astype(F32)
        log_b = (log_all - log_a).astype(BF16).astype(F32)
        log_c = log_all - log_a - log_b
        row = iota((LANES - HEAD_DIM, width), 0)
        tail = jnp.where(row == 0, log_a, jnp.where(row == 1, log_b, jnp.where(row == 2, log_c, 0.0)))
        block = jnp.concatenate([shared, tail], axis=0)
        answer[n * group : (n + 1) * group] = block.T.astype(BF16).reshape(group, QUERY_SLOTS, LANES)


def far_branch(table, plane, arrived):
    vmem, smem = pl.BlockSpec(memory_space=pltpu.VMEM), pl.BlockSpec(memory_space=pltpu.SMEM)
    return pl.pallas_call(
        far_kernel,
        out_shape=jax.ShapeDtypeStruct((PLANES, QUERY_SLOTS, LANES), BF16),
        in_specs=[smem, smem, vmem],
        out_specs=vmem,
        scratch_shapes=[pltpu.VMEM((PLANES * KEY_SLOTS, PLANES // 2 * QUERY_SLOTS), F32)],
        compiler_params=pltpu.CompilerParams(vmem_limit_bytes=VMEM_LIMIT),
        cost_estimate=pl.CostEstimate(flops=500_000_000, bytes_accessed=1_000_000, transcendentals=1_000_000),
        name="far_branch",
    )(table, plane, arrived)


def finish_kernel(table, answers, local_sum, local_best, local_total, listing, out, attended):
    rate = table[RATE]
    slot = iota((QUERY_SLOTS, TILE_DEV), 0) * rate
    lane = iota((QUERY_SLOTS, TILE_DEV), 1)
    row = iota((1, TILE_DEV), 1)
    live = row < table[COUNT_ME]
    for h in range(HEADS):
        rows = slice(h * HEAD_DIM, (h + 1) * HEAD_DIM)
        phase = (h - table[START_ME]) & (rate - 1)
        pick = (lane == slot + phase).astype(BF16)
        wide = dot_tn(answers[h], pick)
        log_all = wide[HEAD_DIM : HEAD_DIM + 1] + wide[HEAD_DIM + 1 : HEAD_DIM + 2] + wide[HEAD_DIM + 2 : HEAD_DIM + 3]
        log_all = jnp.where((row & (rate - 1)) == phase, log_all, BIG_NEGATIVE)
        best = local_best[h : h + 1]
        joint = jnp.maximum(best, log_all)
        near = jnp.exp(best - joint)
        far = jnp.exp(log_all - joint)
        below = jnp.where(live, near * local_total[h : h + 1] + far, 1.0)
        mixed = (near * local_sum[rows] + far * wide[:HEAD_DIM]) / below
        attended[rows] = jnp.where(live, mixed, 0.0).astype(BF16)
    back = (listing[...] == iota((TILE_DEV, TILE_DEV), 0)).astype(BF16)
    out[0] = dot_nt(back, attended[...]).astype(BF16)


def finish(table, answers, local_sum, local_best, local_total, listing):
    vmem = pl.BlockSpec(memory_space=pltpu.VMEM)
    return pl.pallas_call(
        finish_kernel,
        out_shape=jax.ShapeDtypeStruct((1, TILE_DEV, D), BF16),
        in_specs=[pl.BlockSpec(memory_space=pltpu.SMEM)] + [vmem] * 5,
        out_specs=vmem,
        scratch_shapes=[pltpu.VMEM((D, TILE_DEV), BF16)],
        compiler_params=pltpu.CompilerParams(vmem_limit_bytes=VMEM_LIMIT),
        cost_estimate=pl.CostEstimate(flops=100_000_000, bytes_accessed=1_500_000, transcendentals=10_000),
        name="finish_rows",
    )(table, answers, local_sum, local_best, local_total, listing)


def mirrored(x):
    z_low = lax.axis_size("zlo")
    pairs = [
        (low * 2 + high, (z_low - 1 - low) * 2 + (1 - high))
        for low in range(z_low)
        for high in range(2)
    ]
    return lax.ppermute(x, ("zlo", "zhi"), pairs)


def across(x):
    return lax.ppermute(x, "zhi", [(0, 1), (1, 0)])


def other_core(x):
    return lax.ppermute(x, "core", [(0, 1), (1, 0)])


def over_plane(x):
    return lax.all_to_all(jnp.broadcast_to(x[None], (PLANES,) + x.shape), PLANE, 0, 0)


def in_order(own, other, high):
    return jnp.where(high == 0, jnp.concatenate([own, other]), jnp.concatenate([other, own]))


def on_device(ctx_in, resid, enc_out_w, slide_proj, qkv_w, tissue, kept_count, dilation):
    core = lax.axis_index("core")
    high = lax.axis_index("zhi")
    plane_id = lax.axis_index("y") * lax.axis_size("x") + lax.axis_index("x")
    block_id = plane_id * 2 + high
    seg_len, rate = dilation[0, 0], dilation[0, 1]

    w_own = lax.dynamic_slice_in_dim(enc_out_w, core * D, D, 0).T
    p_own = lax.dynamic_slice_in_dim(slide_proj, core * D, D, 0).T
    q_own = lax.dynamic_slice_in_dim(qkv_w, core * (D // 2), D // 2, 0).T
    near_a = over_plane(w_own)
    w_other = mirrored(w_own)
    p_other = mirrored(p_own)
    q_other = mirrored(q_own)
    near_b = other_core(near_a)
    far_a = over_plane(jnp.concatenate([w_other, in_order(p_own, p_other, high)]))
    far_b = other_core(far_a)
    q_pair, far_a = lax.optimization_barrier((in_order(q_own, q_other, high), far_a))
    q_a = over_plane(q_pair)
    q_b = other_core(q_a)

    counts = kept_count[0]
    starts = jnp.cumsum(counts) - counts
    pair_counts = counts.reshape(-1, 2).sum(axis=1)
    pair_starts = starts.reshape(-1, 2)[:, 0]

    def pick(values, index):
        return jnp.sum(jnp.where(jnp.arange(values.shape[0]) == index, values, 0))

    other_id = block_id + 1 - 2 * high
    count_me, start_me = pick(counts, block_id), pick(starts, block_id)
    count_other, start_other = pick(counts, other_id), pick(starts, other_id)
    pair_start, pair_count = pick(pair_starts, plane_id), pick(pair_counts, plane_id)
    base = jnp.where(high == 0, pair_start - HALF, pair_start)
    scalars = [core, high, rate, start_me, count_me, start_other, count_other, pair_start, pair_count, base]
    table = jnp.concatenate(
        [
            jnp.stack([jnp.asarray(s, I32) for s in scalars]),
            jnp.zeros((ALL_STARTS - len(scalars),), I32),
            pair_starts.astype(I32),
            pair_counts.astype(I32),
        ]
    )

    listing = tissue[0, 0]
    own_ctx = jnp.take(ctx_in[0], listing, axis=0)
    own_res = jnp.take(resid[0], listing, axis=0)
    embedded = embed(table, own_ctx, own_res, near_a, near_b, far_a, far_b)

    partner = across(embedded)
    rim_from = jnp.where(high == 0, count_other - HALF, 0)
    rim = lax.dynamic_slice_in_dim(partner, rim_from, HALF, 0)
    halo_pairs = [(p * 2, p * 2 + 2) for p in range(PLANES - 1)]
    halo_pairs += [(p * 2 + 1, p * 2 - 1) for p in range(1, PLANES)]
    halo = lax.ppermute(rim, ("y", "x", "zhi"), halo_pairs)

    payload, q_rows, kv_rows = project(
        table, embedded, partner, halo, q_a.reshape(3 * D, D // 2), q_b.reshape(3 * D, D // 2)
    )
    arrived = lax.all_to_all(payload, PLANE, 0, 0)

    key_pos = base + jnp.arange(WINDOW, dtype=I32)
    key_ok = (key_pos >= 0) & (key_pos < SEQ_LEN)
    key_seg = jnp.where(key_ok, key_pos // seg_len, -1)[:, None]
    query_seg = ((start_me + jnp.arange(TILE_DEV, dtype=I32)) // seg_len)[None, :]
    local_sum, local_best, local_total = local_branch(q_rows, kv_rows, key_seg, query_seg)

    answer = far_branch(table, jnp.asarray(plane_id, I32).reshape(1), arrived)
    answers = lax.all_to_all(answer, PLANE, 0, 0)
    return finish(table, answers, local_sum, local_best, local_total, listing[None, :])


def solution(mesh):
    devices = mesh.devices.reshape(-1, 2, 4, 4, 2)
    split = Mesh(devices, ("zlo", "core", "y", "x", "zhi"))
    slide, seq = ("zlo", "core"), ("y", "x", "zhi")
    return jax.shard_map(
        on_device,
        mesh=split,
        in_specs=(
            P(slide, seq, None),
            P(slide, seq, None),
            P(None, seq),
            P(None, seq),
            P(None, seq),
            P(slide, seq, None),
            P(slide, None),
            P(slide, None),
        ),
        out_specs=P(slide, seq, None),
        check_vma=False,
    )
```

```python
import functools

import jax
import jax.numpy as jnp
from jax import lax
from jax.experimental import pallas as pl
from jax.experimental.pallas import tpu as pltpu
from jax.sharding import Mesh, PartitionSpec as P

HEADS = 16
HEAD_DIM = 48
D = 768
D_ENC = 1536
HALF = 64
TILE_DEV = 192
SEQ_LEN = 4096
WINDOW = 320
KEY_SLOTS = 80
QUERY_SLOTS = 48
LANES = 128
W_ROWS = 48
P_ROWS = 24
Q_ROWS = 72
PLANES = 16
PLANE = ("y", "x")
NORM_EPS = 1e-06
BIG_NEGATIVE = -1e30
SCALE = HEAD_DIM**-0.5
BF16 = jnp.bfloat16
F32 = jnp.float32
I32 = jnp.int32
VMEM_LIMIT = 48 * 1024 * 1024

CORE, HIGH, PLANE_ID, RATE, SEGMENT = range(5)
START_ME, COUNT_ME, START_OTHER, COUNT_OTHER, PAIR_START, PAIR_COUNT = range(5, 11)
ALL_STARTS = 16
ALL_COUNTS = 32


def dot_nn(a, b):
    return lax.dot_general(a, b, (((1,), (0,)), ((), ())), preferred_element_type=F32)


def dot_nt(a, b):
    return lax.dot_general(a, b, (((1,), (1,)), ((), ())), preferred_element_type=F32)


def dot_tn(a, b):
    return lax.dot_general(a, b, (((0,), (0,)), ((), ())), preferred_element_type=F32)


def iota(shape, dim):
    return lax.broadcasted_iota(I32, shape, dim)


def prepare_kernel(place, counts, dilation, ctx, res, listing, own_ctx, own_res, table):
    core, high, plane = place[0], place[1], place[2]
    table[CORE], table[HIGH], table[PLANE_ID] = core, high, plane
    table[SEGMENT], table[RATE] = dilation[0, 0], dilation[0, 1]
    start = jnp.int32(0)
    for p in range(PLANES):
        first, second = counts[0, 2 * p], counts[0, 2 * p + 1]
        table[ALL_STARTS + p] = start
        table[ALL_COUNTS + p] = first + second

        @pl.when(plane == p)
        def _(first=first, second=second, start=start):
            table[PAIR_START] = start
            table[PAIR_COUNT] = first + second
            table[COUNT_ME] = jnp.where(high == 0, first, second)
            table[COUNT_OTHER] = jnp.where(high == 0, second, first)
            table[START_ME] = jnp.where(high == 0, start, start + first)
            table[START_OTHER] = jnp.where(high == 0, start + first, start)

        start = start + first + second
    order = (iota((TILE_DEV, TILE_DEV), 0) == listing[0]).astype(BF16)
    own_ctx[...] = dot_tn(order, ctx[0]).astype(BF16)
    own_res[...] = dot_tn(order, res[0]).astype(BF16)


def prepare(place, counts, dilation, ctx, res, listing):
    vmem, smem = pl.BlockSpec(memory_space=pltpu.VMEM), pl.BlockSpec(memory_space=pltpu.SMEM)
    rows = jax.ShapeDtypeStruct((TILE_DEV, D_ENC), BF16)
    return pl.pallas_call(
        prepare_kernel,
        out_shape=(rows, rows, jax.ShapeDtypeStruct((ALL_COUNTS + PLANES,), I32)),
        in_specs=[smem, smem, smem, vmem, vmem, vmem],
        out_specs=(vmem, vmem, smem),
        compiler_params=pltpu.CompilerParams(vmem_limit_bytes=VMEM_LIMIT),
        cost_estimate=pl.CostEstimate(flops=250_000_000, bytes_accessed=2_400_000, transcendentals=0),
        name="prepare_rows",
    )(place, counts, dilation, ctx, res, listing)


def embed_kernel(table, ctx, res, near_a, near_b, far_a, far_b, out, w, p, hidden, normed, sems):
    core, high = table[CORE], table[HIGH]
    loads = [
        pltpu.make_async_copy(near_a, w.at[core, :, high], sems.at[0]),
        pltpu.make_async_copy(near_b, w.at[1 - core, :, high], sems.at[1]),
        pltpu.make_async_copy(far_a.at[:, :W_ROWS], w.at[core, :, 1 - high], sems.at[2]),
        pltpu.make_async_copy(far_b.at[:, :W_ROWS], w.at[1 - core, :, 1 - high], sems.at[3]),
        pltpu.make_async_copy(far_a.at[:, W_ROWS:], p.at[core], sems.at[4]),
        pltpu.make_async_copy(far_b.at[:, W_ROWS:], p.at[1 - core], sems.at[5]),
    ]
    for load in loads:
        load.start()
    for load in loads[:4]:
        load.wait()
    group = 4
    width = group * 2 * W_ROWS
    total = jnp.zeros((TILE_DEV, 1), F32)
    for n in range(PLANES // group):
        columns = slice(n * width, (n + 1) * width)
        part = res[:, columns].astype(F32)
        for half in range(2):
            block = w[half, n * group : (n + 1) * group].reshape(width, D)
            part += dot_nt(ctx[:, half * D : (half + 1) * D], block)
        hidden[:, columns] = part
        total += jnp.sum(part, axis=1, keepdims=True)
    center = hidden[...] - total / D_ENC
    spread = jnp.sum(center * center, axis=1, keepdims=True) / D_ENC
    normed[...] = (center * lax.rsqrt(spread + NORM_EPS)).astype(BF16)
    for load in loads[4:]:
        load.wait()
    for n in range(2):
        rows = slice(n * PLANES // 2, (n + 1) * PLANES // 2)
        part = dot_nt(normed[:, :D], p[0, rows].reshape(D // 2, D))
        part += dot_nt(normed[:, D:], p[1, rows].reshape(D // 2, D))
        out[:, n * D // 2 : (n + 1) * D // 2] = part.astype(BF16)


def embed(table, ctx, res, near_a, near_b, far_a, far_b):
    vmem = pl.BlockSpec(memory_space=pltpu.VMEM)
    hbm = pl.BlockSpec(memory_space=pl.ANY)
    return pl.pallas_call(
        embed_kernel,
        out_shape=jax.ShapeDtypeStruct((TILE_DEV, D), BF16),
        in_specs=[pl.BlockSpec(memory_space=pltpu.SMEM), vmem, vmem, hbm, hbm, hbm, hbm],
        out_specs=vmem,
        scratch_shapes=[
            pltpu.VMEM((2, PLANES, 2, W_ROWS, D), BF16),
            pltpu.VMEM((2, PLANES, 2 * P_ROWS, D), BF16),
            pltpu.VMEM((TILE_DEV, D_ENC), F32),
            pltpu.VMEM((TILE_DEV, D_ENC), BF16),
            pltpu.SemaphoreType.DMA((6,)),
        ],
        compiler_params=pltpu.CompilerParams(vmem_limit_bytes=VMEM_LIMIT),
        cost_estimate=pl.CostEstimate(flops=1_400_000_000, bytes_accessed=9_000_000, transcendentals=0),
        name="embed_rows",
    )(table, ctx, res, near_a, near_b, far_a, far_b)


def project_kernel(table, own, partner, qa, qb, payload, q_out, kv_out, spanned):
    core, rate, base = table[CORE], table[RATE], table[PAIR_START]

    def placed(first, count, length):
        lane = iota((WINDOW, length), 1)
        hit = (iota((WINDOW, length), 0) == lane + first) & (lane < count)
        return hit.astype(BF16)

    spread = dot_nn(placed(table[START_ME] - base, table[COUNT_ME], TILE_DEV), own[...])
    spread += dot_nn(placed(table[START_OTHER] - base, table[COUNT_OTHER], TILE_DEV), partner[...])
    spanned[...] = spread.astype(BF16)
    half = D // 2
    lanes_a = pl.ds(pl.multiple_of(core * half, LANES), half)
    lanes_b = pl.ds(pl.multiple_of((1 - core) * half, LANES), half)
    own_a, own_b = own[:, lanes_a], own[:, lanes_b]
    q_out[...] = (dot_nt(qa[:D], own_a) + dot_nt(qb[:D], own_b)).astype(BF16)
    span_a, span_b = spanned[:, lanes_a], spanned[:, lanes_b]
    for n in range(2):
        rows = slice((n + 1) * D, (n + 2) * D)
        kv_out[n * D : (n + 1) * D] = (dot_nt(qa[rows], span_a) + dot_nt(qb[rows], span_b)).astype(BF16)
    key_slot = iota((KEY_SLOTS, WINDOW), 0) * rate
    key_lane = iota((KEY_SLOTS, WINDOW), 1)
    query_slot = iota((QUERY_SLOTS, TILE_DEV), 0) * rate
    query_lane = iota((QUERY_SLOTS, TILE_DEV), 1)
    key_rest = jnp.zeros((LANES - 2 * HEAD_DIM, WINDOW), BF16)
    query_rest = jnp.zeros((LANES - HEAD_DIM, TILE_DEV), BF16)
    for h in range(HEADS):
        rows = slice(h * HEAD_DIM, (h + 1) * HEAD_DIM)
        key_first = (h - base) & (rate - 1)
        key_pick = (key_lane == key_slot + key_first).astype(BF16)
        both = jnp.concatenate([kv_out[rows], kv_out[D + h * HEAD_DIM : D + (h + 1) * HEAD_DIM], key_rest], axis=0)
        payload[h, :KEY_SLOTS] = dot_nt(key_pick, both).astype(BF16)
        query_first = (h - table[START_ME]) & (rate - 1)
        query_pick = (query_lane == query_slot + query_first).astype(BF16)
        ask = jnp.concatenate([q_out[rows], query_rest], axis=0)
        payload[h, KEY_SLOTS:] = dot_nt(query_pick, ask).astype(BF16)


def project(table, own, partner, qa, qb):
    vmem = pl.BlockSpec(memory_space=pltpu.VMEM)
    return pl.pallas_call(
        project_kernel,
        out_shape=(
            jax.ShapeDtypeStruct((HEADS, KEY_SLOTS + QUERY_SLOTS, LANES), BF16),
            jax.ShapeDtypeStruct((D, TILE_DEV), BF16),
            jax.ShapeDtypeStruct((2 * D, WINDOW), BF16),
        ),
        in_specs=[pl.BlockSpec(memory_space=pltpu.SMEM)] + [vmem] * 4,
        out_specs=(vmem, vmem, vmem),
        scratch_shapes=[pltpu.VMEM((WINDOW, D), BF16)],
        compiler_params=pltpu.CompilerParams(vmem_limit_bytes=VMEM_LIMIT),
        cost_estimate=pl.CostEstimate(flops=2_000_000_000, bytes_accessed=6_000_000, transcendentals=0),
        name="project_rows",
    )(table, own, partner, qa, qb)


def local_kernel(table, q, kv, halo, qa, qb, out_sum, out_best, out_total, rim):
    core, high, start_me = table[CORE], table[HIGH], table[START_ME]
    half = D // 2
    halo_a = halo[:, pl.ds(pl.multiple_of(core * half, LANES), half)]
    halo_b = halo[:, pl.ds(pl.multiple_of((1 - core) * half, LANES), half)]
    rim[...] = (dot_nt(qa[D:], halo_a) + dot_nt(qb[D:], halo_b)).astype(BF16)
    length = jnp.full((1, 1), table[SEGMENT], I32).astype(F32)

    def segment(position):
        return jnp.floor((position.astype(F32) + 0.5) / length)

    query_seg = segment(start_me + iota((1, TILE_DEV), 1))
    key_at = iota((WINDOW, 1), 0)
    key_seg = jnp.where(key_at < table[PAIR_COUNT], segment(table[PAIR_START] + key_at), -1.0)
    rim_first = table[PAIR_START] + jnp.where(high == 0, -HALF, table[PAIR_COUNT])
    rim_at = rim_first + iota((HALF, 1), 0)
    rim_seg = jnp.where((rim_at >= 0) & (rim_at < SEQ_LEN), segment(rim_at), -1.0)
    key_ok, rim_ok = key_seg == query_seg, rim_seg == query_seg
    for h in range(HEADS):
        rows = slice(h * HEAD_DIM, (h + 1) * HEAD_DIM)
        v_rows = slice(D + h * HEAD_DIM, D + (h + 1) * HEAD_DIM)
        scores = jnp.where(key_ok, dot_tn(kv[rows], q[rows]) * SCALE, BIG_NEGATIVE)
        rim_scores = jnp.where(rim_ok, dot_tn(rim[rows], q[rows]) * SCALE, BIG_NEGATIVE)
        best = jnp.maximum(jnp.max(scores, axis=0, keepdims=True), jnp.max(rim_scores, axis=0, keepdims=True))
        weights, rim_weights = jnp.exp(scores - best), jnp.exp(rim_scores - best)
        out_best[h : h + 1] = best
        out_total[h : h + 1] = jnp.sum(weights, axis=0, keepdims=True) + jnp.sum(rim_weights, axis=0, keepdims=True)
        out_sum[rows] = dot_nn(kv[v_rows], weights.astype(BF16)) + dot_nn(rim[v_rows], rim_weights.astype(BF16))


def local_branch(table, q, kv, halo, qa, qb):
    vmem = pl.BlockSpec(memory_space=pltpu.VMEM)
    stat = jax.ShapeDtypeStruct((HEADS, TILE_DEV), F32)
    return pl.pallas_call(
        local_kernel,
        out_shape=(jax.ShapeDtypeStruct((D, TILE_DEV), F32), stat, stat),
        in_specs=[pl.BlockSpec(memory_space=pltpu.SMEM)] + [vmem] * 5,
        out_specs=(vmem, vmem, vmem),
        scratch_shapes=[pltpu.VMEM((2 * D, HALF), BF16)],
        compiler_params=pltpu.CompilerParams(vmem_limit_bytes=VMEM_LIMIT),
        cost_estimate=pl.CostEstimate(flops=600_000_000, bytes_accessed=6_000_000, transcendentals=1_200_000),
        name="local_branch",
    )(table, q, kv, halo, qa, qb)


def far_kernel(table, arrived, answer, scores):
    rate = table[RATE]
    kv = arrived[:, :KEY_SLOTS].reshape(PLANES * KEY_SLOTS, LANES)
    group = 8
    width = group * QUERY_SLOTS
    slot = iota((KEY_SLOTS, width), 0) * rate
    for n in range(PLANES // group):
        asks = arrived[n * group : (n + 1) * group, KEY_SLOTS:].reshape(width, LANES)
        best = jnp.full((1, width), BIG_NEGATIVE, F32)
        for p in range(PLANES):
            phase = (table[PLANE_ID] - table[ALL_STARTS + p]) & (rate - 1)
            piece = dot_nt(arrived[p, :KEY_SLOTS], asks) * SCALE
            piece = jnp.where(slot + phase < table[ALL_COUNTS + p], piece, BIG_NEGATIVE)
            scores[p * KEY_SLOTS : (p + 1) * KEY_SLOTS] = piece
            best = jnp.maximum(best, jnp.max(piece, axis=0, keepdims=True))
        weights = jnp.exp(scores[...] - best)
        total = jnp.sum(weights, axis=0, keepdims=True)
        summed = dot_tn(kv, weights.astype(BF16))
        shared = summed[HEAD_DIM : 2 * HEAD_DIM] / total
        log_all = best + jnp.log(total)
        log_a = log_all.astype(BF16).astype(F32)
        log_b = (log_all - log_a).astype(BF16).astype(F32)
        log_c = log_all - log_a - log_b
        row = iota((LANES - HEAD_DIM, width), 0)
        tail = jnp.where(row == 0, log_a, jnp.where(row == 1, log_b, jnp.where(row == 2, log_c, 0.0)))
        block = jnp.concatenate([shared, tail], axis=0)
        answer[n * group : (n + 1) * group] = block.T.astype(BF16).reshape(group, QUERY_SLOTS, LANES)


def far_branch(table, arrived):
    vmem, smem = pl.BlockSpec(memory_space=pltpu.VMEM), pl.BlockSpec(memory_space=pltpu.SMEM)
    return pl.pallas_call(
        far_kernel,
        out_shape=jax.ShapeDtypeStruct((PLANES, QUERY_SLOTS, LANES), BF16),
        in_specs=[smem, vmem],
        out_specs=vmem,
        scratch_shapes=[pltpu.VMEM((PLANES * KEY_SLOTS, PLANES // 2 * QUERY_SLOTS), F32)],
        compiler_params=pltpu.CompilerParams(vmem_limit_bytes=VMEM_LIMIT),
        cost_estimate=pl.CostEstimate(flops=500_000_000, bytes_accessed=1_000_000, transcendentals=1_000_000),
        name="far_branch",
    )(table, arrived)


def finish_kernel(table, answers, local_sum, local_best, local_total, listing, out, attended):
    rate = table[RATE]
    slot = iota((QUERY_SLOTS, TILE_DEV), 0) * rate
    lane = iota((QUERY_SLOTS, TILE_DEV), 1)
    row = iota((1, TILE_DEV), 1)
    live = row < table[COUNT_ME]
    for h in range(HEADS):
        rows = slice(h * HEAD_DIM, (h + 1) * HEAD_DIM)
        phase = (h - table[START_ME]) & (rate - 1)
        pick = (lane == slot + phase).astype(BF16)
        wide = dot_tn(answers[h], pick)
        log_all = wide[HEAD_DIM : HEAD_DIM + 1] + wide[HEAD_DIM + 1 : HEAD_DIM + 2] + wide[HEAD_DIM + 2 : HEAD_DIM + 3]
        log_all = jnp.where((row & (rate - 1)) == phase, log_all, BIG_NEGATIVE)
        best = local_best[h : h + 1]
        joint = jnp.maximum(best, log_all)
        near = jnp.exp(best - joint)
        far = jnp.exp(log_all - joint)
        below = jnp.where(live, near * local_total[h : h + 1] + far, 1.0)
        mixed = (near * local_sum[rows] + far * wide[:HEAD_DIM]) / below
        attended[rows] = jnp.where(live, mixed, 0.0).astype(BF16)
    back = (listing[0] == iota((TILE_DEV, TILE_DEV), 0)).astype(BF16)
    out[0] = dot_nt(back, attended[...]).astype(BF16)


def finish(table, answers, local_sum, local_best, local_total, listing):
    vmem = pl.BlockSpec(memory_space=pltpu.VMEM)
    return pl.pallas_call(
        finish_kernel,
        out_shape=jax.ShapeDtypeStruct((1, TILE_DEV, D), BF16),
        in_specs=[pl.BlockSpec(memory_space=pltpu.SMEM)] + [vmem] * 5,
        out_specs=vmem,
        scratch_shapes=[pltpu.VMEM((D, TILE_DEV), BF16)],
        compiler_params=pltpu.CompilerParams(vmem_limit_bytes=VMEM_LIMIT),
        cost_estimate=pl.CostEstimate(flops=100_000_000, bytes_accessed=1_500_000, transcendentals=10_000),
        name="finish_rows",
    )(table, answers, local_sum, local_best, local_total, listing)


def mirrored(x):
    z_low = lax.axis_size("zlo")
    pairs = [
        (low * 2 + high, (z_low - 1 - low) * 2 + (1 - high))
        for low in range(z_low)
        for high in range(2)
    ]
    return lax.ppermute(x, ("zlo", "zhi"), pairs)


def across(x):
    return lax.ppermute(x, "zhi", [(0, 1), (1, 0)])


def other_core(x):
    return lax.ppermute(x, "core", [(0, 1), (1, 0)])


def over_plane(x):
    return lax.all_to_all(x, PLANE, 0, 0)


def copies(x):
    return jnp.broadcast_to(x[None], (PLANES,) + x.shape)


def in_order(own, other, high):
    return jnp.where(high == 0, jnp.concatenate([own, other]), jnp.concatenate([other, own]))


def on_device(ctx_in, resid, enc_out_w, slide_proj, qkv_w, tissue, kept_count, dilation):
    core = lax.axis_index("core")
    high = lax.axis_index("zhi")
    plane_id = lax.axis_index("y") * lax.axis_size("x") + lax.axis_index("x")

    w_own = lax.dynamic_slice_in_dim(enc_out_w, core * D, D, 0).T
    p_own = lax.dynamic_slice_in_dim(slide_proj, core * D, D, 0).T
    q_own = lax.dynamic_slice_in_dim(qkv_w, core * (D // 2), D // 2, 0).T
    near_a = over_plane(copies(w_own))
    w_other = mirrored(w_own)
    p_other = mirrored(p_own)
    q_other = mirrored(q_own)
    place = jnp.stack([core, high, plane_id]).astype(I32)
    own_ctx, own_res, table = prepare(place, kept_count, dilation, ctx_in, resid, tissue)
    far = jnp.concatenate([w_other, in_order(p_own, p_other, high)])
    far, near_a, own_ctx, own_res, table = lax.optimization_barrier((copies(far), near_a, own_ctx, own_res, table))
    far_a = over_plane(far)
    near_b = other_core(near_a)
    q_both = copies(in_order(q_own, q_other, high))
    far_a, near_b, q_both = lax.optimization_barrier((far_a, near_b, q_both))
    far_b = other_core(far_a)
    embedded = embed(table, own_ctx, own_res, near_a, near_b, far_a, far_b)

    q_both, embedded = lax.optimization_barrier((q_both, embedded))
    partner = across(embedded)
    q_a, partner = lax.optimization_barrier((over_plane(q_both), partner))
    q_b = other_core(q_a)
    q_a, q_b = q_a.reshape(3 * D, D // 2), q_b.reshape(3 * D, D // 2)
    rim_from = jnp.where(high == 0, table[COUNT_OTHER] - HALF, 0)
    rim = lax.dynamic_slice_in_dim(partner, rim_from, HALF, 0)
    halo_pairs = [(p * 2, p * 2 + 2) for p in range(PLANES - 1)]
    halo_pairs += [(p * 2 + 1, p * 2 - 1) for p in range(1, PLANES)]
    halo = lax.ppermute(rim, ("y", "x", "zhi"), halo_pairs)

    q_b, halo = lax.optimization_barrier((q_b, halo))
    payload, q_rows, kv_rows = project(table, embedded, partner, q_a, q_b)
    arrived = lax.all_to_all(payload, PLANE, 0, 0)
    local_sum, local_best, local_total = local_branch(table, q_rows, kv_rows, halo, q_a, q_b)
    answer = far_branch(table, arrived)
    answers = lax.all_to_all(answer, PLANE, 0, 0)
    return finish(table, answers, local_sum, local_best, local_total, tissue)


def solution(mesh):
    devices = mesh.devices.reshape(-1, 2, 4, 4, 2)
    split = Mesh(devices, ("zlo", "core", "y", "x", "zhi"))
    slide, seq = ("zlo", "core"), ("y", "x", "zhi")
    return jax.shard_map(
        on_device,
        mesh=split,
        in_specs=(
            P(slide, seq, None),
            P(slide, seq, None),
            P(None, seq),
            P(None, seq),
            P(None, seq),
            P(slide, seq, None),
            P(slide, None),
            P(slide, None),
        ),
        out_specs=P(slide, seq, None),
        check_vma=False,
    )
```

```python
import jax
import jax.numpy as jnp
from jax import lax
from jax.experimental import pallas as pl
from jax.experimental.pallas import tpu as pltpu
from jax.sharding import Mesh, PartitionSpec as P

HEADS = 16
HEAD_DIM = 48
D = 768
D_ENC = 1536
HALF = 64
TILE_DEV = 192
SEQ_LEN = 4096
SLOTS = 48
LANES = 128
W_ROWS = 48
P_ROWS = 24
PLANES = 16
PLANE = ("y", "x")
EVERY = ("zlo", "core", "y", "x", "zhi")
NORM_EPS = 1e-06
BIG_NEGATIVE = -1e30
SCALE = HEAD_DIM**-0.5
BF16 = jnp.bfloat16
F32 = jnp.float32
I32 = jnp.int32
VMEM_LIMIT = 48 * 1024 * 1024

CORE, HIGH, PLANE_ID, RATE, SEGMENT, START_ME, COUNT_ME = range(7)
ALL_STARTS = 8
ALL_COUNTS = 40
BLOCKS = 32


def dot_nn(a, b):
    return lax.dot_general(a, b, (((1,), (0,)), ((), ())), preferred_element_type=F32)


def dot_nt(a, b):
    return lax.dot_general(a, b, (((1,), (1,)), ((), ())), preferred_element_type=F32)


def dot_tn(a, b):
    return lax.dot_general(a, b, (((0,), (0,)), ((), ())), preferred_element_type=F32)


def iota(shape, dim):
    return lax.broadcasted_iota(I32, shape, dim)


def call(kernel, name, out_shape, specs, scratch, flops, size, exps=0):
    vmem = pl.BlockSpec(memory_space=pltpu.VMEM)
    smem = pl.BlockSpec(memory_space=pltpu.SMEM)
    hbm = pl.BlockSpec(memory_space=pl.ANY)
    kinds = {"s": smem, "v": vmem, "h": hbm}
    ins, outs = specs.split("-")
    return pl.pallas_call(
        kernel,
        out_shape=tuple(jax.ShapeDtypeStruct(shape, dtype) for shape, dtype in out_shape),
        in_specs=[kinds[c] for c in ins],
        out_specs=tuple(kinds[c] for c in outs),
        scratch_shapes=scratch,
        compiler_params=pltpu.CompilerParams(vmem_limit_bytes=VMEM_LIMIT),
        cost_estimate=pl.CostEstimate(flops=flops, bytes_accessed=size, transcendentals=exps),
        name=name,
    )


def prepare_kernel(place, counts, dilation, ctx, res, listing, own_ctx, own_res, table):
    table[CORE], table[HIGH], table[PLANE_ID] = place[0], place[1], place[2]
    table[RATE], table[SEGMENT] = dilation[0, 1], dilation[0, 0]
    me = place[2] * 2 + place[1]
    start = jnp.int32(0)
    for b in range(BLOCKS):
        count = counts[0, b]
        table[ALL_STARTS + b] = start
        table[ALL_COUNTS + b] = count

        @pl.when(me == b)
        def _(start=start, count=count):
            table[START_ME] = start
            table[COUNT_ME] = count

        start = start + count
    order = (iota((TILE_DEV, TILE_DEV), 0) == listing[0]).astype(BF16)
    own_ctx[...] = dot_tn(order, ctx[0]).astype(BF16)
    own_res[...] = dot_tn(order, res[0]).astype(BF16)


def prepare(*args):
    rows = ((TILE_DEV, D_ENC), BF16)
    shapes = (rows, rows, ((ALL_COUNTS + BLOCKS,), I32))
    return call(prepare_kernel, "prepare_rows", shapes, "sssvvv-vvs", [], 250_000_000, 2_400_000)(*args)


def embed_kernel(table, ctx, res, near_a, near_b, far_a, far_b, out, rims, w, p, hidden, normed, sems):
    core, high = table[CORE], table[HIGH]
    loads = [
        pltpu.make_async_copy(near_a, w.at[core, :, high], sems.at[0]),
        pltpu.make_async_copy(near_b, w.at[1 - core, :, high], sems.at[1]),
        pltpu.make_async_copy(far_a.at[:, :W_ROWS], w.at[core, :, 1 - high], sems.at[2]),
        pltpu.make_async_copy(far_b.at[:, :W_ROWS], w.at[1 - core, :, 1 - high], sems.at[3]),
        pltpu.make_async_copy(far_a.at[:, W_ROWS:], p.at[core], sems.at[4]),
        pltpu.make_async_copy(far_b.at[:, W_ROWS:], p.at[1 - core], sems.at[5]),
    ]
    for load in loads:
        load.start()
    for load in loads[:4]:
        load.wait()
    group = 4
    width = group * 2 * W_ROWS
    total = jnp.zeros((TILE_DEV, 1), F32)
    for n in range(PLANES // group):
        columns = slice(n * width, (n + 1) * width)
        part = res[:, columns].astype(F32)
        for half in range(2):
            block = w[half, n * group : (n + 1) * group].reshape(width, D)
            part += dot_nt(ctx[:, half * D : (half + 1) * D], block)
        hidden[:, columns] = part
        total += jnp.sum(part, axis=1, keepdims=True)
    center = hidden[...] - total / D_ENC
    spread = jnp.sum(center * center, axis=1, keepdims=True) / D_ENC
    normed[...] = (center * lax.rsqrt(spread + NORM_EPS)).astype(BF16)
    for load in loads[4:]:
        load.wait()
    for n in range(2):
        rows = slice(n * PLANES // 2, (n + 1) * PLANES // 2)
        part = dot_nt(normed[:, :D], p[0, rows].reshape(D // 2, D))
        part += dot_nt(normed[:, D:], p[1, rows].reshape(D // 2, D))
        out[:, n * D // 2 : (n + 1) * D // 2] = part.astype(BF16)
    lane = iota((HALF, TILE_DEV), 1)
    pick = (lane == iota((HALF, TILE_DEV), 0) + (table[COUNT_ME] - HALF)).astype(BF16)
    rims[:HALF] = dot_nn(pick, out[...]).astype(BF16)
    rims[HALF:] = out[:HALF]


def embed(*args):
    scratch = [
        pltpu.VMEM((2, PLANES, 2, W_ROWS, D), BF16),
        pltpu.VMEM((2, PLANES, 2 * P_ROWS, D), BF16),
        pltpu.VMEM((TILE_DEV, D_ENC), F32),
        pltpu.VMEM((TILE_DEV, D_ENC), BF16),
        pltpu.SemaphoreType.DMA((6,)),
    ]
    shapes = (((TILE_DEV, D), BF16), ((2 * HALF, D), BF16))
    return call(embed_kernel, "embed_rows", shapes, "svvhhhh-vv", scratch, 1_400_000_000, 9_000_000)(*args)


def halves(table, ref, width):
    core = table[CORE]
    first = ref[:, pl.ds(pl.multiple_of(core * width, LANES), width)]
    second = ref[:, pl.ds(pl.multiple_of((1 - core) * width, LANES), width)]
    return first, second


def project_kernel(table, own, q_a, q_b, payload, q_out, kv_out):
    rate, start_me = table[RATE], table[START_ME]
    first, second = halves(table, own, D // 2)
    q_out[...] = (dot_nt(q_a[:D], first) + dot_nt(q_b[:D], second)).astype(BF16)
    for n in range(2):
        rows = slice((n + 1) * D, (n + 2) * D)
        kv_out[n * D : (n + 1) * D] = (dot_nt(q_a[rows], first) + dot_nt(q_b[rows], second)).astype(BF16)
    slot = iota((SLOTS, TILE_DEV), 0) * rate
    lane = iota((SLOTS, TILE_DEV), 1)
    key_rest = jnp.zeros((LANES - 2 * HEAD_DIM, TILE_DEV), BF16)
    query_rest = jnp.zeros((LANES - HEAD_DIM, TILE_DEV), BF16)
    for h in range(HEADS):
        rows = slice(h * HEAD_DIM, (h + 1) * HEAD_DIM)
        pick = (lane == slot + ((h - start_me) & (rate - 1))).astype(BF16)
        both = jnp.concatenate([kv_out[rows], kv_out[D + h * HEAD_DIM : D + (h + 1) * HEAD_DIM], key_rest], axis=0)
        ask = jnp.concatenate([q_out[rows], query_rest], axis=0)
        payload[h, :SLOTS] = dot_nt(pick, both).astype(BF16)
        payload[h, SLOTS:] = dot_nt(pick, ask).astype(BF16)


def project(*args):
    shapes = (((HEADS, 2 * SLOTS, LANES), BF16), ((D, TILE_DEV), BF16), ((2 * D, TILE_DEV), BF16))
    return call(project_kernel, "project_rows", shapes, "svvv-vvv", [], 1_000_000_000, 5_000_000)(*args)


def pack_kernel(arrived, out):
    rows = arrived[:, :SLOTS].reshape(PLANES * SLOTS, LANES)
    out[...] = rows.T[: 2 * HEAD_DIM]


def pack(*args):
    shapes = (((2 * HEAD_DIM, PLANES * SLOTS), BF16),)
    return call(pack_kernel, "pack_keys", shapes, "v-v", [], 1_000_000, 500_000)(*args)[0]


def local_kernel(table, q, kv, before, after, q_a, q_b, out_sum, out_best, out_total, rims, rim):
    start_me, count_me = table[START_ME], table[COUNT_ME]
    rims[:HALF] = before[...]
    rims[HALF:] = after[...]
    first, second = halves(table, rims, D // 2)
    rim[...] = (dot_nt(q_a[D:], first) + dot_nt(q_b[D:], second)).astype(BF16)
    length = jnp.full((1, 1), table[SEGMENT], I32).astype(F32)

    def segment(position):
        return jnp.floor((position.astype(F32) + 0.5) / length)

    query_seg = segment(start_me + iota((1, TILE_DEV), 1))
    key_at = iota((TILE_DEV, 1), 0)
    key_seg = jnp.where(key_at < count_me, segment(start_me + key_at), -1.0)
    rim_id = iota((2 * HALF, 1), 0)
    rim_at = start_me + jnp.where(rim_id < HALF, rim_id - HALF, rim_id - HALF + count_me)
    rim_seg = jnp.where((rim_at >= 0) & (rim_at < SEQ_LEN), segment(rim_at), -1.0)
    key_ok, rim_ok = key_seg == query_seg, rim_seg == query_seg
    for h in range(HEADS):
        rows = slice(h * HEAD_DIM, (h + 1) * HEAD_DIM)
        v_rows = slice(D + h * HEAD_DIM, D + (h + 1) * HEAD_DIM)
        scores = jnp.where(key_ok, dot_tn(kv[rows], q[rows]) * SCALE, BIG_NEGATIVE)
        rim_scores = jnp.where(rim_ok, dot_tn(rim[rows], q[rows]) * SCALE, BIG_NEGATIVE)
        best = jnp.maximum(jnp.max(scores, axis=0, keepdims=True), jnp.max(rim_scores, axis=0, keepdims=True))
        weights, rim_weights = jnp.exp(scores - best), jnp.exp(rim_scores - best)
        out_best[h : h + 1] = best
        out_total[h : h + 1] = jnp.sum(weights, axis=0, keepdims=True) + jnp.sum(rim_weights, axis=0, keepdims=True)
        out_sum[rows] = dot_nn(kv[v_rows], weights.astype(BF16)) + dot_nn(rim[v_rows], rim_weights.astype(BF16))


def local_branch(*args):
    stat = ((HEADS, TILE_DEV), F32)
    shapes = (((D, TILE_DEV), F32), stat, stat)
    scratch = [pltpu.VMEM((2 * HALF, D), BF16), pltpu.VMEM((2 * D, 2 * HALF), BF16)]
    return call(local_kernel, "local_branch", shapes, "svvvvvv-vvv", scratch, 600_000_000, 5_000_000, 1_000_000)(*args)


def far_scores(table, high, keys, asks, scores):
    rate = table[RATE]
    slot = iota((SLOTS, asks.shape[0]), 0) * rate
    best = jnp.full((1, asks.shape[0]), BIG_NEGATIVE, F32)
    for p in range(PLANES):
        block = 2 * p + high
        phase = (table[PLANE_ID] - table[ALL_STARTS + block]) & (rate - 1)
        piece = dot_nt(keys[p * SLOTS : (p + 1) * SLOTS], asks) * SCALE
        piece = jnp.where(slot + phase < table[ALL_COUNTS + block], piece, BIG_NEGATIVE)
        scores[p * SLOTS : (p + 1) * SLOTS] = piece
        best = jnp.maximum(best, jnp.max(piece, axis=0, keepdims=True))
    return best


FAR_GROUP = 8
FAR_WIDTH = FAR_GROUP * SLOTS


def far_own_kernel(table, arrived, out_sum, out_best, out_total, scores):
    keys = arrived[:, :SLOTS].reshape(PLANES * SLOTS, LANES)
    for n in range(PLANES // FAR_GROUP):
        lanes = slice(n * FAR_WIDTH, (n + 1) * FAR_WIDTH)
        asks = arrived[n * FAR_GROUP : (n + 1) * FAR_GROUP, SLOTS:].reshape(FAR_WIDTH, LANES)
        best = far_scores(table, table[HIGH], keys, asks, scores)
        weights = jnp.exp(scores[...] - best)
        out_best[:, lanes] = best
        out_total[:, lanes] = jnp.sum(weights, axis=0, keepdims=True)
        out_sum[:, lanes] = dot_tn(keys, weights.astype(BF16))[HEAD_DIM : 2 * HEAD_DIM]


def far_own(*args):
    width = PLANES * SLOTS
    shapes = (((HEAD_DIM, width), F32), ((1, width), F32), ((1, width), F32))
    scratch = [pltpu.VMEM((width, FAR_WIDTH), F32)]
    return call(far_own_kernel, "far_own", shapes, "sv-vvv", scratch, 300_000_000, 700_000, 600_000)(*args)


def far_rest_kernel(table, arrived, other, own_sum, own_best, own_total, answer, scores):
    other_t = other[...]
    keys = other_t.T
    values = other_t[HEAD_DIM:]
    for n in range(PLANES // FAR_GROUP):
        lanes = slice(n * FAR_WIDTH, (n + 1) * FAR_WIDTH)
        asks = arrived[n * FAR_GROUP : (n + 1) * FAR_GROUP, SLOTS:].reshape(FAR_WIDTH, LANES)[:, : 2 * HEAD_DIM]
        best_o = own_best[:, lanes]
        best = jnp.maximum(best_o, far_scores(table, 1 - table[HIGH], keys, asks, scores))
        weights = jnp.exp(scores[...] - best)
        scale_o = jnp.exp(best_o - best)
        total = jnp.sum(weights, axis=0, keepdims=True) + scale_o * own_total[:, lanes]
        summed = dot_nn(values, weights.astype(BF16)) + scale_o * own_sum[:, lanes]
        shared = summed / total
        log_all = best + jnp.log(total)
        log_a = log_all.astype(BF16).astype(F32)
        log_b = (log_all - log_a).astype(BF16).astype(F32)
        log_c = log_all - log_a - log_b
        row = iota((LANES - HEAD_DIM, FAR_WIDTH), 0)
        tail = jnp.where(row == 0, log_a, jnp.where(row == 1, log_b, jnp.where(row == 2, log_c, 0.0)))
        block = jnp.concatenate([shared, tail], axis=0)
        answer[n * FAR_GROUP : (n + 1) * FAR_GROUP] = block.T.astype(BF16).reshape(FAR_GROUP, SLOTS, LANES)


def far_rest(*args):
    shapes = (((PLANES, SLOTS, LANES), BF16),)
    scratch = [pltpu.VMEM((PLANES * SLOTS, FAR_WIDTH), F32)]
    return call(far_rest_kernel, "far_rest", shapes, "svvvvv-v", scratch, 300_000_000, 1_000_000, 600_000)(*args)[0]


def finish_kernel(table, answers, local_sum, local_best, local_total, listing, out, attended):
    rate = table[RATE]
    slot = iota((SLOTS, TILE_DEV), 0) * rate
    lane = iota((SLOTS, TILE_DEV), 1)
    row = iota((1, TILE_DEV), 1)
    live = row < table[COUNT_ME]
    for h in range(HEADS):
        rows = slice(h * HEAD_DIM, (h + 1) * HEAD_DIM)
        phase = (h - table[START_ME]) & (rate - 1)
        pick = (lane == slot + phase).astype(BF16)
        wide = dot_tn(answers[h], pick)
        log_all = wide[HEAD_DIM : HEAD_DIM + 1] + wide[HEAD_DIM + 1 : HEAD_DIM + 2] + wide[HEAD_DIM + 2 : HEAD_DIM + 3]
        log_all = jnp.where((row & (rate - 1)) == phase, log_all, BIG_NEGATIVE)
        best = local_best[h : h + 1]
        joint = jnp.maximum(best, log_all)
        near = jnp.exp(best - joint)
        far = jnp.exp(log_all - joint)
        below = jnp.where(live, near * local_total[h : h + 1] + far, 1.0)
        mixed = (near * local_sum[rows] + far * wide[:HEAD_DIM]) / below
        attended[rows] = jnp.where(live, mixed, 0.0).astype(BF16)
    back = (listing[0] == iota((TILE_DEV, TILE_DEV), 0)).astype(BF16)
    out[0] = dot_nt(back, attended[...]).astype(BF16)


def finish(*args):
    shapes = (((1, TILE_DEV, D), BF16),)
    scratch = [pltpu.VMEM((D, TILE_DEV), BF16)]
    return call(finish_kernel, "finish_rows", shapes, "svvvvv-v", scratch, 100_000_000, 1_500_000, 10_000)(*args)[0]


def mirrored(x):
    z_low = lax.axis_size("zlo")
    pairs = [
        (low * 2 + high, (z_low - 1 - low) * 2 + (1 - high))
        for low in range(z_low)
        for high in range(2)
    ]
    return lax.ppermute(x, ("zlo", "zhi"), pairs)


def across(x):
    return lax.ppermute(x, "zhi", [(0, 1), (1, 0)])


def rank(z, core, plane):
    z_low = lax.axis_size("zlo")
    return ((z % z_low * 2 + core) * PLANES + plane) * 2 + z // z_low


def all_places():
    z_size = 2 * lax.axis_size("zlo")
    return [(z, core, plane) for z in range(z_size) for core in range(2) for plane in range(PLANES)]


def toward(z, core):
    z_size = 2 * lax.axis_size("zlo")
    step = z_size // 4
    return (z + (step if core == 0 else -step)) % z_size


def quarter_way(x):
    pairs = [(rank(z, core, plane), rank(toward(z, core), core, plane)) for z, core, plane in all_places()]
    return lax.ppermute(x, EVERY, pairs)


def to_next(x, sign):
    pairs = []
    z_low = lax.axis_size("zlo")
    for z, core, plane in all_places():
        half_way = toward(z, core)
        block = 2 * plane + z // z_low + sign
        if 0 <= block < 2 * PLANES:
            target = rank(z % z_low + z_low * (block % 2), core, block // 2)
            pairs.append((rank(half_way, core, plane), target))
    return lax.ppermute(x, EVERY, pairs)


def other_core(x):
    return lax.ppermute(x, "core", [(0, 1), (1, 0)])


def over_plane(x):
    return lax.all_to_all(x, PLANE, 0, 0)


def hold(*values):
    return lax.optimization_barrier(values)


def copies(x):
    return jnp.broadcast_to(x[None], (PLANES,) + x.shape)


def in_order(own, other, high):
    return jnp.where(high == 0, jnp.concatenate([own, other]), jnp.concatenate([other, own]))


def on_device(ctx_in, resid, enc_out_w, slide_proj, qkv_w, tissue, kept_count, dilation):
    core = lax.axis_index("core")
    high = lax.axis_index("zhi")
    plane_id = lax.axis_index("y") * lax.axis_size("x") + lax.axis_index("x")

    w_own = lax.dynamic_slice_in_dim(enc_out_w, core * D, D, 0).T
    p_own = lax.dynamic_slice_in_dim(slide_proj, core * D, D, 0).T
    q_own = lax.dynamic_slice_in_dim(qkv_w, core * (D // 2), D // 2, 0).T
    near_a = over_plane(copies(w_own))
    w_other = mirrored(w_own)
    p_other = mirrored(p_own)
    q_other = mirrored(q_own)
    place = jnp.stack([core, high, plane_id]).astype(I32)
    own_ctx, own_res, table = prepare(place, kept_count, dilation, ctx_in, resid, tissue)
    far = jnp.concatenate([w_other, in_order(p_own, p_other, high)])
    far, near_a, own_ctx, own_res, table = hold(copies(far), near_a, own_ctx, own_res, table)
    far_a = over_plane(far)
    near_b = other_core(near_a)
    q_both = copies(in_order(q_own, q_other, high))
    far_a, near_b, q_both = hold(far_a, near_b, q_both)
    q_a = over_plane(q_both)
    far_b = other_core(far_a)
    embedded, rims = embed(table, own_ctx, own_res, near_a, near_b, far_a, far_b)
    rims = quarter_way(rims)
    q_a, embedded, rims = hold(q_a, embedded, rims)
    before, after = to_next(rims[:HALF], 1), to_next(rims[HALF:], -1)
    q_b = other_core(q_a)
    q_a, q_b = q_a.reshape(3 * D, D // 2), q_b.reshape(3 * D, D // 2)
    payload, q_rows, kv_rows = project(table, embedded, q_a, q_b)
    arrived = lax.all_to_all(payload, PLANE, 0, 0)
    other = across(pack(arrived))
    own_sum, own_best, own_total = far_own(table, arrived)
    local_sum, local_best, local_total = local_branch(table, q_rows, kv_rows, before, after, q_a, q_b)
    other, own_sum, local_sum = hold(other, own_sum, local_sum)
    answer = far_rest(table, arrived, other, own_sum, own_best, own_total)
    answers = lax.all_to_all(answer, PLANE, 0, 0)
    return finish(table, answers, local_sum, local_best, local_total, tissue)


def solution(mesh):
    devices = mesh.devices.reshape(-1, 2, 4, 4, 2)
    split = Mesh(devices, ("zlo", "core", "y", "x", "zhi"))
    slide, seq = ("zlo", "core"), ("y", "x", "zhi")
    return jax.shard_map(
        on_device,
        mesh=split,
        in_specs=(
            P(slide, seq, None),
            P(slide, seq, None),
            P(None, seq),
            P(None, seq),
            P(None, seq),
            P(slide, seq, None),
            P(slide, None),
            P(slide, None),
        ),
        out_specs=P(slide, seq, None),
        check_vma=False,
    )
```

```python
import jax
import jax.numpy as jnp
from jax import lax
from jax.experimental import pallas as pl
from jax.experimental.pallas import tpu as pltpu
from jax.sharding import Mesh, PartitionSpec as P

HEADS = 16
HEAD_DIM = 48
D = 768
D_ENC = 1536
HALF = 64
TILE_DEV = 192
SEQ_LEN = 4096
SLOTS = 48
LANES = 128
W_ROWS = 48
P_ROWS = 24
PLANES = 16
PLANE = ("y", "x")
EVERY = ("zlo", "core", "y", "x", "zhi")
NORM_EPS = 1e-06
BIG_NEGATIVE = -1e30
SCALE = HEAD_DIM**-0.5
BF16 = jnp.bfloat16
F32 = jnp.float32
I32 = jnp.int32
VMEM_LIMIT = 48 * 1024 * 1024

CORE, HIGH, PLANE_ID, RATE, SEGMENT, START_ME, COUNT_ME = range(7)
ALL_STARTS = 8
ALL_COUNTS = 40
BLOCKS = 32


def dot_nn(a, b):
    return lax.dot_general(a, b, (((1,), (0,)), ((), ())), preferred_element_type=F32)


def dot_nt(a, b):
    return lax.dot_general(a, b, (((1,), (1,)), ((), ())), preferred_element_type=F32)


def dot_tn(a, b):
    return lax.dot_general(a, b, (((0,), (0,)), ((), ())), preferred_element_type=F32)


def iota(shape, dim):
    return lax.broadcasted_iota(I32, shape, dim)


def call(kernel, name, out_shape, specs, scratch, flops, size, exps=0):
    vmem = pl.BlockSpec(memory_space=pltpu.VMEM)
    smem = pl.BlockSpec(memory_space=pltpu.SMEM)
    hbm = pl.BlockSpec(memory_space=pl.ANY)
    kinds = {"s": smem, "v": vmem, "h": hbm}
    ins, outs = specs.split("-")
    return pl.pallas_call(
        kernel,
        out_shape=tuple(jax.ShapeDtypeStruct(shape, dtype) for shape, dtype in out_shape),
        in_specs=[kinds[c] for c in ins],
        out_specs=tuple(kinds[c] for c in outs),
        scratch_shapes=scratch,
        compiler_params=pltpu.CompilerParams(vmem_limit_bytes=VMEM_LIMIT),
        cost_estimate=pl.CostEstimate(flops=flops, bytes_accessed=size, transcendentals=exps),
        name=name,
    )


def prepare_kernel(place, counts, dilation, ctx, res, listing, own_ctx, own_res, table):
    table[CORE], table[HIGH], table[PLANE_ID] = place[0], place[1], place[2]
    table[RATE], table[SEGMENT] = dilation[0, 1], dilation[0, 0]
    me = place[2] * 2 + place[1]
    start = jnp.int32(0)
    for b in range(BLOCKS):
        count = counts[0, b]
        table[ALL_STARTS + b] = start
        table[ALL_COUNTS + b] = count

        @pl.when(me == b)
        def _(start=start, count=count):
            table[START_ME] = start
            table[COUNT_ME] = count

        start = start + count
    order = (iota((TILE_DEV, TILE_DEV), 0) == listing[0]).astype(BF16)
    own_ctx[...] = dot_tn(order, ctx[0]).astype(BF16)
    for z in range(2):
        own_res[z] = dot_tn(order, res[z]).astype(BF16)


def prepare(*args):
    shapes = (((TILE_DEV, D_ENC), BF16), ((2, TILE_DEV, D), BF16), ((ALL_COUNTS + BLOCKS,), I32))
    return call(prepare_kernel, "prepare_rows", shapes, "sssvvv-vvs", [], 250_000_000, 2_400_000)(*args)


def halves(table, ref, width):
    core = table[CORE]
    first = ref[:, pl.ds(pl.multiple_of(core * width, LANES), width)]
    second = ref[:, pl.ds(pl.multiple_of((1 - core) * width, LANES), width)]
    return first, second


def embed_kernel(table, ctx, res, near_a, near_b, far_a, far_b, out, rims, hidden, normed):
    core, high = table[CORE], table[HIGH]
    first, second = halves(table, ctx, D)
    near = dot_nt(first, near_a[...]) + dot_nt(second, near_b[...]) + res[high].astype(F32)
    hidden[0] = near
    far = dot_nt(first, far_a[:, :W_ROWS].reshape(D, D)) + dot_nt(second, far_b[:, :W_ROWS].reshape(D, D))
    far += res[1 - high].astype(F32)
    hidden[1] = far
    mean = (jnp.sum(near, axis=1, keepdims=True) + jnp.sum(far, axis=1, keepdims=True)) / D_ENC
    near, far = hidden[0] - mean, hidden[1] - mean
    spread = (jnp.sum(near * near, axis=1, keepdims=True) + jnp.sum(far * far, axis=1, keepdims=True)) / D_ENC
    scale = lax.rsqrt(spread + NORM_EPS)
    normed[high] = (near * scale).astype(BF16)
    normed[1 - high] = (far * scale).astype(BF16)
    total = dot_nt(normed[core], far_a[:, W_ROWS:].reshape(D, D))
    total += dot_nt(normed[1 - core], far_b[:, W_ROWS:].reshape(D, D))
    out[...] = total.astype(BF16)
    lane = iota((HALF, TILE_DEV), 1)
    pick = (lane == iota((HALF, TILE_DEV), 0) + (table[COUNT_ME] - HALF)).astype(BF16)
    rims[:HALF] = dot_nn(pick, out[...]).astype(BF16)
    rims[HALF:] = out[:HALF]


def embed(*args):
    scratch = [pltpu.VMEM((2, TILE_DEV, D), F32), pltpu.VMEM((2, TILE_DEV, D), BF16)]
    shapes = (((TILE_DEV, D), BF16), ((2 * HALF, D), BF16))
    return call(embed_kernel, "embed_rows", shapes, "svvvvvv-vv", scratch, 1_400_000_000, 9_000_000)(*args)


def project_kernel(table, own, q_a, q_b, payload, q_out, kv_out):
    rate, start_me = table[RATE], table[START_ME]
    first, second = halves(table, own, D // 2)
    q_out[...] = (dot_nt(q_a[:D], first) + dot_nt(q_b[:D], second)).astype(BF16)
    for n in range(2):
        rows = slice((n + 1) * D, (n + 2) * D)
        kv_out[n * D : (n + 1) * D] = (dot_nt(q_a[rows], first) + dot_nt(q_b[rows], second)).astype(BF16)
    slot = iota((SLOTS, TILE_DEV), 0) * rate
    lane = iota((SLOTS, TILE_DEV), 1)
    key_rest = jnp.zeros((LANES - 2 * HEAD_DIM, TILE_DEV), BF16)
    query_rest = jnp.zeros((LANES - HEAD_DIM, TILE_DEV), BF16)
    for h in range(HEADS):
        rows = slice(h * HEAD_DIM, (h + 1) * HEAD_DIM)
        pick = (lane == slot + ((h - start_me) & (rate - 1))).astype(BF16)
        both = jnp.concatenate([kv_out[rows], kv_out[D + h * HEAD_DIM : D + (h + 1) * HEAD_DIM], key_rest], axis=0)
        ask = jnp.concatenate([q_out[rows], query_rest], axis=0)
        payload[h, :SLOTS] = dot_nt(pick, both).astype(BF16)
        payload[h, SLOTS:] = dot_nt(pick, ask).astype(BF16)


def project(*args):
    shapes = (((HEADS, 2 * SLOTS, LANES), BF16), ((D, TILE_DEV), BF16), ((2 * D, TILE_DEV), BF16))
    return call(project_kernel, "project_rows", shapes, "svvv-vvv", [], 1_000_000_000, 5_000_000)(*args)


def pack_kernel(arrived, out):
    rows = arrived[:, :SLOTS].reshape(PLANES * SLOTS, LANES)
    out[...] = rows.T[: 2 * HEAD_DIM]


def pack(*args):
    shapes = (((2 * HEAD_DIM, PLANES * SLOTS), BF16),)
    return call(pack_kernel, "pack_keys", shapes, "v-v", [], 1_000_000, 500_000)(*args)[0]


def local_kernel(table, q, kv, before, after, q_a, q_b, out_sum, out_best, out_total, rims, rim):
    start_me, count_me = table[START_ME], table[COUNT_ME]
    rims[:HALF] = before[...]
    rims[HALF:] = after[...]
    first, second = halves(table, rims, D // 2)
    rim[...] = (dot_nt(q_a[D:], first) + dot_nt(q_b[D:], second)).astype(BF16)
    length = jnp.full((1, 1), table[SEGMENT], I32).astype(F32)

    def segment(position):
        return jnp.floor((position.astype(F32) + 0.5) / length)

    query_seg = segment(start_me + iota((1, TILE_DEV), 1))
    key_at = iota((TILE_DEV, 1), 0)
    key_seg = jnp.where(key_at < count_me, segment(start_me + key_at), -1.0)
    rim_id = iota((2 * HALF, 1), 0)
    rim_at = start_me + jnp.where(rim_id < HALF, rim_id - HALF, rim_id - HALF + count_me)
    rim_seg = jnp.where((rim_at >= 0) & (rim_at < SEQ_LEN), segment(rim_at), -1.0)
    key_ok, rim_ok = key_seg == query_seg, rim_seg == query_seg
    for h in range(HEADS):
        rows = slice(h * HEAD_DIM, (h + 1) * HEAD_DIM)
        v_rows = slice(D + h * HEAD_DIM, D + (h + 1) * HEAD_DIM)
        scores = jnp.where(key_ok, dot_tn(kv[rows], q[rows]) * SCALE, BIG_NEGATIVE)
        rim_scores = jnp.where(rim_ok, dot_tn(rim[rows], q[rows]) * SCALE, BIG_NEGATIVE)
        best = jnp.maximum(jnp.max(scores, axis=0, keepdims=True), jnp.max(rim_scores, axis=0, keepdims=True))
        weights, rim_weights = jnp.exp(scores - best), jnp.exp(rim_scores - best)
        out_best[h : h + 1] = best
        out_total[h : h + 1] = jnp.sum(weights, axis=0, keepdims=True) + jnp.sum(rim_weights, axis=0, keepdims=True)
        out_sum[rows] = dot_nn(kv[v_rows], weights.astype(BF16)) + dot_nn(rim[v_rows], rim_weights.astype(BF16))


def local_branch(*args):
    stat = ((HEADS, TILE_DEV), F32)
    shapes = (((D, TILE_DEV), F32), stat, stat)
    scratch = [pltpu.VMEM((2 * HALF, D), BF16), pltpu.VMEM((2 * D, 2 * HALF), BF16)]
    return call(local_kernel, "local_branch", shapes, "svvvvvv-vvv", scratch, 600_000_000, 5_000_000, 1_000_000)(*args)


def far_scores(table, high, keys, asks, scores):
    rate = table[RATE]
    slot = iota((SLOTS, asks.shape[0]), 0) * rate
    best = jnp.full((1, asks.shape[0]), BIG_NEGATIVE, F32)
    for p in range(PLANES):
        block = 2 * p + high
        phase = (table[PLANE_ID] - table[ALL_STARTS + block]) & (rate - 1)
        piece = dot_nt(keys[p * SLOTS : (p + 1) * SLOTS], asks) * SCALE
        piece = jnp.where(slot + phase < table[ALL_COUNTS + block], piece, BIG_NEGATIVE)
        scores[p * SLOTS : (p + 1) * SLOTS] = piece
        best = jnp.maximum(best, jnp.max(piece, axis=0, keepdims=True))
    return best


FAR_GROUP = 8
FAR_WIDTH = FAR_GROUP * SLOTS


def far_own_kernel(table, arrived, out_sum, out_best, out_total, scores):
    keys = arrived[:, :SLOTS].reshape(PLANES * SLOTS, LANES)
    for n in range(PLANES // FAR_GROUP):
        lanes = slice(n * FAR_WIDTH, (n + 1) * FAR_WIDTH)
        asks = arrived[n * FAR_GROUP : (n + 1) * FAR_GROUP, SLOTS:].reshape(FAR_WIDTH, LANES)
        best = far_scores(table, table[HIGH], keys, asks, scores)
        weights = jnp.exp(scores[...] - best)
        out_best[:, lanes] = best
        out_total[:, lanes] = jnp.sum(weights, axis=0, keepdims=True)
        out_sum[:, lanes] = dot_tn(keys, weights.astype(BF16))[HEAD_DIM : 2 * HEAD_DIM]


def far_own(*args):
    width = PLANES * SLOTS
    shapes = (((HEAD_DIM, width), F32), ((1, width), F32), ((1, width), F32))
    scratch = [pltpu.VMEM((width, FAR_WIDTH), F32)]
    return call(far_own_kernel, "far_own", shapes, "sv-vvv", scratch, 300_000_000, 700_000, 600_000)(*args)


def far_rest_kernel(table, arrived, other, own_sum, own_best, own_total, answer, scores):
    other_t = other[...]
    keys = other_t.T
    values = other_t[HEAD_DIM:]
    for n in range(PLANES // FAR_GROUP):
        lanes = slice(n * FAR_WIDTH, (n + 1) * FAR_WIDTH)
        asks = arrived[n * FAR_GROUP : (n + 1) * FAR_GROUP, SLOTS:].reshape(FAR_WIDTH, LANES)[:, : 2 * HEAD_DIM]
        best_o = own_best[:, lanes]
        best = jnp.maximum(best_o, far_scores(table, 1 - table[HIGH], keys, asks, scores))
        weights = jnp.exp(scores[...] - best)
        scale_o = jnp.exp(best_o - best)
        total = jnp.sum(weights, axis=0, keepdims=True) + scale_o * own_total[:, lanes]
        summed = dot_nn(values, weights.astype(BF16)) + scale_o * own_sum[:, lanes]
        shared = summed / total
        log_all = best + jnp.log(total)
        log_a = log_all.astype(BF16).astype(F32)
        log_b = (log_all - log_a).astype(BF16).astype(F32)
        log_c = log_all - log_a - log_b
        row = iota((LANES - HEAD_DIM, FAR_WIDTH), 0)
        tail = jnp.where(row == 0, log_a, jnp.where(row == 1, log_b, jnp.where(row == 2, log_c, 0.0)))
        block = jnp.concatenate([shared, tail], axis=0)
        answer[n * FAR_GROUP : (n + 1) * FAR_GROUP] = block.T.astype(BF16).reshape(FAR_GROUP, SLOTS, LANES)


def far_rest(*args):
    shapes = (((PLANES, SLOTS, LANES), BF16),)
    scratch = [pltpu.VMEM((PLANES * SLOTS, FAR_WIDTH), F32)]
    return call(far_rest_kernel, "far_rest", shapes, "svvvvv-v", scratch, 300_000_000, 1_000_000, 600_000)(*args)[0]


def finish_kernel(table, answers, local_sum, local_best, local_total, listing, out, attended):
    rate = table[RATE]
    slot = iota((SLOTS, TILE_DEV), 0) * rate
    lane = iota((SLOTS, TILE_DEV), 1)
    row = iota((1, TILE_DEV), 1)
    live = row < table[COUNT_ME]
    for h in range(HEADS):
        rows = slice(h * HEAD_DIM, (h + 1) * HEAD_DIM)
        phase = (h - table[START_ME]) & (rate - 1)
        pick = (lane == slot + phase).astype(BF16)
        wide = dot_tn(answers[h], pick)
        log_all = wide[HEAD_DIM : HEAD_DIM + 1] + wide[HEAD_DIM + 1 : HEAD_DIM + 2] + wide[HEAD_DIM + 2 : HEAD_DIM + 3]
        log_all = jnp.where((row & (rate - 1)) == phase, log_all, BIG_NEGATIVE)
        best = local_best[h : h + 1]
        joint = jnp.maximum(best, log_all)
        near = jnp.exp(best - joint)
        far = jnp.exp(log_all - joint)
        below = jnp.where(live, near * local_total[h : h + 1] + far, 1.0)
        mixed = (near * local_sum[rows] + far * wide[:HEAD_DIM]) / below
        attended[rows] = jnp.where(live, mixed, 0.0).astype(BF16)
    back = (listing[0] == iota((TILE_DEV, TILE_DEV), 0)).astype(BF16)
    out[0] = dot_nt(back, attended[...]).astype(BF16)


def finish(*args):
    shapes = (((1, TILE_DEV, D), BF16),)
    scratch = [pltpu.VMEM((D, TILE_DEV), BF16)]
    return call(finish_kernel, "finish_rows", shapes, "svvvvv-v", scratch, 100_000_000, 1_500_000, 10_000)(*args)[0]


def mirrored(x):
    z_low = lax.axis_size("zlo")
    pairs = [
        (low * 2 + high, (z_low - 1 - low) * 2 + (1 - high))
        for low in range(z_low)
        for high in range(2)
    ]
    return lax.ppermute(x, ("zlo", "zhi"), pairs)


def across(x):
    return lax.ppermute(x, "zhi", [(0, 1), (1, 0)])


def rank(z, core, plane):
    z_low = lax.axis_size("zlo")
    return ((z % z_low * 2 + core) * PLANES + plane) * 2 + z // z_low


def all_places():
    z_size = 2 * lax.axis_size("zlo")
    return [(z, core, plane) for z in range(z_size) for core in range(2) for plane in range(PLANES)]


def toward(z, core):
    z_size = 2 * lax.axis_size("zlo")
    step = z_size // 4
    return (z + (step if core == 0 else -step)) % z_size


def quarter_way(x):
    pairs = [(rank(z, core, plane), rank(toward(z, core), core, plane)) for z, core, plane in all_places()]
    return lax.ppermute(x, EVERY, pairs)


def to_next(x, sign):
    pairs = []
    z_low = lax.axis_size("zlo")
    for z, core, plane in all_places():
        half_way = toward(z, core)
        block = 2 * plane + z // z_low + sign
        if 0 <= block < 2 * PLANES:
            target = rank(z % z_low + z_low * (block % 2), core, block // 2)
            pairs.append((rank(half_way, core, plane), target))
    return lax.ppermute(x, EVERY, pairs)


def other_core(x):
    return lax.ppermute(x, "core", [(0, 1), (1, 0)])


def over_plane(x):
    return lax.all_to_all(x, PLANE, 0, 0)


def hold(*values):
    return lax.optimization_barrier(values)


def copies(x):
    return jnp.broadcast_to(x[None], (PLANES,) + x.shape)


def in_order(own, other, high):
    return jnp.where(high == 0, jnp.concatenate([own, other]), jnp.concatenate([other, own]))


def on_device(ctx_in, resid, enc_out_w, slide_proj, qkv_w, tissue, kept_count, dilation):
    core = lax.axis_index("core")
    high = lax.axis_index("zhi")
    plane_id = lax.axis_index("y") * lax.axis_size("x") + lax.axis_index("x")

    w_own = lax.dynamic_slice_in_dim(enc_out_w, core * D, D, 0).T
    p_split = slide_proj.reshape(PLANES, 2, W_ROWS, P_ROWS)
    p_own = lax.dynamic_index_in_dim(p_split, core, 1, keepdims=False).reshape(D, P_ROWS).T
    q_own = lax.dynamic_slice_in_dim(qkv_w, core * (D // 2), D // 2, 0).T
    near_a = over_plane(copies(w_own))
    w_other = mirrored(w_own)
    p_other = mirrored(p_own)
    q_other = mirrored(q_own)
    q_pair = in_order(q_own, q_other, high)
    place = jnp.stack([core, high, plane_id]).astype(I32)
    res_split = resid[0].reshape(TILE_DEV, PLANES, 2, W_ROWS).transpose(2, 0, 1, 3).reshape(2, TILE_DEV, D)
    own_ctx, own_res, table = prepare(place, kept_count, dilation, ctx_in, res_split, tissue)
    far = copies(jnp.concatenate([w_other, in_order(p_own, p_other, high)]))
    far, near_a, own_ctx, own_res, table, q_pair = hold(far, near_a, own_ctx, own_res, table, q_pair)
    q_a = lax.all_gather(q_pair, PLANE, axis=0, tiled=True)
    far_a, near_a = hold(over_plane(far), near_a)
    near_a = near_a.reshape(D, D)
    near_b = other_core(near_a)
    far_b = other_core(far_a)
    embedded, rims = embed(table, own_ctx, own_res, near_a, near_b, far_a, far_b)
    rims = quarter_way(rims)
    q_a, embedded = hold(q_a, embedded)
    q_b = other_core(q_a)
    q_b, rims = hold(q_b, rims)
    payload, q_rows, kv_rows = project(table, embedded, q_a, q_b)
    arrived, rims = hold(lax.all_to_all(payload, PLANE, 0, 0), rims)
    other = across(pack(arrived))
    own_sum, own_best, own_total = far_own(table, arrived)
    before, after = to_next(rims[:HALF], 1), to_next(rims[HALF:], -1)
    other, own_sum, before, after = hold(other, own_sum, before, after)
    answer = far_rest(table, arrived, other, own_sum, own_best, own_total)
    q_rows, answer = hold(q_rows, answer)
    local_sum, local_best, local_total = local_branch(table, q_rows, kv_rows, before, after, q_a, q_b)
    answers = lax.all_to_all(answer, PLANE, 0, 0)
    return finish(table, answers, local_sum, local_best, local_total, tissue)


def solution(mesh):
    devices = mesh.devices.reshape(-1, 2, 4, 4, 2)
    split = Mesh(devices, ("zlo", "core", "y", "x", "zhi"))
    slide, seq = ("zlo", "core"), ("y", "x", "zhi")
    return jax.shard_map(
        on_device,
        mesh=split,
        in_specs=(
            P(slide, seq, None),
            P(slide, seq, None),
            P(None, seq),
            P(None, seq),
            P(None, seq),
            P(slide, seq, None),
            P(slide, None),
            P(slide, None),
        ),
        out_specs=P(slide, seq, None),
        check_vma=False,
    )
```

```python
import jax
import jax.numpy as jnp
from jax import lax
from jax.experimental import pallas as pl
from jax.experimental.pallas import tpu as pltpu
from jax.sharding import Mesh, PartitionSpec as P

HEADS = 16
HEAD_DIM = 48
D = 768
D_ENC = 1536
HALF = 64
TILE_DEV = 192
SEQ_LEN = 4096
SLOTS = 48
LANES = 128
W_ROWS = 48
P_ROWS = 24
PLANES = 16
PLANE = ("y", "x")
EVERY = ("zlo", "core", "y", "x", "zhi")
NORM_EPS = 1e-06
BIG_NEGATIVE = -1e30
SCALE = HEAD_DIM**-0.5
BF16 = jnp.bfloat16
F32 = jnp.float32
I32 = jnp.int32
VMEM_LIMIT = 24 * 1024 * 1024

CORE, HIGH, PLANE_ID, RATE, SEGMENT, START_ME, COUNT_ME = range(7)
ALL_STARTS = 8
ALL_COUNTS = 40
BLOCKS = 32


def dot_nn(a, b):
    return lax.dot_general(a, b, (((1,), (0,)), ((), ())), preferred_element_type=F32)


def dot_nt(a, b):
    return lax.dot_general(a, b, (((1,), (1,)), ((), ())), preferred_element_type=F32)


def dot_tn(a, b):
    return lax.dot_general(a, b, (((0,), (0,)), ((), ())), preferred_element_type=F32)


def iota(shape, dim):
    return lax.broadcasted_iota(I32, shape, dim)


def call(kernel, name, out_shape, specs, scratch, flops, size, exps=0):
    vmem = pl.BlockSpec(memory_space=pltpu.VMEM)
    smem = pl.BlockSpec(memory_space=pltpu.SMEM)
    hbm = pl.BlockSpec(memory_space=pl.ANY)
    kinds = {"s": smem, "v": vmem, "h": hbm}
    ins, outs = specs.split("-")
    return pl.pallas_call(
        kernel,
        out_shape=tuple(jax.ShapeDtypeStruct(shape, dtype) for shape, dtype in out_shape),
        in_specs=[kinds[c] for c in ins],
        out_specs=tuple(kinds[c] for c in outs),
        scratch_shapes=scratch,
        compiler_params=pltpu.CompilerParams(vmem_limit_bytes=VMEM_LIMIT),
        cost_estimate=pl.CostEstimate(flops=flops, bytes_accessed=size, transcendentals=exps),
        name=name,
    )


def prepare_kernel(place, counts, dilation, ctx, res, listing, own_ctx, own_res, table):
    table[CORE], table[HIGH], table[PLANE_ID] = place[0], place[1], place[2]
    table[RATE], table[SEGMENT] = dilation[0, 1], dilation[0, 0]
    me = place[2] * 2 + place[1]
    start = jnp.int32(0)
    for b in range(BLOCKS):
        count = counts[0, b]
        table[ALL_STARTS + b] = start
        table[ALL_COUNTS + b] = count

        @pl.when(me == b)
        def _(start=start, count=count):
            table[START_ME] = start
            table[COUNT_ME] = count

        start = start + count
    order = (iota((TILE_DEV, TILE_DEV), 0) == listing[0]).astype(BF16)
    own_ctx[...] = dot_tn(order, ctx[0]).astype(BF16)
    for z in range(2):
        own_res[z] = dot_tn(order, res[z]).astype(BF16)


def prepare(*args):
    shapes = (((TILE_DEV, D_ENC), BF16), ((2, TILE_DEV, D), BF16), ((ALL_COUNTS + BLOCKS,), I32))
    return call(prepare_kernel, "prepare_rows", shapes, "sssvvv-vvs", [], 250_000_000, 2_400_000)(*args)


def halves(table, ref, width):
    core = table[CORE]
    first = ref[:, pl.ds(pl.multiple_of(core * width, LANES), width)]
    second = ref[:, pl.ds(pl.multiple_of((1 - core) * width, LANES), width)]
    return first, second


def embed_kernel(table, ctx, res, near_a, near_b, far_a, far_b, out, rims, hidden, normed):
    core, high = table[CORE], table[HIGH]
    first, second = halves(table, ctx, D)
    near = dot_nt(first, near_a[...]) + dot_nt(second, near_b[...]) + res[high].astype(F32)
    hidden[0] = near
    far = dot_nt(first, far_a[:, :W_ROWS].reshape(D, D)) + dot_nt(second, far_b[:, :W_ROWS].reshape(D, D))
    far += res[1 - high].astype(F32)
    hidden[1] = far
    mean = (jnp.sum(near, axis=1, keepdims=True) + jnp.sum(far, axis=1, keepdims=True)) / D_ENC
    near, far = hidden[0] - mean, hidden[1] - mean
    spread = (jnp.sum(near * near, axis=1, keepdims=True) + jnp.sum(far * far, axis=1, keepdims=True)) / D_ENC
    scale = lax.rsqrt(spread + NORM_EPS)
    normed[high] = (near * scale).astype(BF16)
    normed[1 - high] = (far * scale).astype(BF16)
    total = dot_nt(normed[core], far_a[:, W_ROWS:].reshape(D, D))
    total += dot_nt(normed[1 - core], far_b[:, W_ROWS:].reshape(D, D))
    out[...] = total.astype(BF16)
    lane = iota((HALF, TILE_DEV), 1)
    pick = (lane == iota((HALF, TILE_DEV), 0) + (table[COUNT_ME] - HALF)).astype(BF16)
    rims[:HALF] = dot_nn(pick, out[...]).astype(BF16)
    rims[HALF:] = out[:HALF]


def embed(*args):
    scratch = [pltpu.VMEM((2, TILE_DEV, D), F32), pltpu.VMEM((2, TILE_DEV, D), BF16)]
    shapes = (((TILE_DEV, D), BF16), ((2 * HALF, D), BF16))
    return call(embed_kernel, "embed_rows", shapes, "svvvvvv-vv", scratch, 1_400_000_000, 9_000_000)(*args)


def project_kernel(table, own, q_a, q_b, payload, q_out, kv_out):
    rate, start_me = table[RATE], table[START_ME]
    first, second = halves(table, own, D // 2)
    q_out[...] = (dot_nt(q_a[:D], first) + dot_nt(q_b[:D], second)).astype(BF16)
    for n in range(2):
        rows = slice((n + 1) * D, (n + 2) * D)
        kv_out[n * D : (n + 1) * D] = (dot_nt(q_a[rows], first) + dot_nt(q_b[rows], second)).astype(BF16)
    slot = iota((SLOTS, TILE_DEV), 0) * rate
    lane = iota((SLOTS, TILE_DEV), 1)
    key_rest = jnp.zeros((LANES - 2 * HEAD_DIM, TILE_DEV), BF16)
    query_rest = jnp.zeros((LANES - HEAD_DIM, TILE_DEV), BF16)
    for h in range(HEADS):
        rows = slice(h * HEAD_DIM, (h + 1) * HEAD_DIM)
        pick = (lane == slot + ((h - start_me) & (rate - 1))).astype(BF16)
        both = jnp.concatenate([kv_out[rows], kv_out[D + h * HEAD_DIM : D + (h + 1) * HEAD_DIM], key_rest], axis=0)
        ask = jnp.concatenate([q_out[rows], query_rest], axis=0)
        payload[h, :SLOTS] = dot_nt(pick, both).astype(BF16)
        payload[h, SLOTS:] = dot_nt(pick, ask).astype(BF16)


def project(*args):
    shapes = (((HEADS, 2 * SLOTS, LANES), BF16), ((D, TILE_DEV), BF16), ((2 * D, TILE_DEV), BF16))
    return call(project_kernel, "project_rows", shapes, "svvv-vvv", [], 1_000_000_000, 5_000_000)(*args)


def pack_kernel(arrived, out):
    rows = arrived[:, :SLOTS].reshape(PLANES * SLOTS, LANES)
    out[...] = rows.T[: 2 * HEAD_DIM]


def pack(*args):
    shapes = (((2 * HEAD_DIM, PLANES * SLOTS), BF16),)
    return call(pack_kernel, "pack_keys", shapes, "v-v", [], 1_000_000, 500_000)(*args)[0]


def local_kernel(table, q, kv, before, after, q_a, q_b, out_sum, out_best, out_total, rims, rim):
    start_me, count_me = table[START_ME], table[COUNT_ME]
    rims[:HALF] = before[...]
    rims[HALF:] = after[...]
    first, second = halves(table, rims, D // 2)
    rim[...] = (dot_nt(q_a[D:], first) + dot_nt(q_b[D:], second)).astype(BF16)
    length = jnp.full((1, 1), table[SEGMENT], I32).astype(F32)

    def segment(position):
        return jnp.floor((position.astype(F32) + 0.5) / length)

    query_seg = segment(start_me + iota((1, TILE_DEV), 1))
    key_at = iota((TILE_DEV, 1), 0)
    key_seg = jnp.where(key_at < count_me, segment(start_me + key_at), -1.0)
    rim_id = iota((2 * HALF, 1), 0)
    rim_at = start_me + jnp.where(rim_id < HALF, rim_id - HALF, rim_id - HALF + count_me)
    rim_seg = jnp.where((rim_at >= 0) & (rim_at < SEQ_LEN), segment(rim_at), -1.0)
    key_ok, rim_ok = key_seg == query_seg, rim_seg == query_seg
    for h in range(HEADS):
        rows = slice(h * HEAD_DIM, (h + 1) * HEAD_DIM)
        v_rows = slice(D + h * HEAD_DIM, D + (h + 1) * HEAD_DIM)
        scores = jnp.where(key_ok, dot_tn(kv[rows], q[rows]) * SCALE, BIG_NEGATIVE)
        rim_scores = jnp.where(rim_ok, dot_tn(rim[rows], q[rows]) * SCALE, BIG_NEGATIVE)
        best = jnp.maximum(jnp.max(scores, axis=0, keepdims=True), jnp.max(rim_scores, axis=0, keepdims=True))
        weights, rim_weights = jnp.exp(scores - best), jnp.exp(rim_scores - best)
        out_best[h : h + 1] = best
        out_total[h : h + 1] = jnp.sum(weights, axis=0, keepdims=True) + jnp.sum(rim_weights, axis=0, keepdims=True)
        out_sum[rows] = dot_nn(kv[v_rows], weights.astype(BF16)) + dot_nn(rim[v_rows], rim_weights.astype(BF16))


def local_branch(*args):
    stat = ((HEADS, TILE_DEV), F32)
    shapes = (((D, TILE_DEV), F32), stat, stat)
    scratch = [pltpu.VMEM((2 * HALF, D), BF16), pltpu.VMEM((2 * D, 2 * HALF), BF16)]
    return call(local_kernel, "local_branch", shapes, "svvvvvv-vvv", scratch, 600_000_000, 5_000_000, 1_000_000)(*args)


def far_scores(table, high, keys, asks, scores):
    rate = table[RATE]
    slot = iota((SLOTS, asks.shape[0]), 0) * rate
    best = jnp.full((1, asks.shape[0]), BIG_NEGATIVE, F32)
    for p in range(PLANES):
        block = 2 * p + high
        phase = (table[PLANE_ID] - table[ALL_STARTS + block]) & (rate - 1)
        piece = dot_nt(keys[p * SLOTS : (p + 1) * SLOTS], asks) * SCALE
        piece = jnp.where(slot + phase < table[ALL_COUNTS + block], piece, BIG_NEGATIVE)
        scores[p * SLOTS : (p + 1) * SLOTS] = piece
        best = jnp.maximum(best, jnp.max(piece, axis=0, keepdims=True))
    return best


FAR_GROUP = 8
FAR_WIDTH = FAR_GROUP * SLOTS


def far_own_kernel(table, arrived, out_sum, out_best, out_total, scores):
    keys = arrived[:, :SLOTS].reshape(PLANES * SLOTS, LANES)
    for n in range(PLANES // FAR_GROUP):
        lanes = slice(n * FAR_WIDTH, (n + 1) * FAR_WIDTH)
        asks = arrived[n * FAR_GROUP : (n + 1) * FAR_GROUP, SLOTS:].reshape(FAR_WIDTH, LANES)
        best = far_scores(table, table[HIGH], keys, asks, scores)
        weights = jnp.exp(scores[...] - best)
        out_best[:, lanes] = best
        out_total[:, lanes] = jnp.sum(weights, axis=0, keepdims=True)
        out_sum[:, lanes] = dot_tn(keys, weights.astype(BF16))[HEAD_DIM : 2 * HEAD_DIM]


def far_own(*args):
    width = PLANES * SLOTS
    shapes = (((HEAD_DIM, width), F32), ((1, width), F32), ((1, width), F32))
    scratch = [pltpu.VMEM((width, FAR_WIDTH), F32)]
    return call(far_own_kernel, "far_own", shapes, "sv-vvv", scratch, 300_000_000, 700_000, 600_000)(*args)


def far_rest_kernel(table, arrived, other, own_sum, own_best, own_total, answer, scores):
    other_t = other[...]
    keys = other_t.T
    values = other_t[HEAD_DIM:]
    for n in range(PLANES // FAR_GROUP):
        lanes = slice(n * FAR_WIDTH, (n + 1) * FAR_WIDTH)
        asks = arrived[n * FAR_GROUP : (n + 1) * FAR_GROUP, SLOTS:].reshape(FAR_WIDTH, LANES)[:, : 2 * HEAD_DIM]
        best_o = own_best[:, lanes]
        best = jnp.maximum(best_o, far_scores(table, 1 - table[HIGH], keys, asks, scores))
        weights = jnp.exp(scores[...] - best)
        scale_o = jnp.exp(best_o - best)
        total = jnp.sum(weights, axis=0, keepdims=True) + scale_o * own_total[:, lanes]
        summed = dot_nn(values, weights.astype(BF16)) + scale_o * own_sum[:, lanes]
        shared = summed / total
        log_all = best + jnp.log(total)
        log_a = log_all.astype(BF16).astype(F32)
        log_b = (log_all - log_a).astype(BF16).astype(F32)
        log_c = log_all - log_a - log_b
        row = iota((LANES - HEAD_DIM, FAR_WIDTH), 0)
        tail = jnp.where(row == 0, log_a, jnp.where(row == 1, log_b, jnp.where(row == 2, log_c, 0.0)))
        block = jnp.concatenate([shared, tail], axis=0)
        answer[n * FAR_GROUP : (n + 1) * FAR_GROUP] = block.T.astype(BF16).reshape(FAR_GROUP, SLOTS, LANES)


def far_rest(*args):
    shapes = (((PLANES, SLOTS, LANES), BF16),)
    scratch = [pltpu.VMEM((PLANES * SLOTS, FAR_WIDTH), F32)]
    return call(far_rest_kernel, "far_rest", shapes, "svvvvv-v", scratch, 300_000_000, 1_000_000, 600_000)(*args)[0]


def finish_kernel(table, answers, local_sum, local_best, local_total, listing, out, attended):
    rate = table[RATE]
    slot = iota((SLOTS, TILE_DEV), 0) * rate
    lane = iota((SLOTS, TILE_DEV), 1)
    row = iota((1, TILE_DEV), 1)
    live = row < table[COUNT_ME]
    for h in range(HEADS):
        rows = slice(h * HEAD_DIM, (h + 1) * HEAD_DIM)
        phase = (h - table[START_ME]) & (rate - 1)
        pick = (lane == slot + phase).astype(BF16)
        wide = dot_tn(answers[h], pick)
        log_all = wide[HEAD_DIM : HEAD_DIM + 1] + wide[HEAD_DIM + 1 : HEAD_DIM + 2] + wide[HEAD_DIM + 2 : HEAD_DIM + 3]
        log_all = jnp.where((row & (rate - 1)) == phase, log_all, BIG_NEGATIVE)
        best = local_best[h : h + 1]
        joint = jnp.maximum(best, log_all)
        near = jnp.exp(best - joint)
        far = jnp.exp(log_all - joint)
        below = jnp.where(live, near * local_total[h : h + 1] + far, 1.0)
        mixed = (near * local_sum[rows] + far * wide[:HEAD_DIM]) / below
        attended[rows] = jnp.where(live, mixed, 0.0).astype(BF16)
    back = (listing[0] == iota((TILE_DEV, TILE_DEV), 0)).astype(BF16)
    out[0] = dot_nt(back, attended[...]).astype(BF16)


def finish(*args):
    shapes = (((1, TILE_DEV, D), BF16),)
    scratch = [pltpu.VMEM((D, TILE_DEV), BF16)]
    return call(finish_kernel, "finish_rows", shapes, "svvvvv-v", scratch, 100_000_000, 1_500_000, 10_000)(*args)[0]


def mirrored(x):
    z_low = lax.axis_size("zlo")
    pairs = [
        (low * 2 + high, (z_low - 1 - low) * 2 + (1 - high))
        for low in range(z_low)
        for high in range(2)
    ]
    return lax.ppermute(x, ("zlo", "zhi"), pairs)


def across(x):
    return lax.ppermute(x, "zhi", [(0, 1), (1, 0)])


def rank(z, core, plane):
    z_low = lax.axis_size("zlo")
    return ((z % z_low * 2 + core) * PLANES + plane) * 2 + z // z_low


def all_places():
    z_size = 2 * lax.axis_size("zlo")
    return [(z, core, plane) for z in range(z_size) for core in range(2) for plane in range(PLANES)]


def toward(z, core):
    z_size = 2 * lax.axis_size("zlo")
    step = z_size // 4
    return (z + (step if core == 0 else -step)) % z_size


def quarter_way(x):
    pairs = [(rank(z, core, plane), rank(toward(z, core), core, plane)) for z, core, plane in all_places()]
    return lax.ppermute(x, EVERY, pairs)


def to_next(x, sign):
    pairs = []
    z_low = lax.axis_size("zlo")
    for z, core, plane in all_places():
        half_way = toward(z, core)
        block = 2 * plane + z // z_low + sign
        if 0 <= block < 2 * PLANES:
            target = rank(z % z_low + z_low * (block % 2), core, block // 2)
            pairs.append((rank(half_way, core, plane), target))
    return lax.ppermute(x, EVERY, pairs)


def other_core(x):
    return lax.ppermute(x, "core", [(0, 1), (1, 0)])


def over_plane(x):
    return lax.all_to_all(x, PLANE, 0, 0)


def hold(*values):
    return lax.optimization_barrier(values)


def copies(x):
    return jnp.broadcast_to(x[None], (PLANES,) + x.shape)


def in_order(own, other, high):
    return jnp.where(high == 0, jnp.concatenate([own, other]), jnp.concatenate([other, own]))


def on_device(ctx_in, resid, enc_out_w, slide_proj, qkv_w, tissue, kept_count, dilation):
    core = lax.axis_index("core")
    high = lax.axis_index("zhi")
    plane_id = lax.axis_index("y") * lax.axis_size("x") + lax.axis_index("x")

    w_own = lax.dynamic_slice_in_dim(enc_out_w, core * D, D, 0).T
    p_split = slide_proj.reshape(PLANES, 2, W_ROWS, P_ROWS)
    p_own = lax.dynamic_index_in_dim(p_split, core, 1, keepdims=False).reshape(D, P_ROWS).T
    q_own = lax.dynamic_slice_in_dim(qkv_w, core * (D // 2), D // 2, 0).T
    near_a = over_plane(copies(w_own))
    w_other = mirrored(w_own)
    p_other = mirrored(p_own)
    q_other = mirrored(q_own)
    q_both = copies(in_order(q_own, q_other, high))
    place = jnp.stack([core, high, plane_id]).astype(I32)
    res_split = resid[0].reshape(TILE_DEV, PLANES, 2, W_ROWS).transpose(2, 0, 1, 3).reshape(2, TILE_DEV, D)
    own_ctx, own_res, table = prepare(place, kept_count, dilation, ctx_in, res_split, tissue)
    far = copies(jnp.concatenate([w_other, in_order(p_own, p_other, high)]))
    far, near_a, own_ctx, own_res, table, q_both = hold(far, near_a, own_ctx, own_res, table, q_both)
    far_a, q_both, near_a = hold(over_plane(far), q_both, near_a)
    q_a, far_a, near_a = hold(over_plane(q_both), far_a, near_a)
    near_a, q_a = near_a.reshape(D, D), q_a.reshape(3 * D, D // 2)
    near_b = other_core(near_a)
    far_b = other_core(far_a)
    q_b = other_core(q_a)
    embedded, rims = embed(table, own_ctx, own_res, near_a, near_b, far_a, far_b)
    rims = quarter_way(rims)
    payload, q_rows, kv_rows = project(table, embedded, q_a, q_b)
    arrived, rims = hold(lax.all_to_all(payload, PLANE, 0, 0), rims)
    other = across(pack(arrived))
    own_sum, own_best, own_total = far_own(table, arrived)
    before, after = to_next(rims[:HALF], 1), to_next(rims[HALF:], -1)
    other, own_sum, before, after = hold(other, own_sum, before, after)
    answer = far_rest(table, arrived, other, own_sum, own_best, own_total)
    q_rows, answer = hold(q_rows, answer)
    local_sum, local_best, local_total = local_branch(table, q_rows, kv_rows, before, after, q_a, q_b)
    answers = lax.all_to_all(answer, PLANE, 0, 0)
    return finish(table, answers, local_sum, local_best, local_total, tissue)


def solution(mesh):
    devices = mesh.devices.reshape(-1, 2, 4, 4, 2)
    split = Mesh(devices, ("zlo", "core", "y", "x", "zhi"))
    slide, seq = ("zlo", "core"), ("y", "x", "zhi")
    return jax.shard_map(
        on_device,
        mesh=split,
        in_specs=(
            P(slide, seq, None),
            P(slide, seq, None),
            P(None, seq),
            P(None, seq),
            P(None, seq),
            P(slide, seq, None),
            P(slide, None),
            P(slide, None),
        ),
        out_specs=P(slide, seq, None),
        check_vma=False,
    )
```

```python
import jax
import jax.numpy as jnp
from jax import lax
from jax.experimental import pallas as pl
from jax.experimental.pallas import tpu as pltpu
from jax.sharding import Mesh, PartitionSpec as P

HEADS = 16
HEAD_DIM = 48
D = 768
D_ENC = 1536
HALF = 64
TILE_DEV = 192
SEQ_LEN = 4096
SLOTS = 48
LANES = 128
W_ROWS = 48
P_ROWS = 24
PLANES = 16
PLANE = ("y", "x")
SEQ = ("y", "x", "zhi")
NORM_EPS = 1e-06
BIG_NEGATIVE = -1e30
SCALE = HEAD_DIM**-0.5
BF16 = jnp.bfloat16
F32 = jnp.float32
I32 = jnp.int32
VMEM_LIMIT = 24 * 1024 * 1024

CORE, HIGH, PLANE_ID, RATE, SEGMENT, START_ME, COUNT_ME = range(7)
ALL_STARTS = 8
ALL_COUNTS = 40
BLOCKS = 32


def dot_nn(a, b):
    return lax.dot_general(a, b, (((1,), (0,)), ((), ())), preferred_element_type=F32)


def dot_nt(a, b):
    return lax.dot_general(a, b, (((1,), (1,)), ((), ())), preferred_element_type=F32)


def dot_tn(a, b):
    return lax.dot_general(a, b, (((0,), (0,)), ((), ())), preferred_element_type=F32)


def iota(shape, dim):
    return lax.broadcasted_iota(I32, shape, dim)


def call(kernel, name, out_shape, specs, scratch, flops, size, exps=0):
    vmem = pl.BlockSpec(memory_space=pltpu.VMEM)
    smem = pl.BlockSpec(memory_space=pltpu.SMEM)
    hbm = pl.BlockSpec(memory_space=pl.ANY)
    kinds = {"s": smem, "v": vmem, "h": hbm}
    ins, outs = specs.split("-")
    return pl.pallas_call(
        kernel,
        out_shape=tuple(jax.ShapeDtypeStruct(shape, dtype) for shape, dtype in out_shape),
        in_specs=[kinds[c] for c in ins],
        out_specs=tuple(kinds[c] for c in outs),
        scratch_shapes=scratch,
        compiler_params=pltpu.CompilerParams(vmem_limit_bytes=VMEM_LIMIT),
        cost_estimate=pl.CostEstimate(flops=flops, bytes_accessed=size, transcendentals=exps),
        name=name,
    )


def prepare_kernel(place, counts, dilation, ctx, res, listing, own_ctx, own_res, table):
    table[CORE], table[HIGH], table[PLANE_ID] = place[0], place[1], place[2]
    table[RATE], table[SEGMENT] = dilation[0, 1], dilation[0, 0]
    me = place[2] * 2 + place[1]
    start = jnp.int32(0)
    for b in range(BLOCKS):
        count = counts[0, b]
        table[ALL_STARTS + b] = start
        table[ALL_COUNTS + b] = count

        @pl.when(me == b)
        def _(start=start, count=count):
            table[START_ME] = start
            table[COUNT_ME] = count

        start = start + count
    order = (iota((TILE_DEV, TILE_DEV), 0) == listing[0]).astype(BF16)
    own_ctx[...] = dot_tn(order, ctx[0]).astype(BF16)
    for z in range(2):
        own_res[z] = dot_tn(order, res[z]).astype(BF16)


def prepare(*args):
    shapes = (((TILE_DEV, D_ENC), BF16), ((2, TILE_DEV, D), BF16), ((ALL_COUNTS + BLOCKS,), I32))
    return call(prepare_kernel, "prepare_rows", shapes, "sssvvv-vvs", [], 250_000_000, 2_400_000)(*args)


def halves(table, ref, width):
    core = table[CORE]
    first = ref[:, pl.ds(pl.multiple_of(core * width, LANES), width)]
    second = ref[:, pl.ds(pl.multiple_of((1 - core) * width, LANES), width)]
    return first, second


def embed_kernel(table, ctx, res, near_a, near_b, far_a, far_b, out, tail, head, hidden, normed):
    core, high = table[CORE], table[HIGH]
    first, second = halves(table, ctx, D)
    near = dot_nt(first, near_a[...]) + dot_nt(second, near_b[...]) + res[high].astype(F32)
    hidden[0] = near
    far = dot_nt(first, far_a[:, :W_ROWS].reshape(D, D)) + dot_nt(second, far_b[:, :W_ROWS].reshape(D, D))
    far += res[1 - high].astype(F32)
    hidden[1] = far
    mean = (jnp.sum(near, axis=1, keepdims=True) + jnp.sum(far, axis=1, keepdims=True)) / D_ENC
    near, far = hidden[0] - mean, hidden[1] - mean
    spread = (jnp.sum(near * near, axis=1, keepdims=True) + jnp.sum(far * far, axis=1, keepdims=True)) / D_ENC
    scale = lax.rsqrt(spread + NORM_EPS)
    normed[high] = (near * scale).astype(BF16)
    normed[1 - high] = (far * scale).astype(BF16)
    total = dot_nt(normed[core], far_a[:, W_ROWS:].reshape(D, D))
    total += dot_nt(normed[1 - core], far_b[:, W_ROWS:].reshape(D, D))
    out[...] = total.astype(BF16)
    lane = iota((HALF, TILE_DEV), 1)
    pick = (lane == iota((HALF, TILE_DEV), 0) + (table[COUNT_ME] - HALF)).astype(BF16)
    tail[...] = dot_nn(pick, out[...]).astype(BF16)
    head[...] = out[:HALF]


def embed(*args):
    scratch = [pltpu.VMEM((2, TILE_DEV, D), F32), pltpu.VMEM((2, TILE_DEV, D), BF16)]
    shapes = (((TILE_DEV, D), BF16), ((HALF, D), BF16), ((HALF, D), BF16))
    return call(embed_kernel, "embed_rows", shapes, "svvvvvv-vvv", scratch, 1_400_000_000, 9_000_000)(*args)


def project_kernel(table, own, q_a, q_b, payload, q_out, kv_out):
    rate, start_me = table[RATE], table[START_ME]
    first, second = halves(table, own, D // 2)
    q_out[...] = (dot_nt(q_a[:D], first) + dot_nt(q_b[:D], second)).astype(BF16)
    for n in range(2):
        rows = slice((n + 1) * D, (n + 2) * D)
        kv_out[n * D : (n + 1) * D] = (dot_nt(q_a[rows], first) + dot_nt(q_b[rows], second)).astype(BF16)
    slot = iota((SLOTS, TILE_DEV), 0) * rate
    lane = iota((SLOTS, TILE_DEV), 1)
    key_rest = jnp.zeros((LANES - 2 * HEAD_DIM, TILE_DEV), BF16)
    query_rest = jnp.zeros((LANES - HEAD_DIM, TILE_DEV), BF16)
    for h in range(HEADS):
        rows = slice(h * HEAD_DIM, (h + 1) * HEAD_DIM)
        pick = (lane == slot + ((h - start_me) & (rate - 1))).astype(BF16)
        both = jnp.concatenate([kv_out[rows], kv_out[D + h * HEAD_DIM : D + (h + 1) * HEAD_DIM], key_rest], axis=0)
        ask = jnp.concatenate([q_out[rows], query_rest], axis=0)
        payload[h, :SLOTS] = dot_nt(pick, both).astype(BF16)
        payload[h, SLOTS:] = dot_nt(pick, ask).astype(BF16)


def project(*args):
    shapes = (((HEADS, 2 * SLOTS, LANES), BF16), ((D, TILE_DEV), BF16), ((2 * D, TILE_DEV), BF16))
    return call(project_kernel, "project_rows", shapes, "svvv-vvv", [], 1_000_000_000, 5_000_000)(*args)


def pack_kernel(arrived, out):
    rows = arrived[:, :SLOTS].reshape(PLANES * SLOTS, LANES)
    out[...] = rows.T[: 2 * HEAD_DIM]


def pack(*args):
    shapes = (((2 * HEAD_DIM, PLANES * SLOTS), BF16),)
    return call(pack_kernel, "pack_keys", shapes, "v-v", [], 1_000_000, 500_000)(*args)[0]


def local_kernel(table, q, kv, before, after, q_a, q_b, out_sum, out_best, out_total, rims, rim):
    start_me, count_me = table[START_ME], table[COUNT_ME]
    rims[:HALF] = before[...]
    rims[HALF:] = after[...]
    first, second = halves(table, rims, D // 2)
    rim[...] = (dot_nt(q_a[D:], first) + dot_nt(q_b[D:], second)).astype(BF16)
    length = jnp.full((1, 1), table[SEGMENT], I32).astype(F32)

    def segment(position):
        return jnp.floor((position.astype(F32) + 0.5) / length)

    query_seg = segment(start_me + iota((1, TILE_DEV), 1))
    key_at = iota((TILE_DEV, 1), 0)
    key_seg = jnp.where(key_at < count_me, segment(start_me + key_at), -1.0)
    rim_id = iota((2 * HALF, 1), 0)
    rim_at = start_me + jnp.where(rim_id < HALF, rim_id - HALF, rim_id - HALF + count_me)
    rim_seg = jnp.where((rim_at >= 0) & (rim_at < SEQ_LEN), segment(rim_at), -1.0)
    key_ok, rim_ok = key_seg == query_seg, rim_seg == query_seg
    for h in range(HEADS):
        rows = slice(h * HEAD_DIM, (h + 1) * HEAD_DIM)
        v_rows = slice(D + h * HEAD_DIM, D + (h + 1) * HEAD_DIM)
        scores = jnp.where(key_ok, dot_tn(kv[rows], q[rows]) * SCALE, BIG_NEGATIVE)
        rim_scores = jnp.where(rim_ok, dot_tn(rim[rows], q[rows]) * SCALE, BIG_NEGATIVE)
        best = jnp.maximum(jnp.max(scores, axis=0, keepdims=True), jnp.max(rim_scores, axis=0, keepdims=True))
        weights, rim_weights = jnp.exp(scores - best), jnp.exp(rim_scores - best)
        out_best[h : h + 1] = best
        out_total[h : h + 1] = jnp.sum(weights, axis=0, keepdims=True) + jnp.sum(rim_weights, axis=0, keepdims=True)
        out_sum[rows] = dot_nn(kv[v_rows], weights.astype(BF16)) + dot_nn(rim[v_rows], rim_weights.astype(BF16))


def local_branch(*args):
    stat = ((HEADS, TILE_DEV), F32)
    shapes = (((D, TILE_DEV), F32), stat, stat)
    scratch = [pltpu.VMEM((2 * HALF, D), BF16), pltpu.VMEM((2 * D, 2 * HALF), BF16)]
    return call(local_kernel, "local_branch", shapes, "svvvvvv-vvv", scratch, 600_000_000, 5_000_000, 1_000_000)(*args)


def far_scores(table, high, keys, asks, scores):
    rate = table[RATE]
    slot = iota((SLOTS, asks.shape[0]), 0) * rate
    best = jnp.full((1, asks.shape[0]), BIG_NEGATIVE, F32)
    for p in range(PLANES):
        block = 2 * p + high
        phase = (table[PLANE_ID] - table[ALL_STARTS + block]) & (rate - 1)
        piece = dot_nt(keys[p * SLOTS : (p + 1) * SLOTS], asks) * SCALE
        piece = jnp.where(slot + phase < table[ALL_COUNTS + block], piece, BIG_NEGATIVE)
        scores[p * SLOTS : (p + 1) * SLOTS] = piece
        best = jnp.maximum(best, jnp.max(piece, axis=0, keepdims=True))
    return best


FAR_GROUP = 8
FAR_WIDTH = FAR_GROUP * SLOTS


def far_own_kernel(table, arrived, out_sum, out_best, out_total, scores):
    keys = arrived[:, :SLOTS].reshape(PLANES * SLOTS, LANES)
    for n in range(PLANES // FAR_GROUP):
        lanes = slice(n * FAR_WIDTH, (n + 1) * FAR_WIDTH)
        asks = arrived[n * FAR_GROUP : (n + 1) * FAR_GROUP, SLOTS:].reshape(FAR_WIDTH, LANES)
        best = far_scores(table, table[HIGH], keys, asks, scores)
        weights = jnp.exp(scores[...] - best)
        out_best[:, lanes] = best
        out_total[:, lanes] = jnp.sum(weights, axis=0, keepdims=True)
        out_sum[:, lanes] = dot_tn(keys, weights.astype(BF16))[HEAD_DIM : 2 * HEAD_DIM]


def far_own(*args):
    width = PLANES * SLOTS
    shapes = (((HEAD_DIM, width), F32), ((1, width), F32), ((1, width), F32))
    scratch = [pltpu.VMEM((width, FAR_WIDTH), F32)]
    return call(far_own_kernel, "far_own", shapes, "sv-vvv", scratch, 300_000_000, 700_000, 600_000)(*args)


def far_rest_kernel(table, arrived, other, own_sum, own_best, own_total, answer, scores):
    other_t = other[...]
    keys = other_t.T
    values = other_t[HEAD_DIM:]
    for n in range(PLANES // FAR_GROUP):
        lanes = slice(n * FAR_WIDTH, (n + 1) * FAR_WIDTH)
        asks = arrived[n * FAR_GROUP : (n + 1) * FAR_GROUP, SLOTS:].reshape(FAR_WIDTH, LANES)[:, : 2 * HEAD_DIM]
        best_o = own_best[:, lanes]
        best = jnp.maximum(best_o, far_scores(table, 1 - table[HIGH], keys, asks, scores))
        weights = jnp.exp(scores[...] - best)
        scale_o = jnp.exp(best_o - best)
        total = jnp.sum(weights, axis=0, keepdims=True) + scale_o * own_total[:, lanes]
        summed = dot_nn(values, weights.astype(BF16)) + scale_o * own_sum[:, lanes]
        shared = summed / total
        log_all = best + jnp.log(total)
        log_a = log_all.astype(BF16).astype(F32)
        log_b = (log_all - log_a).astype(BF16).astype(F32)
        log_c = log_all - log_a - log_b
        row = iota((LANES - HEAD_DIM, FAR_WIDTH), 0)
        tail = jnp.where(row == 0, log_a, jnp.where(row == 1, log_b, jnp.where(row == 2, log_c, 0.0)))
        block = jnp.concatenate([shared, tail], axis=0)
        answer[n * FAR_GROUP : (n + 1) * FAR_GROUP] = block.T.astype(BF16).reshape(FAR_GROUP, SLOTS, LANES)


def far_rest(*args):
    shapes = (((PLANES, SLOTS, LANES), BF16),)
    scratch = [pltpu.VMEM((PLANES * SLOTS, FAR_WIDTH), F32)]
    return call(far_rest_kernel, "far_rest", shapes, "svvvvv-v", scratch, 300_000_000, 1_000_000, 600_000)(*args)[0]


def finish_kernel(table, answers, local_sum, local_best, local_total, listing, out, attended):
    rate = table[RATE]
    slot = iota((SLOTS, TILE_DEV), 0) * rate
    lane = iota((SLOTS, TILE_DEV), 1)
    row = iota((1, TILE_DEV), 1)
    live = row < table[COUNT_ME]
    for h in range(HEADS):
        rows = slice(h * HEAD_DIM, (h + 1) * HEAD_DIM)
        phase = (h - table[START_ME]) & (rate - 1)
        pick = (lane == slot + phase).astype(BF16)
        wide = dot_tn(answers[h], pick)
        log_all = wide[HEAD_DIM : HEAD_DIM + 1] + wide[HEAD_DIM + 1 : HEAD_DIM + 2] + wide[HEAD_DIM + 2 : HEAD_DIM + 3]
        log_all = jnp.where((row & (rate - 1)) == phase, log_all, BIG_NEGATIVE)
        best = local_best[h : h + 1]
        joint = jnp.maximum(best, log_all)
        near = jnp.exp(best - joint)
        far = jnp.exp(log_all - joint)
        below = jnp.where(live, near * local_total[h : h + 1] + far, 1.0)
        mixed = (near * local_sum[rows] + far * wide[:HEAD_DIM]) / below
        attended[rows] = jnp.where(live, mixed, 0.0).astype(BF16)
    back = (listing[0] == iota((TILE_DEV, TILE_DEV), 0)).astype(BF16)
    out[0] = dot_nt(back, attended[...]).astype(BF16)


def finish(*args):
    shapes = (((1, TILE_DEV, D), BF16),)
    scratch = [pltpu.VMEM((D, TILE_DEV), BF16)]
    return call(finish_kernel, "finish_rows", shapes, "svvvvv-v", scratch, 100_000_000, 1_500_000, 10_000)(*args)[0]


def mirrored(x):
    z_low = lax.axis_size("zlo")
    pairs = [
        (low * 2 + high, (z_low - 1 - low) * 2 + (1 - high))
        for low in range(z_low)
        for high in range(2)
    ]
    return lax.ppermute(x, ("zlo", "zhi"), pairs)


def across(x):
    return lax.ppermute(x, "zhi", [(0, 1), (1, 0)])


def other_core(x):
    return lax.ppermute(x, "core", [(0, 1), (1, 0)])


def over_plane(x):
    return lax.all_to_all(x, PLANE, 0, 0)


def hold(*values):
    return lax.optimization_barrier(values)


def copies(x):
    return jnp.broadcast_to(x[None], (PLANES,) + x.shape)


def in_order(own, other, high):
    return jnp.where(high == 0, jnp.concatenate([own, other]), jnp.concatenate([other, own]))


def on_device(ctx_in, resid, enc_out_w, slide_proj, qkv_w, tissue, kept_count, dilation):
    core = lax.axis_index("core")
    high = lax.axis_index("zhi")
    plane_id = lax.axis_index("y") * lax.axis_size("x") + lax.axis_index("x")

    w_own = lax.dynamic_slice_in_dim(enc_out_w, core * D, D, 0).T
    p_split = slide_proj.reshape(PLANES, 2, W_ROWS, P_ROWS)
    p_own = lax.dynamic_index_in_dim(p_split, core, 1, keepdims=False).reshape(D, P_ROWS).T
    q_own = lax.dynamic_slice_in_dim(qkv_w, core * (D // 2), D // 2, 0).T
    near_a = over_plane(copies(w_own))
    other_wp = mirrored(jnp.concatenate([w_own, p_own]))
    q_other = mirrored(q_own)
    place = jnp.stack([core, high, plane_id]).astype(I32)
    res_split = resid[0].reshape(TILE_DEV, PLANES, 2, W_ROWS).transpose(2, 0, 1, 3).reshape(2, TILE_DEV, D)
    own_ctx, own_res, table = prepare(place, kept_count, dilation, ctx_in, res_split, tissue)
    far = copies(jnp.concatenate([other_wp[:W_ROWS], in_order(p_own, other_wp[W_ROWS:], high)]))
    far, near_a, own_ctx, own_res, table = hold(far, near_a, own_ctx, own_res, table)
    far_a = over_plane(far)
    near_a = near_a.reshape(D, D)
    near_b = other_core(near_a)
    q_both = copies(in_order(q_own, q_other, high))
    far_a, near_b, q_both = hold(far_a, near_b, q_both)
    q_a = over_plane(q_both)
    far_b = other_core(far_a)
    embedded, tail, head = embed(table, own_ctx, own_res, near_a, near_b, far_a, far_b)
    blocks = 2 * PLANES
    before = lax.ppermute(tail, SEQ, [(b, b + 1) for b in range(blocks - 1)])
    after = lax.ppermute(head, SEQ, [(b + 1, b) for b in range(blocks - 1)])
    q_a, embedded, before, after = hold(q_a, embedded, before, after)
    q_a = q_a.reshape(3 * D, D // 2)
    q_b = other_core(q_a)
    payload, q_rows, kv_rows = project(table, embedded, q_a, q_b)
    arrived = lax.all_to_all(payload, PLANE, 0, 0)
    other = across(pack(arrived))
    own_sum, own_best, own_total = far_own(table, arrived)
    local_sum, local_best, local_total = local_branch(table, q_rows, kv_rows, before, after, q_a, q_b)
    other, own_sum, local_sum = hold(other, own_sum, local_sum)
    answer = far_rest(table, arrived, other, own_sum, own_best, own_total)
    answers = lax.all_to_all(answer, PLANE, 0, 0)
    return finish(table, answers, local_sum, local_best, local_total, tissue)


def solution(mesh):
    devices = mesh.devices.reshape(-1, 2, 4, 4, 2)
    split = Mesh(devices, ("zlo", "core", "y", "x", "zhi"))
    slide, seq = ("zlo", "core"), ("y", "x", "zhi")
    return jax.shard_map(
        on_device,
        mesh=split,
        in_specs=(
            P(slide, seq, None),
            P(slide, seq, None),
            P(None, seq),
            P(None, seq),
            P(None, seq),
            P(slide, seq, None),
            P(slide, None),
            P(slide, None),
        ),
        out_specs=P(slide, seq, None),
        check_vma=False,
    )
```

```python
import jax
import jax.numpy as jnp
from jax import lax
from jax.experimental import pallas as pl
from jax.experimental.pallas import tpu as pltpu
from jax.sharding import Mesh, PartitionSpec as P

HEADS = 16
HEAD_DIM = 48
D = 768
D_ENC = 1536
HALF = 64
TILE_DEV = 192
SEQ_LEN = 4096
SLOTS = 48
LANES = 128
W_ROWS = 48
P_ROWS = 24
PLANES = 16
PLANE = ("y", "x")
SEQ = ("y", "x", "zhi")
EVERY = ("zlo", "core", "y", "x", "zhi")
NORM_EPS = 1e-06
BIG_NEGATIVE = -1e30
SCALE = HEAD_DIM**-0.5
BF16 = jnp.bfloat16
F32 = jnp.float32
I32 = jnp.int32
VMEM_LIMIT = 24 * 1024 * 1024

CORE, HIGH, PLANE_ID, RATE, SEGMENT, START_ME, COUNT_ME = range(7)
ALL_STARTS = 8
ALL_COUNTS = 40
BLOCKS = 32


def dot_nn(a, b):
    return lax.dot_general(a, b, (((1,), (0,)), ((), ())), preferred_element_type=F32)


def dot_nt(a, b):
    return lax.dot_general(a, b, (((1,), (1,)), ((), ())), preferred_element_type=F32)


def dot_tn(a, b):
    return lax.dot_general(a, b, (((0,), (0,)), ((), ())), preferred_element_type=F32)


def iota(shape, dim):
    return lax.broadcasted_iota(I32, shape, dim)


def call(kernel, name, out_shape, specs, scratch, flops, size, exps=0):
    vmem = pl.BlockSpec(memory_space=pltpu.VMEM)
    smem = pl.BlockSpec(memory_space=pltpu.SMEM)
    hbm = pl.BlockSpec(memory_space=pl.ANY)
    kinds = {"s": smem, "v": vmem, "h": hbm}
    ins, outs = specs.split("-")
    return pl.pallas_call(
        kernel,
        out_shape=tuple(jax.ShapeDtypeStruct(shape, dtype) for shape, dtype in out_shape),
        in_specs=[kinds[c] for c in ins],
        out_specs=tuple(kinds[c] for c in outs),
        scratch_shapes=scratch,
        compiler_params=pltpu.CompilerParams(vmem_limit_bytes=VMEM_LIMIT),
        cost_estimate=pl.CostEstimate(flops=flops, bytes_accessed=size, transcendentals=exps),
        name=name,
    )


def prepare_kernel(place, counts, dilation, ctx, res, listing, own_ctx, own_res, table):
    table[CORE], table[HIGH], table[PLANE_ID] = place[0], place[1], place[2]
    table[RATE], table[SEGMENT] = dilation[0, 1], dilation[0, 0]
    me = place[2] * 2 + place[1]
    start = jnp.int32(0)
    for b in range(BLOCKS):
        count = counts[0, b]
        table[ALL_STARTS + b] = start
        table[ALL_COUNTS + b] = count

        @pl.when(me == b)
        def _(start=start, count=count):
            table[START_ME] = start
            table[COUNT_ME] = count

        start = start + count
    order = (iota((TILE_DEV, TILE_DEV), 0) == listing[0]).astype(BF16)
    own_ctx[...] = dot_tn(order, ctx[0]).astype(BF16)
    own_res[...] = dot_tn(order, res[0]).astype(BF16)


def prepare(*args):
    rows = ((TILE_DEV, D_ENC), BF16)
    shapes = (rows, rows, ((ALL_COUNTS + BLOCKS,), I32))
    return call(prepare_kernel, "prepare_rows", shapes, "sssvvv-vvs", [], 250_000_000, 2_400_000)(*args)


def halves(table, ref, width):
    core = table[CORE]
    first = ref[:, pl.ds(pl.multiple_of(core * width, LANES), width)]
    second = ref[:, pl.ds(pl.multiple_of((1 - core) * width, LANES), width)]
    return first, second


def embed_kernel(table, ctx, res, own, other, out, tail, head, w, p, hidden, normed):
    core = table[CORE]
    for block in range(PLANES):
        turned = block % 4 * 4 + block // 4
        at_own = jnp.where(core == 0, block, turned)
        at_other = jnp.where(core == 0, turned, block)
        w_rows = slice(block * 2 * W_ROWS, (block + 1) * 2 * W_ROWS)
        p_rows = slice(block * 2 * P_ROWS, (block + 1) * 2 * P_ROWS)
        w[core, w_rows] = own[at_own, : 2 * W_ROWS]
        p[core, p_rows] = own[at_own, 2 * W_ROWS :]
        w[1 - core, w_rows] = other[at_other, : 2 * W_ROWS]
        p[1 - core, p_rows] = other[at_other, 2 * W_ROWS :]
    total = jnp.zeros((TILE_DEV, 1), F32)
    width = D // 2
    for n in range(4):
        columns = slice(n * width, (n + 1) * width)
        part = res[:, columns].astype(F32) + dot_nt(ctx[:, :D], w[0, columns]) + dot_nt(ctx[:, D:], w[1, columns])
        hidden[:, columns] = part
        total += jnp.sum(part, axis=1, keepdims=True)
    center = hidden[...] - total / D_ENC
    spread = jnp.sum(center * center, axis=1, keepdims=True) / D_ENC
    normed[...] = (center * lax.rsqrt(spread + NORM_EPS)).astype(BF16)
    out[...] = (dot_nt(normed[:, :D], p[0]) + dot_nt(normed[:, D:], p[1])).astype(BF16)
    lane = iota((HALF, TILE_DEV), 1)
    pick = (lane == iota((HALF, TILE_DEV), 0) + (table[COUNT_ME] - HALF)).astype(BF16)
    tail[...] = dot_nn(pick, out[...]).astype(BF16)
    head[...] = out[:HALF]


def embed(*args):
    scratch = [
        pltpu.VMEM((2, D_ENC, D), BF16),
        pltpu.VMEM((2, D, D), BF16),
        pltpu.VMEM((TILE_DEV, D_ENC), F32),
        pltpu.VMEM((TILE_DEV, D_ENC), BF16),
    ]
    shapes = (((TILE_DEV, D), BF16), ((HALF, D), BF16), ((HALF, D), BF16))
    return call(embed_kernel, "embed_rows", shapes, "svvvv-vvv", scratch, 1_400_000_000, 9_000_000)(*args)


def project_kernel(table, own, q_a, q_b, payload, q_out, kv_out):
    rate, start_me = table[RATE], table[START_ME]
    first, second = halves(table, own, D // 2)
    q_out[...] = (dot_nt(q_a[:D], first) + dot_nt(q_b[:D], second)).astype(BF16)
    for n in range(2):
        rows = slice((n + 1) * D, (n + 2) * D)
        kv_out[n * D : (n + 1) * D] = (dot_nt(q_a[rows], first) + dot_nt(q_b[rows], second)).astype(BF16)
    slot = iota((SLOTS, TILE_DEV), 0) * rate
    lane = iota((SLOTS, TILE_DEV), 1)
    key_rest = jnp.zeros((LANES - 2 * HEAD_DIM, TILE_DEV), BF16)
    query_rest = jnp.zeros((LANES - HEAD_DIM, TILE_DEV), BF16)
    for h in range(HEADS):
        rows = slice(h * HEAD_DIM, (h + 1) * HEAD_DIM)
        pick = (lane == slot + ((h - start_me) & (rate - 1))).astype(BF16)
        both = jnp.concatenate([kv_out[rows], kv_out[D + h * HEAD_DIM : D + (h + 1) * HEAD_DIM], key_rest], axis=0)
        ask = jnp.concatenate([q_out[rows], query_rest], axis=0)
        payload[h, :SLOTS] = dot_nt(pick, both).astype(BF16)
        payload[h, SLOTS:] = dot_nt(pick, ask).astype(BF16)


def project(*args):
    shapes = (((HEADS, 2 * SLOTS, LANES), BF16), ((D, TILE_DEV), BF16), ((2 * D, TILE_DEV), BF16))
    return call(project_kernel, "project_rows", shapes, "svvv-vvv", [], 1_000_000_000, 5_000_000)(*args)


def pack_kernel(arrived, out):
    rows = arrived[:, :SLOTS].reshape(PLANES * SLOTS, LANES)
    out[...] = rows.T[: 2 * HEAD_DIM]


def pack(*args):
    shapes = (((2 * HEAD_DIM, PLANES * SLOTS), BF16),)
    return call(pack_kernel, "pack_keys", shapes, "v-v", [], 1_000_000, 500_000)(*args)[0]


def local_kernel(table, q, kv, before, after, q_a, q_b, out_sum, out_best, out_total, rims, rim):
    start_me, count_me = table[START_ME], table[COUNT_ME]
    rims[:HALF] = before[...]
    rims[HALF:] = after[...]
    first, second = halves(table, rims, D // 2)
    rim[...] = (dot_nt(q_a[D:], first) + dot_nt(q_b[D:], second)).astype(BF16)
    length = jnp.full((1, 1), table[SEGMENT], I32).astype(F32)

    def segment(position):
        return jnp.floor((position.astype(F32) + 0.5) / length)

    query_seg = segment(start_me + iota((1, TILE_DEV), 1))
    key_at = iota((TILE_DEV, 1), 0)
    key_seg = jnp.where(key_at < count_me, segment(start_me + key_at), -1.0)
    rim_id = iota((2 * HALF, 1), 0)
    rim_at = start_me + jnp.where(rim_id < HALF, rim_id - HALF, rim_id - HALF + count_me)
    rim_seg = jnp.where((rim_at >= 0) & (rim_at < SEQ_LEN), segment(rim_at), -1.0)
    key_ok, rim_ok = key_seg == query_seg, rim_seg == query_seg
    for h in range(HEADS):
        rows = slice(h * HEAD_DIM, (h + 1) * HEAD_DIM)
        v_rows = slice(D + h * HEAD_DIM, D + (h + 1) * HEAD_DIM)
        scores = jnp.where(key_ok, dot_tn(kv[rows], q[rows]) * SCALE, BIG_NEGATIVE)
        rim_scores = jnp.where(rim_ok, dot_tn(rim[rows], q[rows]) * SCALE, BIG_NEGATIVE)
        best = jnp.maximum(jnp.max(scores, axis=0, keepdims=True), jnp.max(rim_scores, axis=0, keepdims=True))
        weights, rim_weights = jnp.exp(scores - best), jnp.exp(rim_scores - best)
        out_best[h : h + 1] = best
        out_total[h : h + 1] = jnp.sum(weights, axis=0, keepdims=True) + jnp.sum(rim_weights, axis=0, keepdims=True)
        out_sum[rows] = dot_nn(kv[v_rows], weights.astype(BF16)) + dot_nn(rim[v_rows], rim_weights.astype(BF16))


def local_branch(*args):
    stat = ((HEADS, TILE_DEV), F32)
    shapes = (((D, TILE_DEV), F32), stat, stat)
    scratch = [pltpu.VMEM((2 * HALF, D), BF16), pltpu.VMEM((2 * D, 2 * HALF), BF16)]
    return call(local_kernel, "local_branch", shapes, "svvvvvv-vvv", scratch, 600_000_000, 5_000_000, 1_000_000)(*args)


def far_scores(table, high, keys, asks, scores):
    rate = table[RATE]
    slot = iota((SLOTS, asks.shape[0]), 0) * rate
    best = jnp.full((1, asks.shape[0]), BIG_NEGATIVE, F32)
    for p in range(PLANES):
        block = 2 * p + high
        phase = (table[PLANE_ID] - table[ALL_STARTS + block]) & (rate - 1)
        piece = dot_nt(keys[p * SLOTS : (p + 1) * SLOTS], asks) * SCALE
        piece = jnp.where(slot + phase < table[ALL_COUNTS + block], piece, BIG_NEGATIVE)
        scores[p * SLOTS : (p + 1) * SLOTS] = piece
        best = jnp.maximum(best, jnp.max(piece, axis=0, keepdims=True))
    return best


FAR_GROUP = 8
FAR_WIDTH = FAR_GROUP * SLOTS


def far_own_kernel(table, arrived, out_sum, out_best, out_total, scores):
    keys = arrived[:, :SLOTS].reshape(PLANES * SLOTS, LANES)
    for n in range(PLANES // FAR_GROUP):
        lanes = slice(n * FAR_WIDTH, (n + 1) * FAR_WIDTH)
        asks = arrived[n * FAR_GROUP : (n + 1) * FAR_GROUP, SLOTS:].reshape(FAR_WIDTH, LANES)
        best = far_scores(table, table[HIGH], keys, asks, scores)
        weights = jnp.exp(scores[...] - best)
        out_best[:, lanes] = best
        out_total[:, lanes] = jnp.sum(weights, axis=0, keepdims=True)
        out_sum[:, lanes] = dot_tn(keys, weights.astype(BF16))[HEAD_DIM : 2 * HEAD_DIM]


def far_own(*args):
    width = PLANES * SLOTS
    shapes = (((HEAD_DIM, width), F32), ((1, width), F32), ((1, width), F32))
    scratch = [pltpu.VMEM((width, FAR_WIDTH), F32)]
    return call(far_own_kernel, "far_own", shapes, "sv-vvv", scratch, 300_000_000, 700_000, 600_000)(*args)


def far_rest_kernel(table, arrived, other, own_sum, own_best, own_total, answer, scores):
    other_t = other[...]
    keys = other_t.T
    values = other_t[HEAD_DIM:]
    for n in range(PLANES // FAR_GROUP):
        lanes = slice(n * FAR_WIDTH, (n + 1) * FAR_WIDTH)
        asks = arrived[n * FAR_GROUP : (n + 1) * FAR_GROUP, SLOTS:].reshape(FAR_WIDTH, LANES)[:, : 2 * HEAD_DIM]
        best_o = own_best[:, lanes]
        best = jnp.maximum(best_o, far_scores(table, 1 - table[HIGH], keys, asks, scores))
        weights = jnp.exp(scores[...] - best)
        scale_o = jnp.exp(best_o - best)
        total = jnp.sum(weights, axis=0, keepdims=True) + scale_o * own_total[:, lanes]
        summed = dot_nn(values, weights.astype(BF16)) + scale_o * own_sum[:, lanes]
        shared = summed / total
        log_all = best + jnp.log(total)
        log_a = log_all.astype(BF16).astype(F32)
        log_b = (log_all - log_a).astype(BF16).astype(F32)
        log_c = log_all - log_a - log_b
        row = iota((LANES - HEAD_DIM, FAR_WIDTH), 0)
        tail = jnp.where(row == 0, log_a, jnp.where(row == 1, log_b, jnp.where(row == 2, log_c, 0.0)))
        block = jnp.concatenate([shared, tail], axis=0)
        answer[n * FAR_GROUP : (n + 1) * FAR_GROUP] = block.T.astype(BF16).reshape(FAR_GROUP, SLOTS, LANES)


def far_rest(*args):
    shapes = (((PLANES, SLOTS, LANES), BF16),)
    scratch = [pltpu.VMEM((PLANES * SLOTS, FAR_WIDTH), F32)]
    return call(far_rest_kernel, "far_rest", shapes, "svvvvv-v", scratch, 300_000_000, 1_000_000, 600_000)(*args)[0]


def finish_kernel(table, answers, local_sum, local_best, local_total, listing, out, attended):
    rate = table[RATE]
    slot = iota((SLOTS, TILE_DEV), 0) * rate
    lane = iota((SLOTS, TILE_DEV), 1)
    row = iota((1, TILE_DEV), 1)
    live = row < table[COUNT_ME]
    for h in range(HEADS):
        rows = slice(h * HEAD_DIM, (h + 1) * HEAD_DIM)
        phase = (h - table[START_ME]) & (rate - 1)
        pick = (lane == slot + phase).astype(BF16)
        wide = dot_tn(answers[h], pick)
        log_all = wide[HEAD_DIM : HEAD_DIM + 1] + wide[HEAD_DIM + 1 : HEAD_DIM + 2] + wide[HEAD_DIM + 2 : HEAD_DIM + 3]
        log_all = jnp.where((row & (rate - 1)) == phase, log_all, BIG_NEGATIVE)
        best = local_best[h : h + 1]
        joint = jnp.maximum(best, log_all)
        near = jnp.exp(best - joint)
        far = jnp.exp(log_all - joint)
        below = jnp.where(live, near * local_total[h : h + 1] + far, 1.0)
        mixed = (near * local_sum[rows] + far * wide[:HEAD_DIM]) / below
        attended[rows] = jnp.where(live, mixed, 0.0).astype(BF16)
    back = (listing[0] == iota((TILE_DEV, TILE_DEV), 0)).astype(BF16)
    out[0] = dot_nt(back, attended[...]).astype(BF16)


def finish(*args):
    shapes = (((1, TILE_DEV, D), BF16),)
    scratch = [pltpu.VMEM((D, TILE_DEV), BF16)]
    return call(finish_kernel, "finish_rows", shapes, "svvvvv-v", scratch, 100_000_000, 1_500_000, 10_000)(*args)[0]


def mirrored(x):
    z_low = lax.axis_size("zlo")
    pairs = [
        (low * 2 + high, (z_low - 1 - low) * 2 + (1 - high))
        for low in range(z_low)
        for high in range(2)
    ]
    return lax.ppermute(x, ("zlo", "zhi"), pairs)


def across(x):
    return lax.ppermute(x, "zhi", [(0, 1), (1, 0)])


def other_core(x):
    return lax.ppermute(x, "core", [(0, 1), (1, 0)])


def over_plane(x):
    return lax.all_to_all(x, PLANE, 0, 0)


def hold(*values):
    return lax.optimization_barrier(values)


def copies(x):
    return jnp.broadcast_to(x[None], (PLANES,) + x.shape)


def along_lines(x, stage):
    groups = []
    for low in range(lax.axis_size("zlo")):
        for core in range(2):
            for high in range(2):
                for line in range(4):
                    across_x = (core == 0) == (stage == 0)
                    plane = [line * 4 + k if across_x else k * 4 + line for k in range(4)]
                    groups.append([((low * 2 + core) * PLANES + p) * 2 + high for p in plane])
    spread = jnp.broadcast_to(x[None], (4,) + x.shape)
    return lax.all_to_all(spread, EVERY, 0, 0, axis_index_groups=groups)


def in_order(own, other, high):
    return jnp.where(high == 0, jnp.concatenate([own, other]), jnp.concatenate([other, own]))


def on_device(ctx_in, resid, enc_out_w, slide_proj, qkv_w, tissue, kept_count, dilation):
    core = lax.axis_index("core")
    high = lax.axis_index("zhi")
    plane_id = lax.axis_index("y") * lax.axis_size("x") + lax.axis_index("x")

    w_own = lax.dynamic_slice_in_dim(enc_out_w, core * D, D, 0).T
    p_own = lax.dynamic_slice_in_dim(slide_proj, core * D, D, 0).T
    q_own = lax.dynamic_slice_in_dim(qkv_w, core * (D // 2), D // 2, 0).T
    other_wp = mirrored(jnp.concatenate([w_own, p_own]))
    q_other = mirrored(q_own)
    place = jnp.stack([core, high, plane_id]).astype(I32)
    own_ctx, own_res, table = prepare(place, kept_count, dilation, ctx_in, resid, tissue)
    wp = jnp.concatenate(
        [in_order(w_own, other_wp[:W_ROWS], high), in_order(p_own, other_wp[W_ROWS:], high)]
    )
    wp = along_lines(along_lines(wp, 0).reshape(-1, D), 1).reshape(PLANES, -1, D)
    q_both = copies(in_order(q_own, q_other, high))
    wp, q_both = hold(wp, q_both)
    q_a = over_plane(q_both)
    embedded, tail, head = embed(table, own_ctx, own_res, wp, other_core(wp))
    blocks = 2 * PLANES
    before = lax.ppermute(tail, SEQ, [(b, b + 1) for b in range(blocks - 1)])
    after = lax.ppermute(head, SEQ, [(b + 1, b) for b in range(blocks - 1)])
    q_a, embedded, before, after = hold(q_a, embedded, before, after)
    q_a = q_a.reshape(3 * D, D // 2)
    q_b = other_core(q_a)
    payload, q_rows, kv_rows = project(table, embedded, q_a, q_b)
    arrived = lax.all_to_all(payload, PLANE, 0, 0)
    other = across(pack(arrived))
    own_sum, own_best, own_total = far_own(table, arrived)
    local_sum, local_best, local_total = local_branch(table, q_rows, kv_rows, before, after, q_a, q_b)
    other, own_sum, local_sum = hold(other, own_sum, local_sum)
    answer = far_rest(table, arrived, other, own_sum, own_best, own_total)
    answers = lax.all_to_all(answer, PLANE, 0, 0)
    return finish(table, answers, local_sum, local_best, local_total, tissue)


def solution(mesh):
    devices = mesh.devices.reshape(-1, 2, 4, 4, 2)
    split = Mesh(devices, ("zlo", "core", "y", "x", "zhi"))
    slide, seq = ("zlo", "core"), ("y", "x", "zhi")
    return jax.shard_map(
        on_device,
        mesh=split,
        in_specs=(
            P(slide, seq, None),
            P(slide, seq, None),
            P(None, seq),
            P(None, seq),
            P(None, seq),
            P(slide, seq, None),
            P(slide, None),
            P(slide, None),
        ),
        out_specs=P(slide, seq, None),
        check_vma=False,
    )
```

```python
import jax
import jax.numpy as jnp
from jax import lax
from jax.experimental import pallas as pl
from jax.experimental.pallas import tpu as pltpu
from jax.sharding import Mesh, PartitionSpec as P

HEADS = 16
HEAD_DIM = 48
D = 768
D_ENC = 1536
HALF = 64
TILE_DEV = 192
SEQ_LEN = 4096
WINDOW = 320
KEY_SLOTS = 80
SLOTS = 48
LANES = 128
W_ROWS = 48
P_ROWS = 24
PLANES = 16
PLANE = ("y", "x")
SEQ = ("y", "x", "zhi")
EVERY = ("zlo", "core", "y", "x", "zhi")
NORM_EPS = 1e-06
BIG_NEGATIVE = -1e30
SCALE = HEAD_DIM**-0.5
BF16 = jnp.bfloat16
F32 = jnp.float32
I32 = jnp.int32
VMEM_LIMIT = 24 * 1024 * 1024

CORE, HIGH, PLANE_ID, RATE, SEGMENT = range(5)
START_ME, COUNT_ME, START_OTHER, COUNT_OTHER, PAIR_START, PAIR_COUNT = range(5, 11)
ALL_STARTS = 16
ALL_COUNTS = 32


def dot_nn(a, b):
    return lax.dot_general(a, b, (((1,), (0,)), ((), ())), preferred_element_type=F32)


def dot_nt(a, b):
    return lax.dot_general(a, b, (((1,), (1,)), ((), ())), preferred_element_type=F32)


def dot_tn(a, b):
    return lax.dot_general(a, b, (((0,), (0,)), ((), ())), preferred_element_type=F32)


def iota(shape, dim):
    return lax.broadcasted_iota(I32, shape, dim)


def call(kernel, name, out_shape, specs, scratch, flops, size, exps=0):
    vmem = pl.BlockSpec(memory_space=pltpu.VMEM)
    smem = pl.BlockSpec(memory_space=pltpu.SMEM)
    hbm = pl.BlockSpec(memory_space=pl.ANY)
    kinds = {"s": smem, "v": vmem, "h": hbm}
    ins, outs = specs.split("-")
    return pl.pallas_call(
        kernel,
        out_shape=tuple(jax.ShapeDtypeStruct(shape, dtype) for shape, dtype in out_shape),
        in_specs=[kinds[c] for c in ins],
        out_specs=tuple(kinds[c] for c in outs),
        scratch_shapes=scratch,
        compiler_params=pltpu.CompilerParams(vmem_limit_bytes=VMEM_LIMIT),
        cost_estimate=pl.CostEstimate(flops=flops, bytes_accessed=size, transcendentals=exps),
        name=name,
    )


def prepare_kernel(place, counts, dilation, ctx, res, listing, own_ctx, own_res, table):
    table[CORE], table[HIGH], table[PLANE_ID] = place[0], place[1], place[2]
    table[RATE], table[SEGMENT] = dilation[0, 1], dilation[0, 0]
    high = place[1]
    start = jnp.int32(0)
    for p in range(PLANES):
        first, second = counts[0, 2 * p], counts[0, 2 * p + 1]
        table[ALL_STARTS + p] = start
        table[ALL_COUNTS + p] = first + second

        @pl.when(place[2] == p)
        def _(first=first, second=second, start=start):
            table[PAIR_START] = start
            table[PAIR_COUNT] = first + second
            table[COUNT_ME] = jnp.where(high == 0, first, second)
            table[COUNT_OTHER] = jnp.where(high == 0, second, first)
            table[START_ME] = jnp.where(high == 0, start, start + first)
            table[START_OTHER] = jnp.where(high == 0, start + first, start)

        start = start + first + second
    order = (iota((TILE_DEV, TILE_DEV), 0) == listing[0]).astype(BF16)
    own_ctx[...] = dot_tn(order, ctx[0]).astype(BF16)
    own_res[...] = dot_tn(order, res[0]).astype(BF16)


def prepare(*args):
    rows = ((TILE_DEV, D_ENC), BF16)
    shapes = (rows, rows, ((ALL_COUNTS + PLANES,), I32))
    return call(prepare_kernel, "prepare_rows", shapes, "sssvvv-vvs", [], 250_000_000, 2_400_000)(*args)


def halves(table, ref, width):
    core = table[CORE]
    first = ref[:, pl.ds(pl.multiple_of(core * width, LANES), width)]
    second = ref[:, pl.ds(pl.multiple_of((1 - core) * width, LANES), width)]
    return first, second


def embed_kernel(table, ctx, res, own, other, out, w, p, hidden, normed):
    core = table[CORE]
    for block in range(PLANES):
        turned = block % 4 * 4 + block // 4
        at_own = jnp.where(core == 0, block, turned)
        at_other = jnp.where(core == 0, turned, block)
        w_rows = slice(block * 2 * W_ROWS, (block + 1) * 2 * W_ROWS)
        p_rows = slice(block * 2 * P_ROWS, (block + 1) * 2 * P_ROWS)
        w[core, w_rows] = own[at_own, : 2 * W_ROWS]
        p[core, p_rows] = own[at_own, 2 * W_ROWS :]
        w[1 - core, w_rows] = other[at_other, : 2 * W_ROWS]
        p[1 - core, p_rows] = other[at_other, 2 * W_ROWS :]
    total = jnp.zeros((TILE_DEV, 1), F32)
    width = D // 2
    for n in range(4):
        columns = slice(n * width, (n + 1) * width)
        part = res[:, columns].astype(F32) + dot_nt(ctx[:, :D], w[0, columns]) + dot_nt(ctx[:, D:], w[1, columns])
        hidden[:, columns] = part
        total += jnp.sum(part, axis=1, keepdims=True)
    center = hidden[...] - total / D_ENC
    spread = jnp.sum(center * center, axis=1, keepdims=True) / D_ENC
    normed[...] = (center * lax.rsqrt(spread + NORM_EPS)).astype(BF16)
    out[...] = (dot_nt(normed[:, :D], p[0]) + dot_nt(normed[:, D:], p[1])).astype(BF16)


def embed(*args):
    scratch = [
        pltpu.VMEM((2, D_ENC, D), BF16),
        pltpu.VMEM((2, D, D), BF16),
        pltpu.VMEM((TILE_DEV, D_ENC), F32),
        pltpu.VMEM((TILE_DEV, D_ENC), BF16),
    ]
    shapes = (((TILE_DEV, D), BF16),)
    return call(embed_kernel, "embed_rows", shapes, "svvvv-v", scratch, 1_400_000_000, 9_000_000)(*args)[0]


def project_kernel(table, own, partner, qa, qb, payload, q_out, kv_out, spanned):
    core, rate, base = table[CORE], table[RATE], table[PAIR_START]

    def placed(first, count, length):
        lane = iota((WINDOW, length), 1)
        hit = (iota((WINDOW, length), 0) == lane + first) & (lane < count)
        return hit.astype(BF16)

    spread = dot_nn(placed(table[START_ME] - base, table[COUNT_ME], TILE_DEV), own[...])
    spread += dot_nn(placed(table[START_OTHER] - base, table[COUNT_OTHER], TILE_DEV), partner[...])
    spanned[...] = spread.astype(BF16)
    half = D // 2
    lanes_a = pl.ds(pl.multiple_of(core * half, LANES), half)
    lanes_b = pl.ds(pl.multiple_of((1 - core) * half, LANES), half)
    own_a, own_b = own[:, lanes_a], own[:, lanes_b]
    q_out[...] = (dot_nt(qa[:D], own_a) + dot_nt(qb[:D], own_b)).astype(BF16)
    span_a, span_b = spanned[:, lanes_a], spanned[:, lanes_b]
    for n in range(2):
        rows = slice((n + 1) * D, (n + 2) * D)
        kv_out[n * D : (n + 1) * D] = (dot_nt(qa[rows], span_a) + dot_nt(qb[rows], span_b)).astype(BF16)
    key_slot = iota((KEY_SLOTS, WINDOW), 0) * rate
    key_lane = iota((KEY_SLOTS, WINDOW), 1)
    query_slot = iota((SLOTS, TILE_DEV), 0) * rate
    query_lane = iota((SLOTS, TILE_DEV), 1)
    key_rest = jnp.zeros((LANES - 2 * HEAD_DIM, WINDOW), BF16)
    query_rest = jnp.zeros((LANES - HEAD_DIM, TILE_DEV), BF16)
    for h in range(HEADS):
        rows = slice(h * HEAD_DIM, (h + 1) * HEAD_DIM)
        key_first = (h - base) & (rate - 1)
        key_pick = (key_lane == key_slot + key_first).astype(BF16)
        both = jnp.concatenate([kv_out[rows], kv_out[D + h * HEAD_DIM : D + (h + 1) * HEAD_DIM], key_rest], axis=0)
        payload[h, :KEY_SLOTS] = dot_nt(key_pick, both).astype(BF16)
        query_first = (h - table[START_ME]) & (rate - 1)
        query_pick = (query_lane == query_slot + query_first).astype(BF16)
        ask = jnp.concatenate([q_out[rows], query_rest], axis=0)
        payload[h, KEY_SLOTS:] = dot_nt(query_pick, ask).astype(BF16)


def project(*args):
    shapes = (((HEADS, KEY_SLOTS + SLOTS, LANES), BF16), ((D, TILE_DEV), BF16), ((2 * D, WINDOW), BF16))
    scratch = [pltpu.VMEM((WINDOW, D), BF16)]
    return call(project_kernel, "project_rows", shapes, "svvvv-vvv", scratch, 1_500_000_000, 5_000_000)(*args)


def local_kernel(table, q, kv, halo, qa, qb, out_sum, out_best, out_total, rim):
    core, high, start_me = table[CORE], table[HIGH], table[START_ME]
    half = D // 2
    halo_a = halo[:, pl.ds(pl.multiple_of(core * half, LANES), half)]
    halo_b = halo[:, pl.ds(pl.multiple_of((1 - core) * half, LANES), half)]
    rim[...] = (dot_nt(qa[D:], halo_a) + dot_nt(qb[D:], halo_b)).astype(BF16)
    length = jnp.full((1, 1), table[SEGMENT], I32).astype(F32)

    def segment(position):
        return jnp.floor((position.astype(F32) + 0.5) / length)

    query_seg = segment(start_me + iota((1, TILE_DEV), 1))
    key_at = iota((WINDOW, 1), 0)
    key_seg = jnp.where(key_at < table[PAIR_COUNT], segment(table[PAIR_START] + key_at), -1.0)
    rim_first = table[PAIR_START] + jnp.where(high == 0, -HALF, table[PAIR_COUNT])
    rim_at = rim_first + iota((HALF, 1), 0)
    rim_seg = jnp.where((rim_at >= 0) & (rim_at < SEQ_LEN), segment(rim_at), -1.0)
    key_ok, rim_ok = key_seg == query_seg, rim_seg == query_seg
    for h in range(HEADS):
        rows = slice(h * HEAD_DIM, (h + 1) * HEAD_DIM)
        v_rows = slice(D + h * HEAD_DIM, D + (h + 1) * HEAD_DIM)
        scores = jnp.where(key_ok, dot_tn(kv[rows], q[rows]) * SCALE, BIG_NEGATIVE)
        rim_scores = jnp.where(rim_ok, dot_tn(rim[rows], q[rows]) * SCALE, BIG_NEGATIVE)
        best = jnp.maximum(jnp.max(scores, axis=0, keepdims=True), jnp.max(rim_scores, axis=0, keepdims=True))
        weights, rim_weights = jnp.exp(scores - best), jnp.exp(rim_scores - best)
        out_best[h : h + 1] = best
        out_total[h : h + 1] = jnp.sum(weights, axis=0, keepdims=True) + jnp.sum(rim_weights, axis=0, keepdims=True)
        out_sum[rows] = dot_nn(kv[v_rows], weights.astype(BF16)) + dot_nn(rim[v_rows], rim_weights.astype(BF16))


def local_branch(*args):
    stat = ((HEADS, TILE_DEV), F32)
    shapes = (((D, TILE_DEV), F32), stat, stat)
    scratch = [pltpu.VMEM((2 * D, HALF), BF16)]
    return call(local_kernel, "local_branch", shapes, "svvvvv-vvv", scratch, 600_000_000, 5_000_000, 1_000_000)(*args)


def far_kernel(table, arrived, answer, scores):
    rate = table[RATE]
    kv = arrived[:, :KEY_SLOTS].reshape(PLANES * KEY_SLOTS, LANES)
    group = 8
    width = group * SLOTS
    slot = iota((KEY_SLOTS, width), 0) * rate
    for n in range(PLANES // group):
        asks = arrived[n * group : (n + 1) * group, KEY_SLOTS:].reshape(width, LANES)
        best = jnp.full((1, width), BIG_NEGATIVE, F32)
        for p in range(PLANES):
            phase = (table[PLANE_ID] - table[ALL_STARTS + p]) & (rate - 1)
            piece = dot_nt(arrived[p, :KEY_SLOTS], asks) * SCALE
            piece = jnp.where(slot + phase < table[ALL_COUNTS + p], piece, BIG_NEGATIVE)
            scores[p * KEY_SLOTS : (p + 1) * KEY_SLOTS] = piece
            best = jnp.maximum(best, jnp.max(piece, axis=0, keepdims=True))
        weights = jnp.exp(scores[...] - best)
        total = jnp.sum(weights, axis=0, keepdims=True)
        summed = dot_tn(kv, weights.astype(BF16))
        shared = summed[HEAD_DIM : 2 * HEAD_DIM] / total
        log_all = best + jnp.log(total)
        log_a = log_all.astype(BF16).astype(F32)
        log_b = (log_all - log_a).astype(BF16).astype(F32)
        log_c = log_all - log_a - log_b
        row = iota((LANES - HEAD_DIM, width), 0)
        tail = jnp.where(row == 0, log_a, jnp.where(row == 1, log_b, jnp.where(row == 2, log_c, 0.0)))
        block = jnp.concatenate([shared, tail], axis=0)
        answer[n * group : (n + 1) * group] = block.T.astype(BF16).reshape(group, SLOTS, LANES)


def far_branch(*args):
    shapes = (((PLANES, SLOTS, LANES), BF16),)
    scratch = [pltpu.VMEM((PLANES * KEY_SLOTS, PLANES // 2 * SLOTS), F32)]
    return call(far_kernel, "far_branch", shapes, "sv-v", scratch, 500_000_000, 1_000_000, 1_000_000)(*args)[0]


def finish_kernel(table, answers, local_sum, local_best, local_total, listing, out, attended):
    rate = table[RATE]
    slot = iota((SLOTS, TILE_DEV), 0) * rate
    lane = iota((SLOTS, TILE_DEV), 1)
    row = iota((1, TILE_DEV), 1)
    live = row < table[COUNT_ME]
    for h in range(HEADS):
        rows = slice(h * HEAD_DIM, (h + 1) * HEAD_DIM)
        phase = (h - table[START_ME]) & (rate - 1)
        pick = (lane == slot + phase).astype(BF16)
        wide = dot_tn(answers[h], pick)
        log_all = wide[HEAD_DIM : HEAD_DIM + 1] + wide[HEAD_DIM + 1 : HEAD_DIM + 2] + wide[HEAD_DIM + 2 : HEAD_DIM + 3]
        log_all = jnp.where((row & (rate - 1)) == phase, log_all, BIG_NEGATIVE)
        best = local_best[h : h + 1]
        joint = jnp.maximum(best, log_all)
        near = jnp.exp(best - joint)
        far = jnp.exp(log_all - joint)
        below = jnp.where(live, near * local_total[h : h + 1] + far, 1.0)
        mixed = (near * local_sum[rows] + far * wide[:HEAD_DIM]) / below
        attended[rows] = jnp.where(live, mixed, 0.0).astype(BF16)
    back = (listing[0] == iota((TILE_DEV, TILE_DEV), 0)).astype(BF16)
    out[0] = dot_nt(back, attended[...]).astype(BF16)


def finish(*args):
    shapes = (((1, TILE_DEV, D), BF16),)
    scratch = [pltpu.VMEM((D, TILE_DEV), BF16)]
    return call(finish_kernel, "finish_rows", shapes, "svvvvv-v", scratch, 100_000_000, 1_500_000, 10_000)(*args)[0]


def mirrored(x):
    z_low = lax.axis_size("zlo")
    pairs = [
        (low * 2 + high, (z_low - 1 - low) * 2 + (1 - high))
        for low in range(z_low)
        for high in range(2)
    ]
    return lax.ppermute(x, ("zlo", "zhi"), pairs)


def quarter_way(x):
    z_low = lax.axis_size("zlo")

    def rank(z, core):
        return (z % z_low * 2 + core) * 2 + z // z_low

    pairs = []
    for z in range(2 * z_low):
        for core in range(2):
            step = z_low // 2 if core == 0 else -(z_low // 2)
            pairs.append((rank(z, core), rank((z + step) % (2 * z_low), core)))
    return lax.ppermute(x, ("zlo", "core", "zhi"), pairs)


def other_core(x):
    return lax.ppermute(x, "core", [(0, 1), (1, 0)])


def over_plane(x):
    return lax.all_to_all(x, PLANE, 0, 0)


def hold(*values):
    return lax.optimization_barrier(values)


def copies(x):
    return jnp.broadcast_to(x[None], (PLANES,) + x.shape)


def along_lines(x, stage):
    groups = []
    for low in range(lax.axis_size("zlo")):
        for core in range(2):
            for high in range(2):
                for line in range(4):
                    across_x = (core == 0) == (stage == 0)
                    plane = [line * 4 + k if across_x else k * 4 + line for k in range(4)]
                    groups.append([((low * 2 + core) * PLANES + p) * 2 + high for p in plane])
    spread = jnp.broadcast_to(x[None], (4,) + x.shape)
    return lax.all_to_all(spread, EVERY, 0, 0, axis_index_groups=groups)


def in_order(own, other, high):
    return jnp.where(high == 0, jnp.concatenate([own, other]), jnp.concatenate([other, own]))


def on_device(ctx_in, resid, enc_out_w, slide_proj, qkv_w, tissue, kept_count, dilation):
    core = lax.axis_index("core")
    high = lax.axis_index("zhi")
    plane_id = lax.axis_index("y") * lax.axis_size("x") + lax.axis_index("x")

    w_own = lax.dynamic_slice_in_dim(enc_out_w, core * D, D, 0).T
    p_own = lax.dynamic_slice_in_dim(slide_proj, core * D, D, 0).T
    q_own = lax.dynamic_slice_in_dim(qkv_w, core * (D // 2), D // 2, 0).T
    other_wp = mirrored(jnp.concatenate([w_own, p_own]))
    q_other = mirrored(q_own)
    place = jnp.stack([core, high, plane_id]).astype(I32)
    own_ctx, own_res, table = prepare(place, kept_count, dilation, ctx_in, resid, tissue)
    wp = jnp.concatenate(
        [in_order(w_own, other_wp[:W_ROWS], high), in_order(p_own, other_wp[W_ROWS:], high)]
    )
    wp = along_lines(along_lines(wp, 0).reshape(-1, D), 1).reshape(PLANES, -1, D)
    q_both = copies(in_order(q_own, q_other, high))
    wp, q_both = hold(wp, q_both)
    q_a = over_plane(q_both)
    embedded = embed(table, own_ctx, own_res, wp, other_core(wp))
    q_a, embedded, on_way = hold(q_a, embedded, quarter_way(embedded))
    q_a = q_a.reshape(3 * D, D // 2)
    q_b, partner = hold(other_core(q_a), quarter_way(on_way))
    rim_from = jnp.where(high == 0, table[COUNT_OTHER] - HALF, 0)
    rim = lax.dynamic_slice_in_dim(partner, rim_from, HALF, 0)
    halo_pairs = [(p * 2, p * 2 + 2) for p in range(PLANES - 1)]
    halo_pairs += [(p * 2 + 1, p * 2 - 1) for p in range(1, PLANES)]
    halo = lax.ppermute(rim, SEQ, halo_pairs)
    payload, q_rows, kv_rows = project(table, embedded, partner, q_a, q_b)
    arrived = lax.all_to_all(payload, PLANE, 0, 0)
    local_sum, local_best, local_total = local_branch(table, q_rows, kv_rows, halo, q_a, q_b)
    arrived, local_sum = hold(arrived, local_sum)
    answer = far_branch(table, arrived)
    answers = lax.all_to_all(answer, PLANE, 0, 0)
    return finish(table, answers, local_sum, local_best, local_total, tissue)


def solution(mesh):
    devices = mesh.devices.reshape(-1, 2, 4, 4, 2)
    split = Mesh(devices, ("zlo", "core", "y", "x", "zhi"))
    slide, seq = ("zlo", "core"), ("y", "x", "zhi")
    return jax.shard_map(
        on_device,
        mesh=split,
        in_specs=(
            P(slide, seq, None),
            P(slide, seq, None),
            P(None, seq),
            P(None, seq),
            P(None, seq),
            P(slide, seq, None),
            P(slide, None),
            P(slide, None),
        ),
        out_specs=P(slide, seq, None),
        check_vma=False,
    )
```

```python
import jax
import jax.numpy as jnp
from jax import lax
from jax.experimental import pallas as pl
from jax.experimental.pallas import tpu as pltpu
from jax.sharding import Mesh, PartitionSpec as P

HEADS = 16
HEAD_DIM = 48
D = 768
D_ENC = 1536
HALF = 64
TILE_DEV = 192
SEQ_LEN = 4096
WINDOW = 320
KEY_SLOTS = 80
SLOTS = 48
LANES = 128
W_ROWS = 48
P_ROWS = 24
PLANES = 16
PLANE = ("y", "x")
SEQ = ("y", "x", "zhi")
EVERY = ("zlo", "core", "y", "x", "zhi")
NORM_EPS = 1e-06
BIG_NEGATIVE = -1e30
SCALE = HEAD_DIM**-0.5
BF16 = jnp.bfloat16
F32 = jnp.float32
I32 = jnp.int32
VMEM_LIMIT = 24 * 1024 * 1024

CORE, HIGH, PLANE_ID, RATE, SEGMENT = range(5)
START_ME, COUNT_ME, START_OTHER, COUNT_OTHER, PAIR_START, PAIR_COUNT = range(5, 11)
ALL_STARTS = 16
ALL_COUNTS = 32


def dot_nn(a, b):
    return lax.dot_general(a, b, (((1,), (0,)), ((), ())), preferred_element_type=F32)


def dot_nt(a, b):
    return lax.dot_general(a, b, (((1,), (1,)), ((), ())), preferred_element_type=F32)


def dot_tn(a, b):
    return lax.dot_general(a, b, (((0,), (0,)), ((), ())), preferred_element_type=F32)


def iota(shape, dim):
    return lax.broadcasted_iota(I32, shape, dim)


def call(kernel, name, out_shape, specs, scratch, flops, size, exps=0):
    vmem = pl.BlockSpec(memory_space=pltpu.VMEM)
    smem = pl.BlockSpec(memory_space=pltpu.SMEM)
    hbm = pl.BlockSpec(memory_space=pl.ANY)
    kinds = {"s": smem, "v": vmem, "h": hbm}
    ins, outs = specs.split("-")
    return pl.pallas_call(
        kernel,
        out_shape=tuple(jax.ShapeDtypeStruct(shape, dtype) for shape, dtype in out_shape),
        in_specs=[kinds[c] for c in ins],
        out_specs=tuple(kinds[c] for c in outs),
        scratch_shapes=scratch,
        compiler_params=pltpu.CompilerParams(vmem_limit_bytes=VMEM_LIMIT),
        cost_estimate=pl.CostEstimate(flops=flops, bytes_accessed=size, transcendentals=exps),
        name=name,
    )


def prepare_kernel(place, counts, dilation, ctx, res, listing, own_ctx, own_res, table):
    table[CORE], table[HIGH], table[PLANE_ID] = place[0], place[1], place[2]
    table[RATE], table[SEGMENT] = dilation[0, 1], dilation[0, 0]
    high = place[1]
    start = jnp.int32(0)
    for p in range(PLANES):
        first, second = counts[0, 2 * p], counts[0, 2 * p + 1]
        table[ALL_STARTS + p] = start
        table[ALL_COUNTS + p] = first + second

        @pl.when(place[2] == p)
        def _(first=first, second=second, start=start):
            table[PAIR_START] = start
            table[PAIR_COUNT] = first + second
            table[COUNT_ME] = jnp.where(high == 0, first, second)
            table[COUNT_OTHER] = jnp.where(high == 0, second, first)
            table[START_ME] = jnp.where(high == 0, start, start + first)
            table[START_OTHER] = jnp.where(high == 0, start + first, start)

        start = start + first + second
    order = (iota((TILE_DEV, TILE_DEV), 0) == listing[0]).astype(BF16)
    own_ctx[...] = dot_tn(order, ctx[0]).astype(BF16)
    own_res[...] = dot_tn(order, res[0]).astype(BF16)


def prepare(*args):
    rows = ((TILE_DEV, D_ENC), BF16)
    shapes = (rows, rows, ((ALL_COUNTS + PLANES,), I32))
    return call(prepare_kernel, "prepare_rows", shapes, "sssvvv-vvs", [], 250_000_000, 2_400_000)(*args)


def halves(table, ref, width):
    core = table[CORE]
    first = ref[:, pl.ds(pl.multiple_of(core * width, LANES), width)]
    second = ref[:, pl.ds(pl.multiple_of((1 - core) * width, LANES), width)]
    return first, second


def embed_kernel(table, ctx, res, own, other, out, w, p, hidden, normed):
    core = table[CORE]
    for block in range(PLANES):
        turned = block % 4 * 4 + block // 4
        at_own = jnp.where(core == 0, block, turned)
        at_other = jnp.where(core == 0, turned, block)
        w_rows = slice(block * 2 * W_ROWS, (block + 1) * 2 * W_ROWS)
        p_rows = slice(block * 2 * P_ROWS, (block + 1) * 2 * P_ROWS)
        w[core, w_rows] = own[at_own, : 2 * W_ROWS]
        p[core, p_rows] = own[at_own, 2 * W_ROWS :]
        w[1 - core, w_rows] = other[at_other, : 2 * W_ROWS]
        p[1 - core, p_rows] = other[at_other, 2 * W_ROWS :]
    total = jnp.zeros((TILE_DEV, 1), F32)
    width = D // 2
    for n in range(4):
        columns = slice(n * width, (n + 1) * width)
        part = res[:, columns].astype(F32) + dot_nt(ctx[:, :D], w[0, columns]) + dot_nt(ctx[:, D:], w[1, columns])
        hidden[:, columns] = part
        total += jnp.sum(part, axis=1, keepdims=True)
    center = hidden[...] - total / D_ENC
    spread = jnp.sum(center * center, axis=1, keepdims=True) / D_ENC
    normed[...] = (center * lax.rsqrt(spread + NORM_EPS)).astype(BF16)
    out[...] = (dot_nt(normed[:, :D], p[0]) + dot_nt(normed[:, D:], p[1])).astype(BF16)


def embed(*args):
    scratch = [
        pltpu.VMEM((2, D_ENC, D), BF16),
        pltpu.VMEM((2, D, D), BF16),
        pltpu.VMEM((TILE_DEV, D_ENC), F32),
        pltpu.VMEM((TILE_DEV, D_ENC), BF16),
    ]
    shapes = (((TILE_DEV, D), BF16),)
    return call(embed_kernel, "embed_rows", shapes, "svvvv-v", scratch, 1_400_000_000, 9_000_000)(*args)[0]


def key_picks(table, h, first, count):
    rate, base = table[RATE], table[PAIR_START]
    lane = iota((KEY_SLOTS, TILE_DEV), 1)
    place = iota((KEY_SLOTS, TILE_DEV), 0) * rate + ((h - base) & (rate - 1)) + (base - first)
    return ((lane == place) & (lane < count)).astype(BF16)


def key_rows(kv, h):
    rest = jnp.zeros((LANES - 2 * HEAD_DIM, TILE_DEV), BF16)
    return jnp.concatenate([kv[head_rows(h)], kv[head_rows(HEADS + h)], rest], axis=0)


def head_rows(h):
    return slice(h * HEAD_DIM, (h + 1) * HEAD_DIM)


def segments(table, position):
    length = jnp.full((1, 1), table[SEGMENT], I32).astype(F32)
    return jnp.floor((position.astype(F32) + 0.5) / length)


def own_kernel(table, own, q_a, q_b, payload, q_out, kv_out, out_sum, out_best, out_total):
    rate, start_me, count_me = table[RATE], table[START_ME], table[COUNT_ME]
    first, second = halves(table, own, D // 2)
    q_out[...] = (dot_nt(q_a[:D], first) + dot_nt(q_b[:D], second)).astype(BF16)
    kv_out[...] = (dot_nt(q_a[D:], first) + dot_nt(q_b[D:], second)).astype(BF16)
    slot = iota((SLOTS, TILE_DEV), 0) * rate
    lane = iota((SLOTS, TILE_DEV), 1)
    rest = jnp.zeros((LANES - HEAD_DIM, TILE_DEV), BF16)
    for h in range(HEADS):
        payload[h, :KEY_SLOTS] = dot_nt(key_picks(table, h, start_me, count_me), key_rows(kv_out, h)).astype(BF16)
        pick = (lane == slot + ((h - start_me) & (rate - 1))).astype(BF16)
        ask = jnp.concatenate([q_out[head_rows(h)], rest], axis=0)
        payload[h, KEY_SLOTS:] = dot_nt(pick, ask).astype(BF16)
    key_at = iota((TILE_DEV, 1), 0)
    key_seg = jnp.where(key_at < count_me, segments(table, start_me + key_at), -1.0)
    allowed = key_seg == segments(table, start_me + iota((1, TILE_DEV), 1))
    for h in range(HEADS):
        rows = head_rows(h)
        scores = jnp.where(allowed, dot_tn(kv_out[rows], q_out[rows]) * SCALE, BIG_NEGATIVE)
        best = jnp.max(scores, axis=0, keepdims=True)
        weights = jnp.exp(scores - best)
        out_best[h : h + 1] = best
        out_total[h : h + 1] = jnp.sum(weights, axis=0, keepdims=True)
        out_sum[rows] = dot_nn(kv_out[head_rows(HEADS + h)], weights.astype(BF16))


def own_rows(*args):
    stat = ((HEADS, TILE_DEV), F32)
    pay = ((HEADS, KEY_SLOTS + SLOTS, LANES), BF16)
    shapes = (pay, ((D, TILE_DEV), BF16), ((2 * D, TILE_DEV), BF16), ((D, TILE_DEV), F32), stat, stat)
    return call(own_kernel, "own_rows", shapes, "svvv-vvvvvv", [], 1_000_000_000, 5_000_000, 600_000)(*args)


def pair_kernel(table, partner, q_a, q_b, own_payload, payload, rim, kv):
    first, second = halves(table, partner, D // 2)
    kv[...] = (dot_nt(q_a[D:], first) + dot_nt(q_b[D:], second)).astype(BF16)
    for h in range(HEADS):
        picks = key_picks(table, h, table[START_OTHER], table[COUNT_OTHER])
        both = dot_nt(picks, key_rows(kv, h)) + own_payload[h, :KEY_SLOTS].astype(F32)
        payload[h, :KEY_SLOTS] = both.astype(BF16)
        payload[h, KEY_SLOTS:] = own_payload[h, KEY_SLOTS:]
    rim_first = jnp.where(table[HIGH] == 0, 0, table[COUNT_OTHER] - HALF)
    pick = (iota((TILE_DEV, HALF), 0) == iota((TILE_DEV, HALF), 1) + rim_first).astype(BF16)
    rim[...] = dot_nn(kv[...], pick).astype(BF16)


def pair_rows(*args):
    shapes = (((HEADS, KEY_SLOTS + SLOTS, LANES), BF16), ((2 * D, HALF), BF16))
    scratch = [pltpu.VMEM((2 * D, TILE_DEV), BF16)]
    return call(pair_kernel, "pair_rows", shapes, "svvvv-vv", scratch, 700_000_000, 4_000_000)(*args)


def rim_kernel(table, q, near_rim, halo, q_a, q_b, own_sum, own_best, own_total, out_sum, out_best, out_total, far_rim):
    start_me, end_me = table[START_ME], table[START_ME] + table[COUNT_ME]
    first, second = halves(table, halo, D // 2)
    far_rim[...] = (dot_nt(q_a[D:], first) + dot_nt(q_b[D:], second)).astype(BF16)
    query_seg = segments(table, start_me + iota((1, TILE_DEV), 1))

    def allowed(begin):
        at = begin + iota((HALF, 1), 0)
        return jnp.where((at >= 0) & (at < SEQ_LEN), segments(table, at), -1.0) == query_seg

    upper = table[HIGH] == 0
    near_ok = allowed(jnp.where(upper, end_me, start_me - HALF))
    far_ok = allowed(jnp.where(upper, start_me - HALF, end_me))
    for h in range(HEADS):
        rows, v_rows = head_rows(h), head_rows(HEADS + h)
        near = jnp.where(near_ok, dot_tn(near_rim[rows], q[rows]) * SCALE, BIG_NEGATIVE)
        far = jnp.where(far_ok, dot_tn(far_rim[rows], q[rows]) * SCALE, BIG_NEGATIVE)
        best_o = own_best[h : h + 1]
        best = jnp.maximum(jnp.max(jnp.maximum(near, far), axis=0, keepdims=True), best_o)
        near, far, scale = jnp.exp(near - best), jnp.exp(far - best), jnp.exp(best_o - best)
        out_best[h : h + 1] = best
        out_total[h : h + 1] = jnp.sum(near + far, axis=0, keepdims=True) + scale * own_total[h : h + 1]
        summed = dot_nn(near_rim[v_rows], near.astype(BF16)) + dot_nn(far_rim[v_rows], far.astype(BF16))
        out_sum[rows] = summed + scale * own_sum[rows]


def rim_rows(*args):
    stat = ((HEADS, TILE_DEV), F32)
    shapes = (((D, TILE_DEV), F32), stat, stat)
    scratch = [pltpu.VMEM((2 * D, HALF), BF16)]
    return call(rim_kernel, "rim_rows", shapes, "svvvvvvvv-vvv", scratch, 400_000_000, 5_000_000, 400_000)(*args)


def far_kernel(table, arrived, answer, scores):
    rate = table[RATE]
    kv = arrived[:, :KEY_SLOTS].reshape(PLANES * KEY_SLOTS, LANES)
    group = 8
    width = group * SLOTS
    slot = iota((KEY_SLOTS, width), 0) * rate
    for n in range(PLANES // group):
        asks = arrived[n * group : (n + 1) * group, KEY_SLOTS:].reshape(width, LANES)
        best = jnp.full((1, width), BIG_NEGATIVE, F32)
        for p in range(PLANES):
            phase = (table[PLANE_ID] - table[ALL_STARTS + p]) & (rate - 1)
            piece = dot_nt(arrived[p, :KEY_SLOTS], asks) * SCALE
            piece = jnp.where(slot + phase < table[ALL_COUNTS + p], piece, BIG_NEGATIVE)
            scores[p * KEY_SLOTS : (p + 1) * KEY_SLOTS] = piece
            best = jnp.maximum(best, jnp.max(piece, axis=0, keepdims=True))
        weights = jnp.exp(scores[...] - best)
        total = jnp.sum(weights, axis=0, keepdims=True)
        summed = dot_tn(kv, weights.astype(BF16))
        shared = summed[HEAD_DIM : 2 * HEAD_DIM] / total
        log_all = best + jnp.log(total)
        log_a = log_all.astype(BF16).astype(F32)
        log_b = (log_all - log_a).astype(BF16).astype(F32)
        log_c = log_all - log_a - log_b
        row = iota((LANES - HEAD_DIM, width), 0)
        tail = jnp.where(row == 0, log_a, jnp.where(row == 1, log_b, jnp.where(row == 2, log_c, 0.0)))
        block = jnp.concatenate([shared, tail], axis=0)
        answer[n * group : (n + 1) * group] = block.T.astype(BF16).reshape(group, SLOTS, LANES)


def far_branch(*args):
    shapes = (((PLANES, SLOTS, LANES), BF16),)
    scratch = [pltpu.VMEM((PLANES * KEY_SLOTS, PLANES // 2 * SLOTS), F32)]
    return call(far_kernel, "far_branch", shapes, "sv-v", scratch, 500_000_000, 1_000_000, 1_000_000)(*args)[0]


def finish_kernel(table, answers, local_sum, local_best, local_total, listing, out, attended):
    rate = table[RATE]
    slot = iota((SLOTS, TILE_DEV), 0) * rate
    lane = iota((SLOTS, TILE_DEV), 1)
    row = iota((1, TILE_DEV), 1)
    live = row < table[COUNT_ME]
    for h in range(HEADS):
        rows = slice(h * HEAD_DIM, (h + 1) * HEAD_DIM)
        phase = (h - table[START_ME]) & (rate - 1)
        pick = (lane == slot + phase).astype(BF16)
        wide = dot_tn(answers[h], pick)
        log_all = wide[HEAD_DIM : HEAD_DIM + 1] + wide[HEAD_DIM + 1 : HEAD_DIM + 2] + wide[HEAD_DIM + 2 : HEAD_DIM + 3]
        log_all = jnp.where((row & (rate - 1)) == phase, log_all, BIG_NEGATIVE)
        best = local_best[h : h + 1]
        joint = jnp.maximum(best, log_all)
        near = jnp.exp(best - joint)
        far = jnp.exp(log_all - joint)
        below = jnp.where(live, near * local_total[h : h + 1] + far, 1.0)
        mixed = (near * local_sum[rows] + far * wide[:HEAD_DIM]) / below
        attended[rows] = jnp.where(live, mixed, 0.0).astype(BF16)
    back = (listing[0] == iota((TILE_DEV, TILE_DEV), 0)).astype(BF16)
    out[0] = dot_nt(back, attended[...]).astype(BF16)


def finish(*args):
    shapes = (((1, TILE_DEV, D), BF16),)
    scratch = [pltpu.VMEM((D, TILE_DEV), BF16)]
    return call(finish_kernel, "finish_rows", shapes, "svvvvv-v", scratch, 100_000_000, 1_500_000, 10_000)(*args)[0]


def mirrored(x):
    z_low = lax.axis_size("zlo")
    pairs = [
        (low * 2 + high, (z_low - 1 - low) * 2 + (1 - high))
        for low in range(z_low)
        for high in range(2)
    ]
    return lax.ppermute(x, ("zlo", "zhi"), pairs)


def along_z(x, part):
    z_low = lax.axis_size("zlo")

    def rank(z, core):
        return (z % z_low * 2 + core) * 2 + z // z_low

    half = z_low // 2 if part == 0 else z_low - z_low // 2
    pairs = []
    for z in range(2 * z_low):
        for core in range(2):
            step = half if core == 0 else -half
            pairs.append((rank(z, core), rank((z + step) % (2 * z_low), core)))
    return lax.ppermute(x, ("zlo", "core", "zhi"), pairs)


def other_core(x):
    return lax.ppermute(x, "core", [(0, 1), (1, 0)])


def over_plane(x):
    return lax.all_to_all(x, PLANE, 0, 0)


def hold(*values):
    return lax.optimization_barrier(values)


def copies(x):
    return jnp.broadcast_to(x[None], (PLANES,) + x.shape)


def along_lines(x, stage):
    groups = []
    for low in range(lax.axis_size("zlo")):
        for core in range(2):
            for high in range(2):
                for line in range(4):
                    across_x = (core == 0) == (stage == 0)
                    plane = [line * 4 + k if across_x else k * 4 + line for k in range(4)]
                    groups.append([((low * 2 + core) * PLANES + p) * 2 + high for p in plane])
    spread = jnp.broadcast_to(x[None], (4,) + x.shape)
    return lax.all_to_all(spread, EVERY, 0, 0, axis_index_groups=groups)


def in_order(own, other, high):
    return jnp.where(high == 0, jnp.concatenate([own, other]), jnp.concatenate([other, own]))


def on_device(ctx_in, resid, enc_out_w, slide_proj, qkv_w, tissue, kept_count, dilation):
    core = lax.axis_index("core")
    high = lax.axis_index("zhi")
    plane_id = lax.axis_index("y") * lax.axis_size("x") + lax.axis_index("x")

    w_own = lax.dynamic_slice_in_dim(enc_out_w, core * D, D, 0).T
    p_own = lax.dynamic_slice_in_dim(slide_proj, core * D, D, 0).T
    q_own = lax.dynamic_slice_in_dim(qkv_w, core * (D // 2), D // 2, 0).T
    other_wp = mirrored(jnp.concatenate([w_own, p_own]))
    q_other = mirrored(q_own)
    place = jnp.stack([core, high, plane_id]).astype(I32)
    own_ctx, own_res, table = prepare(place, kept_count, dilation, ctx_in, resid, tissue)
    wp = jnp.concatenate(
        [in_order(w_own, other_wp[:W_ROWS], high), in_order(p_own, other_wp[W_ROWS:], high)]
    )
    wp = along_lines(along_lines(wp, 0).reshape(-1, D), 1).reshape(PLANES, -1, D)
    q_both = copies(in_order(q_own, q_other, high))
    wp, q_both = hold(wp, q_both)
    q_a = over_plane(q_both)
    embedded = embed(table, own_ctx, own_res, wp, other_core(wp))
    on_way = along_z(embedded, 0)
    q_a, embedded, on_way = hold(q_a, embedded, on_way)
    q_a = q_a.reshape(3 * D, D // 2)
    q_b = other_core(q_a)
    partner = along_z(on_way, 1)
    own_payload, q_rows, _, own_sum, own_best, own_total = own_rows(table, embedded, q_a, q_b)
    partner, own_payload = hold(partner, own_payload)
    rim_from = jnp.where(high == 0, table[COUNT_OTHER] - HALF, 0)
    rim = lax.dynamic_slice_in_dim(partner, rim_from, HALF, 0)
    halo_pairs = [(p * 2, p * 2 + 2) for p in range(PLANES - 1)]
    halo_pairs += [(p * 2 + 1, p * 2 - 1) for p in range(1, PLANES)]
    halo = lax.ppermute(rim, SEQ, halo_pairs)
    payload, near_rim = pair_rows(table, partner, q_a, q_b, own_payload)
    arrived = lax.all_to_all(payload, PLANE, 0, 0)
    local_sum, local_best, local_total = rim_rows(
        table, q_rows, near_rim, halo, q_a, q_b, own_sum, own_best, own_total
    )
    arrived, local_sum = hold(arrived, local_sum)
    answer = far_branch(table, arrived)
    answers = lax.all_to_all(answer, PLANE, 0, 0)
    return finish(table, answers, local_sum, local_best, local_total, tissue)


def solution(mesh):
    devices = mesh.devices.reshape(-1, 2, 4, 4, 2)
    split = Mesh(devices, ("zlo", "core", "y", "x", "zhi"))
    slide, seq = ("zlo", "core"), ("y", "x", "zhi")
    return jax.shard_map(
        on_device,
        mesh=split,
        in_specs=(
            P(slide, seq, None),
            P(slide, seq, None),
            P(None, seq),
            P(None, seq),
            P(None, seq),
            P(slide, seq, None),
            P(slide, None),
            P(slide, None),
        ),
        out_specs=P(slide, seq, None),
        check_vma=False,
    )
```

```python
import jax
import jax.numpy as jnp
from jax import lax
from jax.experimental import pallas as pl
from jax.experimental.pallas import tpu as pltpu
from jax.sharding import Mesh, PartitionSpec as P

HEADS = 16
HEAD_DIM = 48
D = 768
D_ENC = 1536
HALF = 64
TILE_DEV = 192
CHUNK = 96
SEQ_LEN = 4096
WINDOW = 320
KEY_SLOTS = 80
SLOTS = 48
LANES = 128
W_ROWS = 48
P_ROWS = 24
PLANES = 16
PLANE = ("y", "x")
SEQ = ("y", "x", "zhi")
EVERY = ("zlo", "core", "y", "x", "zhi")
NORM_EPS = 1e-06
BIG_NEGATIVE = -1e30
SCALE = HEAD_DIM**-0.5
BF16 = jnp.bfloat16
F32 = jnp.float32
I32 = jnp.int32
VMEM_LIMIT = 24 * 1024 * 1024

CORE, HIGH, PLANE_ID, RATE, SEGMENT = range(5)
START_ME, COUNT_ME, START_OTHER, COUNT_OTHER, PAIR_START, PAIR_COUNT = range(5, 11)
ALL_STARTS = 16
ALL_COUNTS = 32


def dot_nn(a, b):
    return lax.dot_general(a, b, (((1,), (0,)), ((), ())), preferred_element_type=F32)


def dot_nt(a, b):
    return lax.dot_general(a, b, (((1,), (1,)), ((), ())), preferred_element_type=F32)


def dot_tn(a, b):
    return lax.dot_general(a, b, (((0,), (0,)), ((), ())), preferred_element_type=F32)


def iota(shape, dim):
    return lax.broadcasted_iota(I32, shape, dim)


def call(kernel, name, out_shape, specs, scratch, flops, size, exps=0):
    vmem = pl.BlockSpec(memory_space=pltpu.VMEM)
    smem = pl.BlockSpec(memory_space=pltpu.SMEM)
    hbm = pl.BlockSpec(memory_space=pl.ANY)
    kinds = {"s": smem, "v": vmem, "h": hbm}
    ins, outs = specs.split("-")
    return pl.pallas_call(
        kernel,
        out_shape=tuple(jax.ShapeDtypeStruct(shape, dtype) for shape, dtype in out_shape),
        in_specs=[kinds[c] for c in ins],
        out_specs=tuple(kinds[c] for c in outs),
        scratch_shapes=scratch,
        compiler_params=pltpu.CompilerParams(vmem_limit_bytes=VMEM_LIMIT),
        cost_estimate=pl.CostEstimate(flops=flops, bytes_accessed=size, transcendentals=exps),
        name=name,
    )


def prepare_kernel(place, counts, dilation, ctx, res, listing, own_ctx, own_res, table):
    table[CORE], table[HIGH], table[PLANE_ID] = place[0], place[1], place[2]
    table[RATE], table[SEGMENT] = dilation[0, 1], dilation[0, 0]
    high = place[1]
    start = jnp.int32(0)
    for p in range(PLANES):
        first, second = counts[0, 2 * p], counts[0, 2 * p + 1]
        table[ALL_STARTS + p] = start
        table[ALL_COUNTS + p] = first + second

        @pl.when(place[2] == p)
        def _(first=first, second=second, start=start):
            table[PAIR_START] = start
            table[PAIR_COUNT] = first + second
            table[COUNT_ME] = jnp.where(high == 0, first, second)
            table[COUNT_OTHER] = jnp.where(high == 0, second, first)
            table[START_ME] = jnp.where(high == 0, start, start + first)
            table[START_OTHER] = jnp.where(high == 0, start + first, start)

        start = start + first + second
    order = (iota((TILE_DEV, TILE_DEV), 0) == listing[0]).astype(BF16)
    own_ctx[...] = dot_tn(order, ctx[0]).astype(BF16)
    own_res[...] = dot_tn(order, res[0]).astype(BF16)


def prepare(*args):
    rows = ((TILE_DEV, D_ENC), BF16)
    shapes = (rows, rows, ((ALL_COUNTS + PLANES,), I32))
    return call(prepare_kernel, "prepare_rows", shapes, "sssvvv-vvs", [], 250_000_000, 2_400_000)(*args)


def halves(table, ref, width):
    core = table[CORE]
    first = ref[:, pl.ds(pl.multiple_of(core * width, LANES), width)]
    second = ref[:, pl.ds(pl.multiple_of((1 - core) * width, LANES), width)]
    return first, second


def embed_kernel(table, ctx, res, own, other, out, lower, upper, w, p, hidden, normed):
    core = table[CORE]
    for block in range(PLANES):
        turned = block % 4 * 4 + block // 4
        at_own = jnp.where(core == 0, block, turned)
        at_other = jnp.where(core == 0, turned, block)
        w_rows = slice(block * 2 * W_ROWS, (block + 1) * 2 * W_ROWS)
        p_rows = slice(block * 2 * P_ROWS, (block + 1) * 2 * P_ROWS)
        w[core, w_rows] = own[at_own, : 2 * W_ROWS]
        p[core, p_rows] = own[at_own, 2 * W_ROWS :]
        w[1 - core, w_rows] = other[at_other, : 2 * W_ROWS]
        p[1 - core, p_rows] = other[at_other, 2 * W_ROWS :]
    total = jnp.zeros((TILE_DEV, 1), F32)
    width = D // 2
    for n in range(4):
        columns = slice(n * width, (n + 1) * width)
        part = res[:, columns].astype(F32) + dot_nt(ctx[:, :D], w[0, columns]) + dot_nt(ctx[:, D:], w[1, columns])
        hidden[:, columns] = part
        total += jnp.sum(part, axis=1, keepdims=True)
    center = hidden[...] - total / D_ENC
    spread = jnp.sum(center * center, axis=1, keepdims=True) / D_ENC
    normed[...] = (center * lax.rsqrt(spread + NORM_EPS)).astype(BF16)
    out[...] = (dot_nt(normed[:, :D], p[0]) + dot_nt(normed[:, D:], p[1])).astype(BF16)
    lower[...] = out[:CHUNK]
    upper[...] = out[CHUNK:]


def embed(*args):
    scratch = [
        pltpu.VMEM((2, D_ENC, D), BF16),
        pltpu.VMEM((2, D, D), BF16),
        pltpu.VMEM((TILE_DEV, D_ENC), F32),
        pltpu.VMEM((TILE_DEV, D_ENC), BF16),
    ]
    shapes = (((TILE_DEV, D), BF16), ((CHUNK, D), BF16), ((CHUNK, D), BF16))
    return call(embed_kernel, "embed_rows", shapes, "svvvv-vvv", scratch, 1_400_000_000, 9_000_000)(*args)


def key_picks(table, h, first, count):
    rate, base = table[RATE], table[PAIR_START]
    lane = iota((KEY_SLOTS, TILE_DEV), 1)
    place = iota((KEY_SLOTS, TILE_DEV), 0) * rate + ((h - base) & (rate - 1)) + (base - first)
    return ((lane == place) & (lane < count)).astype(BF16)


def key_rows(kv, h):
    rest = jnp.zeros((LANES - 2 * HEAD_DIM, TILE_DEV), BF16)
    return jnp.concatenate([kv[head_rows(h)], kv[head_rows(HEADS + h)], rest], axis=0)


def head_rows(h):
    return slice(h * HEAD_DIM, (h + 1) * HEAD_DIM)


def segments(table, position):
    length = jnp.full((1, 1), table[SEGMENT], I32).astype(F32)
    return jnp.floor((position.astype(F32) + 0.5) / length)


def own_kernel(table, own, q_a, q_b, payload, q_out, kv_out, out_sum, out_best, out_total):
    rate, start_me, count_me = table[RATE], table[START_ME], table[COUNT_ME]
    first, second = halves(table, own, D // 2)
    q_out[...] = (dot_nt(q_a[:D], first) + dot_nt(q_b[:D], second)).astype(BF16)
    kv_out[...] = (dot_nt(q_a[D:], first) + dot_nt(q_b[D:], second)).astype(BF16)
    slot = iota((SLOTS, TILE_DEV), 0) * rate
    lane = iota((SLOTS, TILE_DEV), 1)
    rest = jnp.zeros((LANES - HEAD_DIM, TILE_DEV), BF16)
    for h in range(HEADS):
        payload[h, :KEY_SLOTS] = dot_nt(key_picks(table, h, start_me, count_me), key_rows(kv_out, h)).astype(BF16)
        pick = (lane == slot + ((h - start_me) & (rate - 1))).astype(BF16)
        ask = jnp.concatenate([q_out[head_rows(h)], rest], axis=0)
        payload[h, KEY_SLOTS:] = dot_nt(pick, ask).astype(BF16)
    key_at = iota((TILE_DEV, 1), 0)
    key_seg = jnp.where(key_at < count_me, segments(table, start_me + key_at), -1.0)
    allowed = key_seg == segments(table, start_me + iota((1, TILE_DEV), 1))
    for h in range(HEADS):
        rows = head_rows(h)
        scores = jnp.where(allowed, dot_tn(kv_out[rows], q_out[rows]) * SCALE, BIG_NEGATIVE)
        best = jnp.max(scores, axis=0, keepdims=True)
        weights = jnp.exp(scores - best)
        out_best[h : h + 1] = best
        out_total[h : h + 1] = jnp.sum(weights, axis=0, keepdims=True)
        out_sum[rows] = dot_nn(kv_out[head_rows(HEADS + h)], weights.astype(BF16))


def own_rows(*args):
    stat = ((HEADS, TILE_DEV), F32)
    pay = ((HEADS, KEY_SLOTS + SLOTS, LANES), BF16)
    shapes = (pay, ((D, TILE_DEV), BF16), ((2 * D, TILE_DEV), BF16), ((D, TILE_DEV), F32), stat, stat)
    return call(own_kernel, "own_rows", shapes, "svvv-vvvvvv", [], 1_000_000_000, 5_000_000, 600_000)(*args)


def pair_kernel(table, lower, upper, q_a, q_b, own_payload, payload, rim, kv, partner):
    partner[:CHUNK] = lower[...]
    partner[CHUNK:] = upper[...]
    first, second = halves(table, partner, D // 2)
    kv[...] = (dot_nt(q_a[D:], first) + dot_nt(q_b[D:], second)).astype(BF16)
    for h in range(HEADS):
        picks = key_picks(table, h, table[START_OTHER], table[COUNT_OTHER])
        both = dot_nt(picks, key_rows(kv, h)) + own_payload[h, :KEY_SLOTS].astype(F32)
        payload[h, :KEY_SLOTS] = both.astype(BF16)
        payload[h, KEY_SLOTS:] = own_payload[h, KEY_SLOTS:]
    rim_first = jnp.where(table[HIGH] == 0, 0, table[COUNT_OTHER] - HALF)
    pick = (iota((TILE_DEV, HALF), 0) == iota((TILE_DEV, HALF), 1) + rim_first).astype(BF16)
    rim[...] = dot_nn(kv[...], pick).astype(BF16)


def pair_rows(*args):
    shapes = (((HEADS, KEY_SLOTS + SLOTS, LANES), BF16), ((2 * D, HALF), BF16))
    scratch = [pltpu.VMEM((2 * D, TILE_DEV), BF16), pltpu.VMEM((TILE_DEV, D), BF16)]
    return call(pair_kernel, "pair_rows", shapes, "svvvvv-vv", scratch, 700_000_000, 4_000_000)(*args)


def rim_kernel(table, q, near_rim, halo, q_a, q_b, own_sum, own_best, own_total, out_sum, out_best, out_total, far_rim):
    start_me, end_me = table[START_ME], table[START_ME] + table[COUNT_ME]
    first, second = halves(table, halo, D // 2)
    far_rim[...] = (dot_nt(q_a[D:], first) + dot_nt(q_b[D:], second)).astype(BF16)
    query_seg = segments(table, start_me + iota((1, TILE_DEV), 1))

    def allowed(begin):
        at = begin + iota((HALF, 1), 0)
        return jnp.where((at >= 0) & (at < SEQ_LEN), segments(table, at), -1.0) == query_seg

    upper = table[HIGH] == 0
    near_ok = allowed(jnp.where(upper, end_me, start_me - HALF))
    far_ok = allowed(jnp.where(upper, start_me - HALF, end_me))
    for h in range(HEADS):
        rows, v_rows = head_rows(h), head_rows(HEADS + h)
        near = jnp.where(near_ok, dot_tn(near_rim[rows], q[rows]) * SCALE, BIG_NEGATIVE)
        far = jnp.where(far_ok, dot_tn(far_rim[rows], q[rows]) * SCALE, BIG_NEGATIVE)
        best_o = own_best[h : h + 1]
        best = jnp.maximum(jnp.max(jnp.maximum(near, far), axis=0, keepdims=True), best_o)
        near, far, scale = jnp.exp(near - best), jnp.exp(far - best), jnp.exp(best_o - best)
        out_best[h : h + 1] = best
        out_total[h : h + 1] = jnp.sum(near + far, axis=0, keepdims=True) + scale * own_total[h : h + 1]
        summed = dot_nn(near_rim[v_rows], near.astype(BF16)) + dot_nn(far_rim[v_rows], far.astype(BF16))
        out_sum[rows] = summed + scale * own_sum[rows]


def rim_rows(*args):
    stat = ((HEADS, TILE_DEV), F32)
    shapes = (((D, TILE_DEV), F32), stat, stat)
    scratch = [pltpu.VMEM((2 * D, HALF), BF16)]
    return call(rim_kernel, "rim_rows", shapes, "svvvvvvvv-vvv", scratch, 400_000_000, 5_000_000, 400_000)(*args)


def far_kernel(table, arrived, answer, scores):
    rate = table[RATE]
    kv = arrived[:, :KEY_SLOTS].reshape(PLANES * KEY_SLOTS, LANES)
    group = 8
    width = group * SLOTS
    slot = iota((KEY_SLOTS, width), 0) * rate
    for n in range(PLANES // group):
        asks = arrived[n * group : (n + 1) * group, KEY_SLOTS:].reshape(width, LANES)
        best = jnp.full((1, width), BIG_NEGATIVE, F32)
        for p in range(PLANES):
            phase = (table[PLANE_ID] - table[ALL_STARTS + p]) & (rate - 1)
            piece = dot_nt(arrived[p, :KEY_SLOTS], asks) * SCALE
            piece = jnp.where(slot + phase < table[ALL_COUNTS + p], piece, BIG_NEGATIVE)
            scores[p * KEY_SLOTS : (p + 1) * KEY_SLOTS] = piece
            best = jnp.maximum(best, jnp.max(piece, axis=0, keepdims=True))
        weights = jnp.exp(scores[...] - best)
        total = jnp.sum(weights, axis=0, keepdims=True)
        summed = dot_tn(kv, weights.astype(BF16))
        shared = summed[HEAD_DIM : 2 * HEAD_DIM] / total
        log_all = best + jnp.log(total)
        log_a = log_all.astype(BF16).astype(F32)
        log_b = (log_all - log_a).astype(BF16).astype(F32)
        log_c = log_all - log_a - log_b
        row = iota((LANES - HEAD_DIM, width), 0)
        tail = jnp.where(row == 0, log_a, jnp.where(row == 1, log_b, jnp.where(row == 2, log_c, 0.0)))
        block = jnp.concatenate([shared, tail], axis=0)
        answer[n * group : (n + 1) * group] = block.T.astype(BF16).reshape(group, SLOTS, LANES)


def far_branch(*args):
    shapes = (((PLANES, SLOTS, LANES), BF16),)
    scratch = [pltpu.VMEM((PLANES * KEY_SLOTS, PLANES // 2 * SLOTS), F32)]
    return call(far_kernel, "far_branch", shapes, "sv-v", scratch, 500_000_000, 1_000_000, 1_000_000)(*args)[0]


def finish_kernel(table, answers, local_sum, local_best, local_total, listing, out, attended):
    rate = table[RATE]
    slot = iota((SLOTS, TILE_DEV), 0) * rate
    lane = iota((SLOTS, TILE_DEV), 1)
    row = iota((1, TILE_DEV), 1)
    live = row < table[COUNT_ME]
    for h in range(HEADS):
        rows = slice(h * HEAD_DIM, (h + 1) * HEAD_DIM)
        phase = (h - table[START_ME]) & (rate - 1)
        pick = (lane == slot + phase).astype(BF16)
        wide = dot_tn(answers[h], pick)
        log_all = wide[HEAD_DIM : HEAD_DIM + 1] + wide[HEAD_DIM + 1 : HEAD_DIM + 2] + wide[HEAD_DIM + 2 : HEAD_DIM + 3]
        log_all = jnp.where((row & (rate - 1)) == phase, log_all, BIG_NEGATIVE)
        best = local_best[h : h + 1]
        joint = jnp.maximum(best, log_all)
        near = jnp.exp(best - joint)
        far = jnp.exp(log_all - joint)
        below = jnp.where(live, near * local_total[h : h + 1] + far, 1.0)
        mixed = (near * local_sum[rows] + far * wide[:HEAD_DIM]) / below
        attended[rows] = jnp.where(live, mixed, 0.0).astype(BF16)
    back = (listing[0] == iota((TILE_DEV, TILE_DEV), 0)).astype(BF16)
    out[0] = dot_nt(back, attended[...]).astype(BF16)


def finish(*args):
    shapes = (((1, TILE_DEV, D), BF16),)
    scratch = [pltpu.VMEM((D, TILE_DEV), BF16)]
    return call(finish_kernel, "finish_rows", shapes, "svvvvv-v", scratch, 100_000_000, 1_500_000, 10_000)(*args)[0]


def mirrored(x):
    z_low = lax.axis_size("zlo")
    pairs = [
        (low * 2 + high, (z_low - 1 - low) * 2 + (1 - high))
        for low in range(z_low)
        for high in range(2)
    ]
    return lax.ppermute(x, ("zlo", "zhi"), pairs)


def along_z(x, part):
    z_low = lax.axis_size("zlo")

    def rank(z, core):
        return (z % z_low * 2 + core) * 2 + z // z_low

    half = z_low // 2 if part == 0 else z_low - z_low // 2
    pairs = []
    for z in range(2 * z_low):
        for core in range(2):
            step = half if core == 0 else -half
            pairs.append((rank(z, core), rank((z + step) % (2 * z_low), core)))
    return lax.ppermute(x, ("zlo", "core", "zhi"), pairs)


def other_core(x):
    return lax.ppermute(x, "core", [(0, 1), (1, 0)])


def over_plane(x):
    return lax.all_to_all(x, PLANE, 0, 0)


def hold(*values):
    return lax.optimization_barrier(values)


def copies(x):
    return jnp.broadcast_to(x[None], (PLANES,) + x.shape)


def along_lines(x, stage):
    groups = []
    for low in range(lax.axis_size("zlo")):
        for core in range(2):
            for high in range(2):
                for line in range(4):
                    across_x = (core == 0) == (stage == 0)
                    plane = [line * 4 + k if across_x else k * 4 + line for k in range(4)]
                    groups.append([((low * 2 + core) * PLANES + p) * 2 + high for p in plane])
    spread = jnp.broadcast_to(x[None], (4,) + x.shape)
    return lax.all_to_all(spread, EVERY, 0, 0, axis_index_groups=groups)


def in_order(own, other, high):
    return jnp.where(high == 0, jnp.concatenate([own, other]), jnp.concatenate([other, own]))


def on_device(ctx_in, resid, enc_out_w, slide_proj, qkv_w, tissue, kept_count, dilation):
    core = lax.axis_index("core")
    high = lax.axis_index("zhi")
    plane_id = lax.axis_index("y") * lax.axis_size("x") + lax.axis_index("x")

    w_own = lax.dynamic_slice_in_dim(enc_out_w, core * D, D, 0).T
    p_own = lax.dynamic_slice_in_dim(slide_proj, core * D, D, 0).T
    q_own = lax.dynamic_slice_in_dim(qkv_w, core * (D // 2), D // 2, 0).T
    other_wp = mirrored(jnp.concatenate([w_own, p_own]))
    q_other = mirrored(q_own)
    place = jnp.stack([core, high, plane_id]).astype(I32)
    own_ctx, own_res, table = prepare(place, kept_count, dilation, ctx_in, resid, tissue)
    wp = jnp.concatenate(
        [in_order(w_own, other_wp[:W_ROWS], high), in_order(p_own, other_wp[W_ROWS:], high)]
    )
    wp = along_lines(along_lines(wp, 0).reshape(-1, D), 1).reshape(PLANES, -1, D)
    q_both = copies(in_order(q_own, q_other, high))
    wp, q_both = hold(wp, q_both)
    q_a = over_plane(q_both)
    embedded, lower, upper = embed(table, own_ctx, own_res, wp, other_core(wp))
    lower = along_z(along_z(lower, 0), 1)
    upper = along_z(upper, 0)
    q_a, embedded, lower, upper = hold(q_a, embedded, lower, upper)
    q_a = q_a.reshape(3 * D, D // 2)
    q_b = other_core(q_a)
    upper = along_z(upper, 1)
    own_payload, q_rows, _, own_sum, own_best, own_total = own_rows(table, embedded, q_a, q_b)
    upper, own_payload = hold(upper, own_payload)
    rim_from = jnp.where(high == 0, table[COUNT_OTHER] - HALF, 0)
    rim = lax.dynamic_slice_in_dim(jnp.concatenate([lower, upper]), rim_from, HALF, 0)
    halo_pairs = [(p * 2, p * 2 + 2) for p in range(PLANES - 1)]
    halo_pairs += [(p * 2 + 1, p * 2 - 1) for p in range(1, PLANES)]
    halo = lax.ppermute(rim, SEQ, halo_pairs)
    payload, near_rim = pair_rows(table, lower, upper, q_a, q_b, own_payload)
    arrived, halo = hold(lax.all_to_all(payload, PLANE, 0, 0), halo)
    local_sum, local_best, local_total = rim_rows(
        table, q_rows, near_rim, halo, q_a, q_b, own_sum, own_best, own_total
    )
    answer = far_branch(table, arrived)
    answers = lax.all_to_all(answer, PLANE, 0, 0)
    return finish(table, answers, local_sum, local_best, local_total, tissue)


def solution(mesh):
    devices = mesh.devices.reshape(-1, 2, 4, 4, 2)
    split = Mesh(devices, ("zlo", "core", "y", "x", "zhi"))
    slide, seq = ("zlo", "core"), ("y", "x", "zhi")
    return jax.shard_map(
        on_device,
        mesh=split,
        in_specs=(
            P(slide, seq, None),
            P(slide, seq, None),
            P(None, seq),
            P(None, seq),
            P(None, seq),
            P(slide, seq, None),
            P(slide, None),
            P(slide, None),
        ),
        out_specs=P(slide, seq, None),
        check_vma=False,
    )
```

```python
import jax
import jax.numpy as jnp
from jax import lax
from jax.experimental import pallas as pl
from jax.experimental.pallas import tpu as pltpu
from jax.sharding import Mesh, PartitionSpec as P

HEADS = 16
HEAD_DIM = 48
D = 768
D_ENC = 1536
HALF = 64
TILE_DEV = 192
CHUNK = 64
SEQ_LEN = 4096
WINDOW = 320
KEY_SLOTS = 80
SLOTS = 48
LANES = 128
W_ROWS = 48
P_ROWS = 24
PLANES = 16
PLANE = ("y", "x")
SEQ = ("y", "x", "zhi")
EVERY = ("zlo", "core", "y", "x", "zhi")
NORM_EPS = 1e-06
BIG_NEGATIVE = -1e30
SCALE = HEAD_DIM**-0.5
BF16 = jnp.bfloat16
F32 = jnp.float32
I32 = jnp.int32
VMEM_LIMIT = 24 * 1024 * 1024

CORE, HIGH, PLANE_ID, RATE, SEGMENT = range(5)
START_ME, COUNT_ME, START_OTHER, COUNT_OTHER, PAIR_START, PAIR_COUNT = range(5, 11)
ALL_STARTS = 16
ALL_COUNTS = 32


def dot_nn(a, b):
    return lax.dot_general(a, b, (((1,), (0,)), ((), ())), preferred_element_type=F32)


def dot_nt(a, b):
    return lax.dot_general(a, b, (((1,), (1,)), ((), ())), preferred_element_type=F32)


def dot_tn(a, b):
    return lax.dot_general(a, b, (((0,), (0,)), ((), ())), preferred_element_type=F32)


def iota(shape, dim):
    return lax.broadcasted_iota(I32, shape, dim)


def call(kernel, name, out_shape, specs, scratch, flops, size, exps=0):
    vmem = pl.BlockSpec(memory_space=pltpu.VMEM)
    smem = pl.BlockSpec(memory_space=pltpu.SMEM)
    hbm = pl.BlockSpec(memory_space=pl.ANY)
    kinds = {"s": smem, "v": vmem, "h": hbm}
    ins, outs = specs.split("-")
    return pl.pallas_call(
        kernel,
        out_shape=tuple(jax.ShapeDtypeStruct(shape, dtype) for shape, dtype in out_shape),
        in_specs=[kinds[c] for c in ins],
        out_specs=tuple(kinds[c] for c in outs),
        scratch_shapes=scratch,
        compiler_params=pltpu.CompilerParams(vmem_limit_bytes=VMEM_LIMIT),
        cost_estimate=pl.CostEstimate(flops=flops, bytes_accessed=size, transcendentals=exps),
        name=name,
    )


def prepare_kernel(place, counts, dilation, ctx, res, listing, own_ctx, own_res, table):
    table[CORE], table[HIGH], table[PLANE_ID] = place[0], place[1], place[2]
    table[RATE], table[SEGMENT] = dilation[0, 1], dilation[0, 0]
    high = place[1]
    start = jnp.int32(0)
    for p in range(PLANES):
        first, second = counts[0, 2 * p], counts[0, 2 * p + 1]
        table[ALL_STARTS + p] = start
        table[ALL_COUNTS + p] = first + second

        @pl.when(place[2] == p)
        def _(first=first, second=second, start=start):
            table[PAIR_START] = start
            table[PAIR_COUNT] = first + second
            table[COUNT_ME] = jnp.where(high == 0, first, second)
            table[COUNT_OTHER] = jnp.where(high == 0, second, first)
            table[START_ME] = jnp.where(high == 0, start, start + first)
            table[START_OTHER] = jnp.where(high == 0, start + first, start)

        start = start + first + second
    order = (iota((TILE_DEV, TILE_DEV), 0) == listing[0]).astype(BF16)
    own_ctx[...] = dot_tn(order, ctx[0]).astype(BF16)
    own_res[...] = dot_tn(order, res[0]).astype(BF16)


def prepare(*args):
    rows = ((TILE_DEV, D_ENC), BF16)
    shapes = (rows, rows, ((ALL_COUNTS + PLANES,), I32))
    return call(prepare_kernel, "prepare_rows", shapes, "sssvvv-vvs", [], 250_000_000, 2_400_000)(*args)


def halves(table, ref, width):
    core = table[CORE]
    first = ref[:, pl.ds(pl.multiple_of(core * width, LANES), width)]
    second = ref[:, pl.ds(pl.multiple_of((1 - core) * width, LANES), width)]
    return first, second


def embed_kernel(table, ctx, res, own, other, out, lower, upper, w, p, hidden, normed, sems):
    core = table[CORE]
    w_loads, p_loads = [], []
    for block in range(PLANES):
        turned = block % 4 * 4 + block // 4
        at_own = jnp.where(core == 0, block, turned)
        at_other = jnp.where(core == 0, turned, block)
        for n, (source, half, at) in enumerate(((own, core, at_own), (other, 1 - core, at_other))):
            w_loads.append(
                pltpu.make_async_copy(source.at[at, : 2 * W_ROWS], w.at[half, block], sems.at[0, n, block])
            )
            p_loads.append(
                pltpu.make_async_copy(source.at[at, 2 * W_ROWS :], p.at[half, block], sems.at[1, n, block])
            )
    for load in w_loads + p_loads:
        load.start()
    total = jnp.zeros((TILE_DEV, 1), F32)
    width = D // 2
    group = PLANES // 4
    for n in range(4):
        for load in w_loads[2 * group * n : 2 * group * (n + 1)]:
            load.wait()
        columns = slice(n * width, (n + 1) * width)
        part = res[:, columns].astype(F32)
        for half in range(2):
            rows = w[half, n * group : (n + 1) * group].reshape(width, D)
            part += dot_nt(ctx[:, half * D : (half + 1) * D], rows)
        hidden[:, columns] = part
        total += jnp.sum(part, axis=1, keepdims=True)
    center = hidden[...] - total / D_ENC
    spread = jnp.sum(center * center, axis=1, keepdims=True) / D_ENC
    normed[...] = (center * lax.rsqrt(spread + NORM_EPS)).astype(BF16)
    for load in p_loads:
        load.wait()
    out[...] = (dot_nt(normed[:, :D], p[0].reshape(D, D)) + dot_nt(normed[:, D:], p[1].reshape(D, D))).astype(BF16)
    lower[...] = out[:CHUNK]
    upper[...] = out[CHUNK:]


def embed(*args):
    scratch = [
        pltpu.VMEM((2, PLANES, 2 * W_ROWS, D), BF16),
        pltpu.VMEM((2, PLANES, 2 * P_ROWS, D), BF16),
        pltpu.VMEM((TILE_DEV, D_ENC), F32),
        pltpu.VMEM((TILE_DEV, D_ENC), BF16),
        pltpu.SemaphoreType.DMA((2, 2, PLANES)),
    ]
    shapes = (((TILE_DEV, D), BF16), ((CHUNK, D), BF16), ((TILE_DEV - CHUNK, D), BF16))
    return call(embed_kernel, "embed_rows", shapes, "svvhh-vvv", scratch, 1_400_000_000, 9_000_000)(*args)


def key_picks(table, h, first, count):
    rate, base = table[RATE], table[PAIR_START]
    lane = iota((KEY_SLOTS, TILE_DEV), 1)
    place = iota((KEY_SLOTS, TILE_DEV), 0) * rate + ((h - base) & (rate - 1)) + (base - first)
    return ((lane == place) & (lane < count)).astype(BF16)


def key_rows(kv, h):
    rest = jnp.zeros((LANES - 2 * HEAD_DIM, TILE_DEV), BF16)
    return jnp.concatenate([kv[head_rows(h)], kv[head_rows(HEADS + h)], rest], axis=0)


def head_rows(h):
    return slice(h * HEAD_DIM, (h + 1) * HEAD_DIM)


def segments(table, position):
    length = jnp.full((1, 1), table[SEGMENT], I32).astype(F32)
    return jnp.floor((position.astype(F32) + 0.5) / length)


def own_kernel(table, own, q_a, q_b, payload, q_out, kv_out, out_sum, out_best, out_total):
    rate, start_me, count_me = table[RATE], table[START_ME], table[COUNT_ME]
    first, second = halves(table, own, D // 2)
    q_out[...] = (dot_nt(q_a[:D], first) + dot_nt(q_b[:D], second)).astype(BF16)
    kv_out[...] = (dot_nt(q_a[D:], first) + dot_nt(q_b[D:], second)).astype(BF16)
    slot = iota((SLOTS, TILE_DEV), 0) * rate
    lane = iota((SLOTS, TILE_DEV), 1)
    rest = jnp.zeros((LANES - HEAD_DIM, TILE_DEV), BF16)
    for h in range(HEADS):
        payload[h, :KEY_SLOTS] = dot_nt(key_picks(table, h, start_me, count_me), key_rows(kv_out, h)).astype(BF16)
        pick = (lane == slot + ((h - start_me) & (rate - 1))).astype(BF16)
        ask = jnp.concatenate([q_out[head_rows(h)], rest], axis=0)
        payload[h, KEY_SLOTS:] = dot_nt(pick, ask).astype(BF16)
    key_at = iota((TILE_DEV, 1), 0)
    key_seg = jnp.where(key_at < count_me, segments(table, start_me + key_at), -1.0)
    allowed = key_seg == segments(table, start_me + iota((1, TILE_DEV), 1))
    for h in range(HEADS):
        rows = head_rows(h)
        scores = jnp.where(allowed, dot_tn(kv_out[rows], q_out[rows]) * SCALE, BIG_NEGATIVE)
        best = jnp.max(scores, axis=0, keepdims=True)
        weights = jnp.exp(scores - best)
        out_best[h : h + 1] = best
        out_total[h : h + 1] = jnp.sum(weights, axis=0, keepdims=True)
        out_sum[rows] = dot_nn(kv_out[head_rows(HEADS + h)], weights.astype(BF16))


def own_rows(*args):
    stat = ((HEADS, TILE_DEV), F32)
    pay = ((HEADS, KEY_SLOTS + SLOTS, LANES), BF16)
    shapes = (pay, ((D, TILE_DEV), BF16), ((2 * D, TILE_DEV), BF16), ((D, TILE_DEV), F32), stat, stat)
    return call(own_kernel, "own_rows", shapes, "svvv-vvvvvv", [], 1_000_000_000, 5_000_000, 600_000)(*args)


def pair_kernel(table, lower, upper, q_a, q_b, own_payload, payload, rim, kv, partner):
    partner[:CHUNK] = lower[...]
    partner[CHUNK:] = upper[...]
    first, second = halves(table, partner, D // 2)
    kv[...] = (dot_nt(q_a[D:], first) + dot_nt(q_b[D:], second)).astype(BF16)
    for h in range(HEADS):
        picks = key_picks(table, h, table[START_OTHER], table[COUNT_OTHER])
        both = dot_nt(picks, key_rows(kv, h)) + own_payload[h, :KEY_SLOTS].astype(F32)
        payload[h, :KEY_SLOTS] = both.astype(BF16)
        payload[h, KEY_SLOTS:] = own_payload[h, KEY_SLOTS:]
    rim_first = jnp.where(table[HIGH] == 0, 0, table[COUNT_OTHER] - HALF)
    pick = (iota((TILE_DEV, HALF), 0) == iota((TILE_DEV, HALF), 1) + rim_first).astype(BF16)
    rim[...] = dot_nn(kv[...], pick).astype(BF16)


def pair_rows(*args):
    shapes = (((HEADS, KEY_SLOTS + SLOTS, LANES), BF16), ((2 * D, HALF), BF16))
    scratch = [pltpu.VMEM((2 * D, TILE_DEV), BF16), pltpu.VMEM((TILE_DEV, D), BF16)]
    return call(pair_kernel, "pair_rows", shapes, "svvvvv-vv", scratch, 700_000_000, 4_000_000)(*args)


def rim_kernel(table, q, near_rim, halo, q_a, q_b, own_sum, own_best, own_total, out_sum, out_best, out_total, far_rim):
    start_me, end_me = table[START_ME], table[START_ME] + table[COUNT_ME]
    first, second = halves(table, halo, D // 2)
    far_rim[...] = (dot_nt(q_a[D:], first) + dot_nt(q_b[D:], second)).astype(BF16)
    query_seg = segments(table, start_me + iota((1, TILE_DEV), 1))

    def allowed(begin):
        at = begin + iota((HALF, 1), 0)
        return jnp.where((at >= 0) & (at < SEQ_LEN), segments(table, at), -1.0) == query_seg

    upper = table[HIGH] == 0
    near_ok = allowed(jnp.where(upper, end_me, start_me - HALF))
    far_ok = allowed(jnp.where(upper, start_me - HALF, end_me))
    for h in range(HEADS):
        rows, v_rows = head_rows(h), head_rows(HEADS + h)
        near = jnp.where(near_ok, dot_tn(near_rim[rows], q[rows]) * SCALE, BIG_NEGATIVE)
        far = jnp.where(far_ok, dot_tn(far_rim[rows], q[rows]) * SCALE, BIG_NEGATIVE)
        best_o = own_best[h : h + 1]
        best = jnp.maximum(jnp.max(jnp.maximum(near, far), axis=0, keepdims=True), best_o)
        near, far, scale = jnp.exp(near - best), jnp.exp(far - best), jnp.exp(best_o - best)
        out_best[h : h + 1] = best
        out_total[h : h + 1] = jnp.sum(near + far, axis=0, keepdims=True) + scale * own_total[h : h + 1]
        summed = dot_nn(near_rim[v_rows], near.astype(BF16)) + dot_nn(far_rim[v_rows], far.astype(BF16))
        out_sum[rows] = summed + scale * own_sum[rows]


def rim_rows(*args):
    stat = ((HEADS, TILE_DEV), F32)
    shapes = (((D, TILE_DEV), F32), stat, stat)
    scratch = [pltpu.VMEM((2 * D, HALF), BF16)]
    return call(rim_kernel, "rim_rows", shapes, "svvvvvvvv-vvv", scratch, 400_000_000, 5_000_000, 400_000)(*args)


def far_kernel(table, arrived, answer, scores):
    rate = table[RATE]
    kv = arrived[:, :KEY_SLOTS].reshape(PLANES * KEY_SLOTS, LANES)
    group = 8
    width = group * SLOTS
    slot = iota((KEY_SLOTS, width), 0) * rate
    for n in range(PLANES // group):
        asks = arrived[n * group : (n + 1) * group, KEY_SLOTS:].reshape(width, LANES)
        best = jnp.full((1, width), BIG_NEGATIVE, F32)
        for p in range(PLANES):
            phase = (table[PLANE_ID] - table[ALL_STARTS + p]) & (rate - 1)
            piece = dot_nt(arrived[p, :KEY_SLOTS], asks) * SCALE
            piece = jnp.where(slot + phase < table[ALL_COUNTS + p], piece, BIG_NEGATIVE)
            scores[p * KEY_SLOTS : (p + 1) * KEY_SLOTS] = piece
            best = jnp.maximum(best, jnp.max(piece, axis=0, keepdims=True))
        weights = jnp.exp(scores[...] - best)
        total = jnp.sum(weights, axis=0, keepdims=True)
        summed = dot_tn(kv, weights.astype(BF16))
        shared = summed[HEAD_DIM : 2 * HEAD_DIM] / total
        log_all = best + jnp.log(total)
        log_a = log_all.astype(BF16).astype(F32)
        log_b = (log_all - log_a).astype(BF16).astype(F32)
        log_c = log_all - log_a - log_b
        row = iota((LANES - HEAD_DIM, width), 0)
        tail = jnp.where(row == 0, log_a, jnp.where(row == 1, log_b, jnp.where(row == 2, log_c, 0.0)))
        block = jnp.concatenate([shared, tail], axis=0)
        answer[n * group : (n + 1) * group] = block.T.astype(BF16).reshape(group, SLOTS, LANES)


def far_branch(*args):
    shapes = (((PLANES, SLOTS, LANES), BF16),)
    scratch = [pltpu.VMEM((PLANES * KEY_SLOTS, PLANES // 2 * SLOTS), F32)]
    return call(far_kernel, "far_branch", shapes, "sv-v", scratch, 500_000_000, 1_000_000, 1_000_000)(*args)[0]


def finish_kernel(table, answers, local_sum, local_best, local_total, listing, out, attended):
    rate = table[RATE]
    slot = iota((SLOTS, TILE_DEV), 0) * rate
    lane = iota((SLOTS, TILE_DEV), 1)
    row = iota((1, TILE_DEV), 1)
    live = row < table[COUNT_ME]
    for h in range(HEADS):
        rows = slice(h * HEAD_DIM, (h + 1) * HEAD_DIM)
        phase = (h - table[START_ME]) & (rate - 1)
        pick = (lane == slot + phase).astype(BF16)
        wide = dot_tn(answers[h], pick)
        log_all = wide[HEAD_DIM : HEAD_DIM + 1] + wide[HEAD_DIM + 1 : HEAD_DIM + 2] + wide[HEAD_DIM + 2 : HEAD_DIM + 3]
        log_all = jnp.where((row & (rate - 1)) == phase, log_all, BIG_NEGATIVE)
        best = local_best[h : h + 1]
        joint = jnp.maximum(best, log_all)
        near = jnp.exp(best - joint)
        far = jnp.exp(log_all - joint)
        below = jnp.where(live, near * local_total[h : h + 1] + far, 1.0)
        mixed = (near * local_sum[rows] + far * wide[:HEAD_DIM]) / below
        attended[rows] = jnp.where(live, mixed, 0.0).astype(BF16)
    back = (listing[0] == iota((TILE_DEV, TILE_DEV), 0)).astype(BF16)
    out[0] = dot_nt(back, attended[...]).astype(BF16)


def finish(*args):
    shapes = (((1, TILE_DEV, D), BF16),)
    scratch = [pltpu.VMEM((D, TILE_DEV), BF16)]
    return call(finish_kernel, "finish_rows", shapes, "svvvvv-v", scratch, 100_000_000, 1_500_000, 10_000)(*args)[0]


def mirrored(x):
    z_low = lax.axis_size("zlo")
    pairs = [
        (low * 2 + high, (z_low - 1 - low) * 2 + (1 - high))
        for low in range(z_low)
        for high in range(2)
    ]
    return lax.ppermute(x, ("zlo", "zhi"), pairs)


def along_z(x, part):
    z_low = lax.axis_size("zlo")

    def rank(z, core):
        return (z % z_low * 2 + core) * 2 + z // z_low

    half = z_low // 2 if part == 0 else z_low - z_low // 2
    pairs = []
    for z in range(2 * z_low):
        for core in range(2):
            step = half if core == 0 else -half
            pairs.append((rank(z, core), rank((z + step) % (2 * z_low), core)))
    return lax.ppermute(x, ("zlo", "core", "zhi"), pairs)


def other_core(x):
    return lax.ppermute(x, "core", [(0, 1), (1, 0)])


def over_plane(x):
    return lax.all_to_all(x, PLANE, 0, 0)


def hold(*values):
    return lax.optimization_barrier(values)


def copies(x):
    return jnp.broadcast_to(x[None], (PLANES,) + x.shape)


def along_lines(x, stage):
    groups = []
    for low in range(lax.axis_size("zlo")):
        for core in range(2):
            for high in range(2):
                for line in range(4):
                    across_x = (core == 0) == (stage == 0)
                    plane = [line * 4 + k if across_x else k * 4 + line for k in range(4)]
                    groups.append([((low * 2 + core) * PLANES + p) * 2 + high for p in plane])
    spread = jnp.broadcast_to(x[None], (4,) + x.shape)
    return lax.all_to_all(spread, EVERY, 0, 0, axis_index_groups=groups)


def in_order(own, other, high):
    return jnp.where(high == 0, jnp.concatenate([own, other]), jnp.concatenate([other, own]))


def on_device(ctx_in, resid, enc_out_w, slide_proj, qkv_w, tissue, kept_count, dilation):
    core = lax.axis_index("core")
    high = lax.axis_index("zhi")
    plane_id = lax.axis_index("y") * lax.axis_size("x") + lax.axis_index("x")

    w_own = lax.dynamic_slice_in_dim(enc_out_w, core * D, D, 0).T
    p_own = lax.dynamic_slice_in_dim(slide_proj, core * D, D, 0).T
    q_own = lax.dynamic_slice_in_dim(qkv_w, core * (D // 2), D // 2, 0).T
    other_wp = mirrored(jnp.concatenate([w_own, p_own]))
    q_other = mirrored(q_own)
    place = jnp.stack([core, high, plane_id]).astype(I32)
    own_ctx, own_res, table = prepare(place, kept_count, dilation, ctx_in, resid, tissue)
    wp = jnp.concatenate(
        [in_order(w_own, other_wp[:W_ROWS], high), in_order(p_own, other_wp[W_ROWS:], high)]
    )
    wp = along_lines(along_lines(wp, 0).reshape(-1, D), 1).reshape(PLANES, -1, D)
    q_both = copies(in_order(q_own, q_other, high))
    wp, q_both = hold(wp, q_both)
    q_a = over_plane(q_both)
    embedded, lower, upper = embed(table, own_ctx, own_res, wp, other_core(wp))
    lower = along_z(along_z(lower, 0), 1)
    upper = along_z(upper, 0)
    q_a, embedded, lower, upper = hold(q_a, embedded, lower, upper)
    q_a = q_a.reshape(3 * D, D // 2)
    q_b = other_core(q_a)
    upper = along_z(upper, 1)
    own_payload, q_rows, _, own_sum, own_best, own_total = own_rows(table, embedded, q_a, q_b)
    upper, own_payload = hold(upper, own_payload)
    rim_from = jnp.where(high == 0, table[COUNT_OTHER] - HALF, 0)
    rim = lax.dynamic_slice_in_dim(jnp.concatenate([lower, upper]), rim_from, HALF, 0)
    halo_pairs = [(p * 2, p * 2 + 2) for p in range(PLANES - 1)]
    halo_pairs += [(p * 2 + 1, p * 2 - 1) for p in range(1, PLANES)]
    halo = lax.ppermute(rim, SEQ, halo_pairs)
    payload, near_rim = pair_rows(table, lower, upper, q_a, q_b, own_payload)
    arrived, halo = hold(lax.all_to_all(payload, PLANE, 0, 0), halo)
    local_sum, local_best, local_total = rim_rows(
        table, q_rows, near_rim, halo, q_a, q_b, own_sum, own_best, own_total
    )
    answer = far_branch(table, arrived)
    answers = lax.all_to_all(answer, PLANE, 0, 0)
    return finish(table, answers, local_sum, local_best, local_total, tissue)


def solution(mesh):
    devices = mesh.devices.reshape(-1, 2, 4, 4, 2)
    split = Mesh(devices, ("zlo", "core", "y", "x", "zhi"))
    slide, seq = ("zlo", "core"), ("y", "x", "zhi")
    return jax.shard_map(
        on_device,
        mesh=split,
        in_specs=(
            P(slide, seq, None),
            P(slide, seq, None),
            P(None, seq),
            P(None, seq),
            P(None, seq),
            P(slide, seq, None),
            P(slide, None),
            P(slide, None),
        ),
        out_specs=P(slide, seq, None),
        check_vma=False,
    )
```

```python
import jax
import jax.numpy as jnp
from jax import lax
from jax.experimental import pallas as pl
from jax.experimental.pallas import tpu as pltpu
from jax.sharding import Mesh, PartitionSpec as P

HEADS = 16
HEAD_DIM = 48
D = 768
D_ENC = 1536
HALF = 64
TILE_DEV = 192
CHUNK = 64
SEQ_LEN = 4096
WINDOW = 320
KEY_SLOTS = 80
SLOTS = 48
LANES = 128
W_ROWS = 48
P_ROWS = 24
PLANES = 16
PLANE = ("y", "x")
SEQ = ("y", "x", "zhi")
EVERY = ("zlo", "core", "y", "x", "zhi")
NORM_EPS = 1e-06
BIG_NEGATIVE = -1e30
SCALE = HEAD_DIM**-0.5
BF16 = jnp.bfloat16
F32 = jnp.float32
I32 = jnp.int32
VMEM_LIMIT = 24 * 1024 * 1024

CORE, HIGH, PLANE_ID, RATE, SEGMENT = range(5)
START_ME, COUNT_ME, START_OTHER, COUNT_OTHER, PAIR_START, PAIR_COUNT = range(5, 11)
ALL_STARTS = 16
ALL_COUNTS = 32


def dot_nn(a, b):
    return lax.dot_general(a, b, (((1,), (0,)), ((), ())), preferred_element_type=F32)


def dot_nt(a, b):
    return lax.dot_general(a, b, (((1,), (1,)), ((), ())), preferred_element_type=F32)


def dot_tn(a, b):
    return lax.dot_general(a, b, (((0,), (0,)), ((), ())), preferred_element_type=F32)


def iota(shape, dim):
    return lax.broadcasted_iota(I32, shape, dim)


def call(kernel, name, out_shape, specs, scratch, flops, size, exps=0):
    vmem = pl.BlockSpec(memory_space=pltpu.VMEM)
    smem = pl.BlockSpec(memory_space=pltpu.SMEM)
    hbm = pl.BlockSpec(memory_space=pl.ANY)
    kinds = {"s": smem, "v": vmem, "h": hbm}
    ins, outs = specs.split("-")
    return pl.pallas_call(
        kernel,
        out_shape=tuple(jax.ShapeDtypeStruct(shape, dtype) for shape, dtype in out_shape),
        in_specs=[kinds[c] for c in ins],
        out_specs=tuple(kinds[c] for c in outs),
        scratch_shapes=scratch,
        compiler_params=pltpu.CompilerParams(vmem_limit_bytes=VMEM_LIMIT),
        cost_estimate=pl.CostEstimate(flops=flops, bytes_accessed=size, transcendentals=exps),
        name=name,
    )


def prepare_kernel(place, counts, dilation, ctx, res, listing, own_ctx, own_res, table):
    table[CORE], table[HIGH], table[PLANE_ID] = place[0], place[1], place[2]
    table[RATE], table[SEGMENT] = dilation[0, 1], dilation[0, 0]
    high = place[1]
    start = jnp.int32(0)
    for p in range(PLANES):
        first, second = counts[0, 2 * p], counts[0, 2 * p + 1]
        table[ALL_STARTS + p] = start
        table[ALL_COUNTS + p] = first + second

        @pl.when(place[2] == p)
        def _(first=first, second=second, start=start):
            table[PAIR_START] = start
            table[PAIR_COUNT] = first + second
            table[COUNT_ME] = jnp.where(high == 0, first, second)
            table[COUNT_OTHER] = jnp.where(high == 0, second, first)
            table[START_ME] = jnp.where(high == 0, start, start + first)
            table[START_OTHER] = jnp.where(high == 0, start + first, start)

        start = start + first + second
    order = (iota((TILE_DEV, TILE_DEV), 0) == listing[0]).astype(BF16)
    own_ctx[...] = dot_tn(order, ctx[0]).astype(BF16)
    own_res[...] = dot_tn(order, res[0]).astype(BF16)


def prepare(*args):
    rows = ((TILE_DEV, D_ENC), BF16)
    shapes = (rows, rows, ((ALL_COUNTS + PLANES,), I32))
    return call(prepare_kernel, "prepare_rows", shapes, "sssvvv-vvs", [], 250_000_000, 2_400_000)(*args)


def halves(table, ref, width):
    core = table[CORE]
    first = ref[:, pl.ds(pl.multiple_of(core * width, LANES), width)]
    second = ref[:, pl.ds(pl.multiple_of((1 - core) * width, LANES), width)]
    return first, second


def block_loads(core, own, other, to, sems):
    loads = []
    for block in range(PLANES):
        turned = block % 4 * 4 + block // 4
        at_own = jnp.where(core == 0, block, turned)
        at_other = jnp.where(core == 0, turned, block)
        for n, (source, half, at) in enumerate(((own, core, at_own), (other, 1 - core, at_other))):
            loads.append(pltpu.make_async_copy(source.at[at], to.at[half, block], sems.at[n, block]))
    for load in loads:
        load.start()
    return loads


def hidden_kernel(table, ctx, res, own, other, normed, w, hidden, sems):
    loads = block_loads(table[CORE], own, other, w, sems)
    total = jnp.zeros((TILE_DEV, 1), F32)
    width = D // 2
    group = PLANES // 4
    for n in range(4):
        for load in loads[2 * group * n : 2 * group * (n + 1)]:
            load.wait()
        columns = slice(n * width, (n + 1) * width)
        part = res[:, columns].astype(F32)
        for half in range(2):
            rows = w[half, n * group : (n + 1) * group].reshape(width, D)
            part += dot_nt(ctx[:, half * D : (half + 1) * D], rows)
        hidden[:, columns] = part
        total += jnp.sum(part, axis=1, keepdims=True)
    center = hidden[...] - total / D_ENC
    spread = jnp.sum(center * center, axis=1, keepdims=True) / D_ENC
    normed[...] = (center * lax.rsqrt(spread + NORM_EPS)).astype(BF16)


def hidden_rows(*args):
    scratch = [
        pltpu.VMEM((2, PLANES, 2 * W_ROWS, D), BF16),
        pltpu.VMEM((TILE_DEV, D_ENC), F32),
        pltpu.SemaphoreType.DMA((2, PLANES)),
    ]
    shapes = (((TILE_DEV, D_ENC), BF16),)
    return call(hidden_kernel, "hidden_rows", shapes, "svvhh-v", scratch, 900_000_000, 6_000_000)(*args)[0]


def embed_kernel(table, normed, own, other, out, lower, upper, p, sems):
    for load in block_loads(table[CORE], own, other, p, sems):
        load.wait()
    out[...] = (dot_nt(normed[:, :D], p[0].reshape(D, D)) + dot_nt(normed[:, D:], p[1].reshape(D, D))).astype(BF16)
    lower[...] = out[:CHUNK]
    upper[...] = out[CHUNK:]


def embed(*args):
    scratch = [pltpu.VMEM((2, PLANES, 2 * P_ROWS, D), BF16), pltpu.SemaphoreType.DMA((2, PLANES))]
    shapes = (((TILE_DEV, D), BF16), ((CHUNK, D), BF16), ((TILE_DEV - CHUNK, D), BF16))
    return call(embed_kernel, "embed_rows", shapes, "svhh-vvv", scratch, 500_000_000, 3_000_000)(*args)


def key_picks(table, h, first, count):
    rate, base = table[RATE], table[PAIR_START]
    lane = iota((KEY_SLOTS, TILE_DEV), 1)
    place = iota((KEY_SLOTS, TILE_DEV), 0) * rate + ((h - base) & (rate - 1)) + (base - first)
    return ((lane == place) & (lane < count)).astype(BF16)


def key_rows(kv, h):
    rest = jnp.zeros((LANES - 2 * HEAD_DIM, TILE_DEV), BF16)
    return jnp.concatenate([kv[head_rows(h)], kv[head_rows(HEADS + h)], rest], axis=0)


def head_rows(h):
    return slice(h * HEAD_DIM, (h + 1) * HEAD_DIM)


def segments(table, position):
    length = jnp.full((1, 1), table[SEGMENT], I32).astype(F32)
    return jnp.floor((position.astype(F32) + 0.5) / length)


def own_kernel(table, own, q_a, q_b, payload, q_out, kv_out, out_sum, out_best, out_total):
    rate, start_me, count_me = table[RATE], table[START_ME], table[COUNT_ME]
    first, second = halves(table, own, D // 2)
    q_out[...] = (dot_nt(q_a[:D], first) + dot_nt(q_b[:D], second)).astype(BF16)
    kv_out[...] = (dot_nt(q_a[D:], first) + dot_nt(q_b[D:], second)).astype(BF16)
    slot = iota((SLOTS, TILE_DEV), 0) * rate
    lane = iota((SLOTS, TILE_DEV), 1)
    rest = jnp.zeros((LANES - HEAD_DIM, TILE_DEV), BF16)
    for h in range(HEADS):
        payload[h, :KEY_SLOTS] = dot_nt(key_picks(table, h, start_me, count_me), key_rows(kv_out, h)).astype(BF16)
        pick = (lane == slot + ((h - start_me) & (rate - 1))).astype(BF16)
        ask = jnp.concatenate([q_out[head_rows(h)], rest], axis=0)
        payload[h, KEY_SLOTS:] = dot_nt(pick, ask).astype(BF16)
    key_at = iota((TILE_DEV, 1), 0)
    key_seg = jnp.where(key_at < count_me, segments(table, start_me + key_at), -1.0)
    allowed = key_seg == segments(table, start_me + iota((1, TILE_DEV), 1))
    for h in range(HEADS):
        rows = head_rows(h)
        scores = jnp.where(allowed, dot_tn(kv_out[rows], q_out[rows]) * SCALE, BIG_NEGATIVE)
        best = jnp.max(scores, axis=0, keepdims=True)
        weights = jnp.exp(scores - best)
        out_best[h : h + 1] = best
        out_total[h : h + 1] = jnp.sum(weights, axis=0, keepdims=True)
        out_sum[rows] = dot_nn(kv_out[head_rows(HEADS + h)], weights.astype(BF16))


def own_rows(*args):
    stat = ((HEADS, TILE_DEV), F32)
    pay = ((HEADS, KEY_SLOTS + SLOTS, LANES), BF16)
    shapes = (pay, ((D, TILE_DEV), BF16), ((2 * D, TILE_DEV), BF16), ((D, TILE_DEV), F32), stat, stat)
    return call(own_kernel, "own_rows", shapes, "svvv-vvvvvv", [], 1_000_000_000, 5_000_000, 600_000)(*args)


def pair_kernel(table, lower, upper, q_a, q_b, own_payload, payload, rim, kv, partner):
    partner[:CHUNK] = lower[...]
    partner[CHUNK:] = upper[...]
    first, second = halves(table, partner, D // 2)
    kv[...] = (dot_nt(q_a[D:], first) + dot_nt(q_b[D:], second)).astype(BF16)
    for h in range(HEADS):
        picks = key_picks(table, h, table[START_OTHER], table[COUNT_OTHER])
        both = dot_nt(picks, key_rows(kv, h)) + own_payload[h, :KEY_SLOTS].astype(F32)
        payload[h, :KEY_SLOTS] = both.astype(BF16)
        payload[h, KEY_SLOTS:] = own_payload[h, KEY_SLOTS:]
    rim_first = jnp.where(table[HIGH] == 0, 0, table[COUNT_OTHER] - HALF)
    pick = (iota((TILE_DEV, HALF), 0) == iota((TILE_DEV, HALF), 1) + rim_first).astype(BF16)
    rim[...] = dot_nn(kv[...], pick).astype(BF16)


def pair_rows(*args):
    shapes = (((HEADS, KEY_SLOTS + SLOTS, LANES), BF16), ((2 * D, HALF), BF16))
    scratch = [pltpu.VMEM((2 * D, TILE_DEV), BF16), pltpu.VMEM((TILE_DEV, D), BF16)]
    return call(pair_kernel, "pair_rows", shapes, "svvvvv-vv", scratch, 700_000_000, 4_000_000)(*args)


def rim_kernel(table, q, near_rim, halo, q_a, q_b, own_sum, own_best, own_total, out_sum, out_best, out_total, far_rim):
    start_me, end_me = table[START_ME], table[START_ME] + table[COUNT_ME]
    first, second = halves(table, halo, D // 2)
    far_rim[...] = (dot_nt(q_a[D:], first) + dot_nt(q_b[D:], second)).astype(BF16)
    query_seg = segments(table, start_me + iota((1, TILE_DEV), 1))

    def allowed(begin):
        at = begin + iota((HALF, 1), 0)
        return jnp.where((at >= 0) & (at < SEQ_LEN), segments(table, at), -1.0) == query_seg

    upper = table[HIGH] == 0
    near_ok = allowed(jnp.where(upper, end_me, start_me - HALF))
    far_ok = allowed(jnp.where(upper, start_me - HALF, end_me))
    for h in range(HEADS):
        rows, v_rows = head_rows(h), head_rows(HEADS + h)
        near = jnp.where(near_ok, dot_tn(near_rim[rows], q[rows]) * SCALE, BIG_NEGATIVE)
        far = jnp.where(far_ok, dot_tn(far_rim[rows], q[rows]) * SCALE, BIG_NEGATIVE)
        best_o = own_best[h : h + 1]
        best = jnp.maximum(jnp.max(jnp.maximum(near, far), axis=0, keepdims=True), best_o)
        near, far, scale = jnp.exp(near - best), jnp.exp(far - best), jnp.exp(best_o - best)
        out_best[h : h + 1] = best
        out_total[h : h + 1] = jnp.sum(near + far, axis=0, keepdims=True) + scale * own_total[h : h + 1]
        summed = dot_nn(near_rim[v_rows], near.astype(BF16)) + dot_nn(far_rim[v_rows], far.astype(BF16))
        out_sum[rows] = summed + scale * own_sum[rows]


def rim_rows(*args):
    stat = ((HEADS, TILE_DEV), F32)
    shapes = (((D, TILE_DEV), F32), stat, stat)
    scratch = [pltpu.VMEM((2 * D, HALF), BF16)]
    return call(rim_kernel, "rim_rows", shapes, "svvvvvvvv-vvv", scratch, 400_000_000, 5_000_000, 400_000)(*args)


def far_kernel(table, arrived, answer, scores):
    rate = table[RATE]
    kv = arrived[:, :KEY_SLOTS].reshape(PLANES * KEY_SLOTS, LANES)
    group = 8
    width = group * SLOTS
    slot = iota((KEY_SLOTS, width), 0) * rate
    for n in range(PLANES // group):
        asks = arrived[n * group : (n + 1) * group, KEY_SLOTS:].reshape(width, LANES)
        best = jnp.full((1, width), BIG_NEGATIVE, F32)
        for p in range(PLANES):
            phase = (table[PLANE_ID] - table[ALL_STARTS + p]) & (rate - 1)
            piece = dot_nt(arrived[p, :KEY_SLOTS], asks) * SCALE
            piece = jnp.where(slot + phase < table[ALL_COUNTS + p], piece, BIG_NEGATIVE)
            scores[p * KEY_SLOTS : (p + 1) * KEY_SLOTS] = piece
            best = jnp.maximum(best, jnp.max(piece, axis=0, keepdims=True))
        weights = jnp.exp(scores[...] - best)
        total = jnp.sum(weights, axis=0, keepdims=True)
        summed = dot_tn(kv, weights.astype(BF16))
        shared = summed[HEAD_DIM : 2 * HEAD_DIM] / total
        log_all = best + jnp.log(total)
        log_a = log_all.astype(BF16).astype(F32)
        log_b = (log_all - log_a).astype(BF16).astype(F32)
        log_c = log_all - log_a - log_b
        row = iota((LANES - HEAD_DIM, width), 0)
        tail = jnp.where(row == 0, log_a, jnp.where(row == 1, log_b, jnp.where(row == 2, log_c, 0.0)))
        block = jnp.concatenate([shared, tail], axis=0)
        answer[n * group : (n + 1) * group] = block.T.astype(BF16).reshape(group, SLOTS, LANES)


def far_branch(*args):
    shapes = (((PLANES, SLOTS, LANES), BF16),)
    scratch = [pltpu.VMEM((PLANES * KEY_SLOTS, PLANES // 2 * SLOTS), F32)]
    return call(far_kernel, "far_branch", shapes, "sv-v", scratch, 500_000_000, 1_000_000, 1_000_000)(*args)[0]


def finish_kernel(table, answers, local_sum, local_best, local_total, listing, out, attended):
    rate = table[RATE]
    slot = iota((SLOTS, TILE_DEV), 0) * rate
    lane = iota((SLOTS, TILE_DEV), 1)
    row = iota((1, TILE_DEV), 1)
    live = row < table[COUNT_ME]
    for h in range(HEADS):
        rows = slice(h * HEAD_DIM, (h + 1) * HEAD_DIM)
        phase = (h - table[START_ME]) & (rate - 1)
        pick = (lane == slot + phase).astype(BF16)
        wide = dot_tn(answers[h], pick)
        log_all = wide[HEAD_DIM : HEAD_DIM + 1] + wide[HEAD_DIM + 1 : HEAD_DIM + 2] + wide[HEAD_DIM + 2 : HEAD_DIM + 3]
        log_all = jnp.where((row & (rate - 1)) == phase, log_all, BIG_NEGATIVE)
        best = local_best[h : h + 1]
        joint = jnp.maximum(best, log_all)
        near = jnp.exp(best - joint)
        far = jnp.exp(log_all - joint)
        below = jnp.where(live, near * local_total[h : h + 1] + far, 1.0)
        mixed = (near * local_sum[rows] + far * wide[:HEAD_DIM]) / below
        attended[rows] = jnp.where(live, mixed, 0.0).astype(BF16)
    back = (listing[0] == iota((TILE_DEV, TILE_DEV), 0)).astype(BF16)
    out[0] = dot_nt(back, attended[...]).astype(BF16)


def finish(*args):
    shapes = (((1, TILE_DEV, D), BF16),)
    scratch = [pltpu.VMEM((D, TILE_DEV), BF16)]
    return call(finish_kernel, "finish_rows", shapes, "svvvvv-v", scratch, 100_000_000, 1_500_000, 10_000)(*args)[0]


def mirrored(x):
    z_low = lax.axis_size("zlo")
    pairs = [
        (low * 2 + high, (z_low - 1 - low) * 2 + (1 - high))
        for low in range(z_low)
        for high in range(2)
    ]
    return lax.ppermute(x, ("zlo", "zhi"), pairs)


def along_z(x, part):
    z_low = lax.axis_size("zlo")

    def rank(z, core):
        return (z % z_low * 2 + core) * 2 + z // z_low

    half = z_low // 2 if part == 0 else z_low - z_low // 2
    pairs = []
    for z in range(2 * z_low):
        for core in range(2):
            step = half if core == 0 else -half
            pairs.append((rank(z, core), rank((z + step) % (2 * z_low), core)))
    return lax.ppermute(x, ("zlo", "core", "zhi"), pairs)


def other_core(x):
    return lax.ppermute(x, "core", [(0, 1), (1, 0)])


def over_plane(x):
    return lax.all_to_all(x, PLANE, 0, 0)


def hold(*values):
    return lax.optimization_barrier(values)


def copies(x):
    return jnp.broadcast_to(x[None], (PLANES,) + x.shape)


def along_lines(x, stage):
    groups = []
    for low in range(lax.axis_size("zlo")):
        for core in range(2):
            for high in range(2):
                for line in range(4):
                    across_x = (core == 0) == (stage == 0)
                    plane = [line * 4 + k if across_x else k * 4 + line for k in range(4)]
                    groups.append([((low * 2 + core) * PLANES + p) * 2 + high for p in plane])
    spread = jnp.broadcast_to(x[None], (4,) + x.shape)
    return lax.all_to_all(spread, EVERY, 0, 0, axis_index_groups=groups)


def in_order(own, other, high):
    return jnp.where(high == 0, jnp.concatenate([own, other]), jnp.concatenate([other, own]))


def on_device(ctx_in, resid, enc_out_w, slide_proj, qkv_w, tissue, kept_count, dilation):
    core = lax.axis_index("core")
    high = lax.axis_index("zhi")
    plane_id = lax.axis_index("y") * lax.axis_size("x") + lax.axis_index("x")

    w_own = lax.dynamic_slice_in_dim(enc_out_w, core * D, D, 0).T
    p_own = lax.dynamic_slice_in_dim(slide_proj, core * D, D, 0).T
    q_own = lax.dynamic_slice_in_dim(qkv_w, core * (D // 2), D // 2, 0).T
    other_wp = mirrored(jnp.concatenate([w_own, p_own]))
    q_other = mirrored(q_own)
    place = jnp.stack([core, high, plane_id]).astype(I32)
    own_ctx, own_res, table = prepare(place, kept_count, dilation, ctx_in, resid, tissue)
    wp = jnp.concatenate(
        [in_order(w_own, other_wp[:W_ROWS], high), in_order(p_own, other_wp[W_ROWS:], high)]
    )
    lines = along_lines(wp, 0)
    w_lines, p_lines = lines[:, : 2 * W_ROWS].reshape(-1, D), lines[:, 2 * W_ROWS :].reshape(-1, D)
    w_all = along_lines(w_lines, 1).reshape(PLANES, -1, D)
    w_all, p_lines = hold(w_all, p_lines)
    p_all = along_lines(p_lines, 1).reshape(PLANES, -1, D)
    normed = hidden_rows(table, own_ctx, own_res, w_all, other_core(w_all))
    p_all, normed, q_both = hold(p_all, normed, copies(in_order(q_own, q_other, high)))
    q_a = over_plane(q_both)
    embedded, lower, upper = embed(table, normed, p_all, other_core(p_all))
    lower = along_z(along_z(lower, 0), 1)
    upper = along_z(upper, 0)
    q_a, embedded, lower, upper = hold(q_a, embedded, lower, upper)
    q_a = q_a.reshape(3 * D, D // 2)
    q_b = other_core(q_a)
    upper = along_z(upper, 1)
    own_payload, q_rows, _, own_sum, own_best, own_total = own_rows(table, embedded, q_a, q_b)
    upper, own_payload = hold(upper, own_payload)
    rim_from = jnp.where(high == 0, table[COUNT_OTHER] - HALF, 0)
    rim = lax.dynamic_slice_in_dim(jnp.concatenate([lower, upper]), rim_from, HALF, 0)
    halo_pairs = [(p * 2, p * 2 + 2) for p in range(PLANES - 1)]
    halo_pairs += [(p * 2 + 1, p * 2 - 1) for p in range(1, PLANES)]
    halo = lax.ppermute(rim, SEQ, halo_pairs)
    payload, near_rim = pair_rows(table, lower, upper, q_a, q_b, own_payload)
    arrived, halo = hold(lax.all_to_all(payload, PLANE, 0, 0), halo)
    local_sum, local_best, local_total = rim_rows(
        table, q_rows, near_rim, halo, q_a, q_b, own_sum, own_best, own_total
    )
    answer = far_branch(table, arrived)
    answers = lax.all_to_all(answer, PLANE, 0, 0)
    return finish(table, answers, local_sum, local_best, local_total, tissue)


def solution(mesh):
    devices = mesh.devices.reshape(-1, 2, 4, 4, 2)
    split = Mesh(devices, ("zlo", "core", "y", "x", "zhi"))
    slide, seq = ("zlo", "core"), ("y", "x", "zhi")
    return jax.shard_map(
        on_device,
        mesh=split,
        in_specs=(
            P(slide, seq, None),
            P(slide, seq, None),
            P(None, seq),
            P(None, seq),
            P(None, seq),
            P(slide, seq, None),
            P(slide, None),
            P(slide, None),
        ),
        out_specs=P(slide, seq, None),
        check_vma=False,
    )
```

```python
import jax
import jax.numpy as jnp
from jax import lax
from jax.experimental import pallas as pl
from jax.experimental.pallas import tpu as pltpu
from jax.sharding import Mesh, PartitionSpec as P

HEADS = 16
HEAD_DIM = 48
D = 768
D_ENC = 1536
HALF = 64
TILE_DEV = 192
CHUNK = 64
SEQ_LEN = 4096
WINDOW = 320
KEY_SLOTS = 80
SLOTS = 48
LANES = 128
W_ROWS = 48
P_ROWS = 24
PLANES = 16
PLANE = ("y", "x")
SEQ = ("y", "x", "zhi")
EVERY = ("zlo", "core", "y", "x", "zhi")
NORM_EPS = 1e-06
BIG_NEGATIVE = -1e30
SCALE = HEAD_DIM**-0.5
BF16 = jnp.bfloat16
F32 = jnp.float32
I32 = jnp.int32
VMEM_LIMIT = 24 * 1024 * 1024

CORE, HIGH, PLANE_ID, RATE, SEGMENT = range(5)
START_ME, COUNT_ME, START_OTHER, COUNT_OTHER, PAIR_START, PAIR_COUNT = range(5, 11)
ALL_STARTS = 16
ALL_COUNTS = 32


def dot_nn(a, b):
    return lax.dot_general(a, b, (((1,), (0,)), ((), ())), preferred_element_type=F32)


def dot_nt(a, b):
    return lax.dot_general(a, b, (((1,), (1,)), ((), ())), preferred_element_type=F32)


def dot_tn(a, b):
    return lax.dot_general(a, b, (((0,), (0,)), ((), ())), preferred_element_type=F32)


def iota(shape, dim):
    return lax.broadcasted_iota(I32, shape, dim)


def call(kernel, name, out_shape, specs, scratch, flops, size, exps=0):
    vmem = pl.BlockSpec(memory_space=pltpu.VMEM)
    smem = pl.BlockSpec(memory_space=pltpu.SMEM)
    hbm = pl.BlockSpec(memory_space=pl.ANY)
    kinds = {"s": smem, "v": vmem, "h": hbm}
    ins, outs = specs.split("-")
    return pl.pallas_call(
        kernel,
        out_shape=tuple(jax.ShapeDtypeStruct(shape, dtype) for shape, dtype in out_shape),
        in_specs=[kinds[c] for c in ins],
        out_specs=tuple(kinds[c] for c in outs),
        scratch_shapes=scratch,
        compiler_params=pltpu.CompilerParams(vmem_limit_bytes=VMEM_LIMIT),
        cost_estimate=pl.CostEstimate(flops=flops, bytes_accessed=size, transcendentals=exps),
        name=name,
    )


def prepare_kernel(place, counts, dilation, ctx, res, listing, own_ctx, own_res, table):
    table[CORE], table[HIGH], table[PLANE_ID] = place[0], place[1], place[2]
    table[RATE], table[SEGMENT] = dilation[0, 1], dilation[0, 0]
    high = place[1]
    start = jnp.int32(0)
    for p in range(PLANES):
        first, second = counts[0, 2 * p], counts[0, 2 * p + 1]
        table[ALL_STARTS + p] = start
        table[ALL_COUNTS + p] = first + second

        @pl.when(place[2] == p)
        def _(first=first, second=second, start=start):
            table[PAIR_START] = start
            table[PAIR_COUNT] = first + second
            table[COUNT_ME] = jnp.where(high == 0, first, second)
            table[COUNT_OTHER] = jnp.where(high == 0, second, first)
            table[START_ME] = jnp.where(high == 0, start, start + first)
            table[START_OTHER] = jnp.where(high == 0, start + first, start)

        start = start + first + second
    order = (iota((TILE_DEV, TILE_DEV), 0) == listing[0]).astype(BF16)
    own_ctx[...] = dot_tn(order, ctx[0]).astype(BF16)
    own_res[...] = dot_tn(order, res[0]).astype(BF16)


def prepare(*args):
    rows = ((TILE_DEV, D_ENC), BF16)
    shapes = (rows, rows, ((ALL_COUNTS + PLANES,), I32))
    return call(prepare_kernel, "prepare_rows", shapes, "sssvvv-vvs", [], 250_000_000, 2_400_000)(*args)


def halves(table, ref, width):
    core = table[CORE]
    first = ref[:, pl.ds(pl.multiple_of(core * width, LANES), width)]
    second = ref[:, pl.ds(pl.multiple_of((1 - core) * width, LANES), width)]
    return first, second


def embed_kernel(table, ctx, res, own, other, out, lower, upper, w, p, hidden, normed, sems):
    core = table[CORE]
    w_loads, p_loads = [], []
    for block in range(PLANES):
        turned = block % 4 * 4 + block // 4
        at_own = jnp.where(core == 0, block, turned)
        at_other = jnp.where(core == 0, turned, block)
        for n, (source, half, at) in enumerate(((own, core, at_own), (other, 1 - core, at_other))):
            w_loads.append(
                pltpu.make_async_copy(source.at[at, : 2 * W_ROWS], w.at[half, block], sems.at[0, n, block])
            )
            p_loads.append(
                pltpu.make_async_copy(source.at[at, 2 * W_ROWS :], p.at[half, block], sems.at[1, n, block])
            )
    for load in w_loads + p_loads:
        load.start()
    total = jnp.zeros((TILE_DEV, 1), F32)
    width = D // 2
    group = PLANES // 4
    for n in range(4):
        for load in w_loads[2 * group * n : 2 * group * (n + 1)]:
            load.wait()
        columns = slice(n * width, (n + 1) * width)
        part = res[:, columns].astype(F32)
        for half in range(2):
            rows = w[half, n * group : (n + 1) * group].reshape(width, D)
            part += dot_nt(ctx[:, half * D : (half + 1) * D], rows)
        hidden[:, columns] = part
        total += jnp.sum(part, axis=1, keepdims=True)
    center = hidden[...] - total / D_ENC
    spread = jnp.sum(center * center, axis=1, keepdims=True) / D_ENC
    normed[...] = (center * lax.rsqrt(spread + NORM_EPS)).astype(BF16)
    for load in p_loads:
        load.wait()
    out[...] = (dot_nt(normed[:, :D], p[0].reshape(D, D)) + dot_nt(normed[:, D:], p[1].reshape(D, D))).astype(BF16)
    pass_first = jnp.where(table[HIGH] == 0, 0, table[COUNT_ME] - CHUNK)
    pick = (iota((CHUNK, TILE_DEV), 1) == iota((CHUNK, TILE_DEV), 0) + pass_first).astype(BF16)
    lower[...] = dot_nn(pick, out[...]).astype(BF16)

    @pl.when(table[HIGH] == 0)
    def _():
        upper[...] = out[CHUNK:]

    @pl.when(table[HIGH] != 0)
    def _():
        upper[...] = out[: TILE_DEV - CHUNK]


def embed(*args):
    scratch = [
        pltpu.VMEM((2, PLANES, 2 * W_ROWS, D), BF16),
        pltpu.VMEM((2, PLANES, 2 * P_ROWS, D), BF16),
        pltpu.VMEM((TILE_DEV, D_ENC), F32),
        pltpu.VMEM((TILE_DEV, D_ENC), BF16),
        pltpu.SemaphoreType.DMA((2, 2, PLANES)),
    ]
    shapes = (((TILE_DEV, D), BF16), ((CHUNK, D), BF16), ((TILE_DEV - CHUNK, D), BF16))
    return call(embed_kernel, "embed_rows", shapes, "svvhh-vvv", scratch, 1_400_000_000, 9_000_000)(*args)


def key_picks(table, h, first, block_rows):
    rate, base = table[RATE], table[PAIR_START]
    place = iota((KEY_SLOTS, TILE_DEV), 0) * rate + ((h - base) & (rate - 1)) + (base - first)
    return (block_rows == place).astype(BF16)


def live_rows(rows, lane, count):
    return jnp.where(lane < count, rows, -SEQ_LEN)


def key_rows(kv, h):
    rest = jnp.zeros((LANES - 2 * HEAD_DIM, TILE_DEV), BF16)
    return jnp.concatenate([kv[head_rows(h)], kv[head_rows(HEADS + h)], rest], axis=0)


def head_rows(h):
    return slice(h * HEAD_DIM, (h + 1) * HEAD_DIM)


def segments(table, position):
    length = jnp.full((1, 1), table[SEGMENT], I32).astype(F32)
    return jnp.floor((position.astype(F32) + 0.5) / length)


def own_kernel(table, own, q_a, q_b, payload, q_out, kv_out, out_sum, out_best, out_total):
    rate, start_me, count_me = table[RATE], table[START_ME], table[COUNT_ME]
    first, second = halves(table, own, D // 2)
    q_out[...] = (dot_nt(q_a[:D], first) + dot_nt(q_b[:D], second)).astype(BF16)
    kv_out[...] = (dot_nt(q_a[D:], first) + dot_nt(q_b[D:], second)).astype(BF16)
    slot = iota((SLOTS, TILE_DEV), 0) * rate
    lane = iota((SLOTS, TILE_DEV), 1)
    rest = jnp.zeros((LANES - HEAD_DIM, TILE_DEV), BF16)
    wide_lane = iota((KEY_SLOTS, TILE_DEV), 1)
    block_rows = live_rows(wide_lane, wide_lane, count_me)
    for h in range(HEADS):
        payload[h, :KEY_SLOTS] = dot_nt(key_picks(table, h, start_me, block_rows), key_rows(kv_out, h)).astype(BF16)
        pick = (lane == slot + ((h - start_me) & (rate - 1))).astype(BF16)
        ask = jnp.concatenate([q_out[head_rows(h)], rest], axis=0)
        payload[h, KEY_SLOTS:] = dot_nt(pick, ask).astype(BF16)
    key_at = iota((TILE_DEV, 1), 0)
    key_seg = jnp.where(key_at < count_me, segments(table, start_me + key_at), -1.0)
    allowed = key_seg == segments(table, start_me + iota((1, TILE_DEV), 1))
    for h in range(HEADS):
        rows = head_rows(h)
        scores = jnp.where(allowed, dot_tn(kv_out[rows], q_out[rows]) * SCALE, BIG_NEGATIVE)
        best = jnp.max(scores, axis=0, keepdims=True)
        weights = jnp.exp(scores - best)
        out_best[h : h + 1] = best
        out_total[h : h + 1] = jnp.sum(weights, axis=0, keepdims=True)
        out_sum[rows] = dot_nn(kv_out[head_rows(HEADS + h)], weights.astype(BF16))


def own_rows(*args):
    stat = ((HEADS, TILE_DEV), F32)
    pay = ((HEADS, KEY_SLOTS + SLOTS, LANES), BF16)
    shapes = (pay, ((D, TILE_DEV), BF16), ((2 * D, TILE_DEV), BF16), ((D, TILE_DEV), F32), stat, stat)
    return call(own_kernel, "own_rows", shapes, "svvv-vvvvvv", [], 1_000_000_000, 5_000_000, 600_000)(*args)


def pair_kernel(table, lower, upper, q_a, q_b, own_payload, payload, rim, kv, partner):
    partner[:CHUNK] = lower[...]
    partner[CHUNK:] = upper[...]
    first, second = halves(table, partner, D // 2)
    kv[...] = (dot_nt(q_a[D:], first) + dot_nt(q_b[D:], second)).astype(BF16)
    count, upward = table[COUNT_OTHER], table[HIGH] == 0
    lane = iota((KEY_SLOTS, TILE_DEV), 1)
    turned = jnp.where(lane < CHUNK, lane + (count - CHUNK), lane - CHUNK)
    block_rows = live_rows(jnp.where(upward, turned, lane), lane, count)
    for h in range(HEADS):
        picks = key_picks(table, h, table[START_OTHER], block_rows)
        both = dot_nt(picks, key_rows(kv, h)) + own_payload[h, :KEY_SLOTS].astype(F32)
        payload[h, :KEY_SLOTS] = both.astype(BF16)
        payload[h, KEY_SLOTS:] = own_payload[h, KEY_SLOTS:]
    rim_first = jnp.where(upward, CHUNK, count - HALF)
    pick = (iota((TILE_DEV, HALF), 0) == iota((TILE_DEV, HALF), 1) + rim_first).astype(BF16)
    rim[...] = dot_nn(kv[...], pick).astype(BF16)


def pair_rows(*args):
    shapes = (((HEADS, KEY_SLOTS + SLOTS, LANES), BF16), ((2 * D, HALF), BF16))
    scratch = [pltpu.VMEM((2 * D, TILE_DEV), BF16), pltpu.VMEM((TILE_DEV, D), BF16)]
    return call(pair_kernel, "pair_rows", shapes, "svvvvv-vv", scratch, 700_000_000, 4_000_000)(*args)


def rim_kernel(table, q, near_rim, halo, q_a, q_b, own_sum, own_best, own_total, out_sum, out_best, out_total, far_rim):
    start_me, end_me = table[START_ME], table[START_ME] + table[COUNT_ME]
    first, second = halves(table, halo, D // 2)
    far_rim[...] = (dot_nt(q_a[D:], first) + dot_nt(q_b[D:], second)).astype(BF16)
    query_seg = segments(table, start_me + iota((1, TILE_DEV), 1))

    def allowed(begin):
        at = begin + iota((HALF, 1), 0)
        return jnp.where((at >= 0) & (at < SEQ_LEN), segments(table, at), -1.0) == query_seg

    upper = table[HIGH] == 0
    near_ok = allowed(jnp.where(upper, end_me, start_me - HALF))
    far_ok = allowed(jnp.where(upper, start_me - HALF, end_me))
    for h in range(HEADS):
        rows, v_rows = head_rows(h), head_rows(HEADS + h)
        near = jnp.where(near_ok, dot_tn(near_rim[rows], q[rows]) * SCALE, BIG_NEGATIVE)
        far = jnp.where(far_ok, dot_tn(far_rim[rows], q[rows]) * SCALE, BIG_NEGATIVE)
        best_o = own_best[h : h + 1]
        best = jnp.maximum(jnp.max(jnp.maximum(near, far), axis=0, keepdims=True), best_o)
        near, far, scale = jnp.exp(near - best), jnp.exp(far - best), jnp.exp(best_o - best)
        out_best[h : h + 1] = best
        out_total[h : h + 1] = jnp.sum(near + far, axis=0, keepdims=True) + scale * own_total[h : h + 1]
        summed = dot_nn(near_rim[v_rows], near.astype(BF16)) + dot_nn(far_rim[v_rows], far.astype(BF16))
        out_sum[rows] = summed + scale * own_sum[rows]


def rim_rows(*args):
    stat = ((HEADS, TILE_DEV), F32)
    shapes = (((D, TILE_DEV), F32), stat, stat)
    scratch = [pltpu.VMEM((2 * D, HALF), BF16)]
    return call(rim_kernel, "rim_rows", shapes, "svvvvvvvv-vvv", scratch, 400_000_000, 5_000_000, 400_000)(*args)


def far_kernel(table, arrived, answer, scores):
    rate = table[RATE]
    kv = arrived[:, :KEY_SLOTS].reshape(PLANES * KEY_SLOTS, LANES)
    group = 8
    width = group * SLOTS
    slot = iota((KEY_SLOTS, width), 0) * rate
    for n in range(PLANES // group):
        asks = arrived[n * group : (n + 1) * group, KEY_SLOTS:].reshape(width, LANES)
        best = jnp.full((1, width), BIG_NEGATIVE, F32)
        for p in range(PLANES):
            phase = (table[PLANE_ID] - table[ALL_STARTS + p]) & (rate - 1)
            piece = dot_nt(arrived[p, :KEY_SLOTS], asks) * SCALE
            piece = jnp.where(slot + phase < table[ALL_COUNTS + p], piece, BIG_NEGATIVE)
            scores[p * KEY_SLOTS : (p + 1) * KEY_SLOTS] = piece
            best = jnp.maximum(best, jnp.max(piece, axis=0, keepdims=True))
        weights = jnp.exp(scores[...] - best)
        total = jnp.sum(weights, axis=0, keepdims=True)
        summed = dot_tn(kv, weights.astype(BF16))
        shared = summed[HEAD_DIM : 2 * HEAD_DIM] / total
        log_all = best + jnp.log(total)
        log_a = log_all.astype(BF16).astype(F32)
        log_b = (log_all - log_a).astype(BF16).astype(F32)
        log_c = log_all - log_a - log_b
        row = iota((LANES - HEAD_DIM, width), 0)
        tail = jnp.where(row == 0, log_a, jnp.where(row == 1, log_b, jnp.where(row == 2, log_c, 0.0)))
        block = jnp.concatenate([shared, tail], axis=0)
        answer[n * group : (n + 1) * group] = block.T.astype(BF16).reshape(group, SLOTS, LANES)


def far_branch(*args):
    shapes = (((PLANES, SLOTS, LANES), BF16),)
    scratch = [pltpu.VMEM((PLANES * KEY_SLOTS, PLANES // 2 * SLOTS), F32)]
    return call(far_kernel, "far_branch", shapes, "sv-v", scratch, 500_000_000, 1_000_000, 1_000_000)(*args)[0]


def finish_kernel(table, answers, local_sum, local_best, local_total, listing, out, attended):
    rate = table[RATE]
    slot = iota((SLOTS, TILE_DEV), 0) * rate
    lane = iota((SLOTS, TILE_DEV), 1)
    row = iota((1, TILE_DEV), 1)
    live = row < table[COUNT_ME]
    for h in range(HEADS):
        rows = slice(h * HEAD_DIM, (h + 1) * HEAD_DIM)
        phase = (h - table[START_ME]) & (rate - 1)
        pick = (lane == slot + phase).astype(BF16)
        wide = dot_tn(answers[h], pick)
        log_all = wide[HEAD_DIM : HEAD_DIM + 1] + wide[HEAD_DIM + 1 : HEAD_DIM + 2] + wide[HEAD_DIM + 2 : HEAD_DIM + 3]
        log_all = jnp.where((row & (rate - 1)) == phase, log_all, BIG_NEGATIVE)
        best = local_best[h : h + 1]
        joint = jnp.maximum(best, log_all)
        near = jnp.exp(best - joint)
        far = jnp.exp(log_all - joint)
        below = jnp.where(live, near * local_total[h : h + 1] + far, 1.0)
        mixed = (near * local_sum[rows] + far * wide[:HEAD_DIM]) / below
        attended[rows] = jnp.where(live, mixed, 0.0).astype(BF16)
    back = (listing[0] == iota((TILE_DEV, TILE_DEV), 0)).astype(BF16)
    out[0] = dot_nt(back, attended[...]).astype(BF16)


def finish(*args):
    shapes = (((1, TILE_DEV, D), BF16),)
    scratch = [pltpu.VMEM((D, TILE_DEV), BF16)]
    return call(finish_kernel, "finish_rows", shapes, "svvvvv-v", scratch, 100_000_000, 1_500_000, 10_000)(*args)[0]


def mirrored(x):
    z_low = lax.axis_size("zlo")
    pairs = [
        (low * 2 + high, (z_low - 1 - low) * 2 + (1 - high))
        for low in range(z_low)
        for high in range(2)
    ]
    return lax.ppermute(x, ("zlo", "zhi"), pairs)


def along_z(x, part):
    z_low = lax.axis_size("zlo")

    def rank(z, core):
        return (z % z_low * 2 + core) * 2 + z // z_low

    half = z_low // 2 if part == 0 else z_low - z_low // 2
    pairs = []
    for z in range(2 * z_low):
        for core in range(2):
            step = half if core == 0 else -half
            pairs.append((rank(z, core), rank((z + step) % (2 * z_low), core)))
    return lax.ppermute(x, ("zlo", "core", "zhi"), pairs)


def other_core(x):
    return lax.ppermute(x, "core", [(0, 1), (1, 0)])


def over_plane(x):
    return lax.all_to_all(x, PLANE, 0, 0)


def hold(*values):
    return lax.optimization_barrier(values)


def copies(x):
    return jnp.broadcast_to(x[None], (PLANES,) + x.shape)


def along_lines(x, stage):
    groups = []
    for low in range(lax.axis_size("zlo")):
        for core in range(2):
            for high in range(2):
                for line in range(4):
                    across_x = (core == 0) == (stage == 0)
                    plane = [line * 4 + k if across_x else k * 4 + line for k in range(4)]
                    groups.append([((low * 2 + core) * PLANES + p) * 2 + high for p in plane])
    spread = jnp.broadcast_to(x[None], (4,) + x.shape)
    return lax.all_to_all(spread, EVERY, 0, 0, axis_index_groups=groups)


def in_order(own, other, high):
    return jnp.where(high == 0, jnp.concatenate([own, other]), jnp.concatenate([other, own]))


def on_device(ctx_in, resid, enc_out_w, slide_proj, qkv_w, tissue, kept_count, dilation):
    core = lax.axis_index("core")
    high = lax.axis_index("zhi")
    plane_id = lax.axis_index("y") * lax.axis_size("x") + lax.axis_index("x")

    w_own = lax.dynamic_slice_in_dim(enc_out_w, core * D, D, 0).T
    p_own = lax.dynamic_slice_in_dim(slide_proj, core * D, D, 0).T
    q_own = lax.dynamic_slice_in_dim(qkv_w, core * (D // 2), D // 2, 0).T
    other_wp = mirrored(jnp.concatenate([w_own, p_own]))
    q_other = mirrored(q_own)
    place = jnp.stack([core, high, plane_id]).astype(I32)
    own_ctx, own_res, table = prepare(place, kept_count, dilation, ctx_in, resid, tissue)
    wp = jnp.concatenate(
        [in_order(w_own, other_wp[:W_ROWS], high), in_order(p_own, other_wp[W_ROWS:], high)]
    )
    wp = along_lines(along_lines(wp, 0).reshape(-1, D), 1).reshape(PLANES, -1, D)
    q_both = copies(in_order(q_own, q_other, high))
    wp, q_both = hold(wp, q_both)
    q_a = over_plane(q_both)
    embedded, lower, upper = embed(table, own_ctx, own_res, wp, other_core(wp))
    lower = along_z(along_z(lower, 0), 1)
    upper = along_z(upper, 0)
    q_a, embedded, lower, upper = hold(q_a, embedded, lower, upper)
    q_a = q_a.reshape(3 * D, D // 2)
    q_b = other_core(q_a)
    upper = along_z(upper, 1)
    own_payload, q_rows, _, own_sum, own_best, own_total = own_rows(table, embedded, q_a, q_b)
    halo_pairs = [(p * 2, p * 2 + 2) for p in range(PLANES - 1)]
    halo_pairs += [(p * 2 + 1, p * 2 - 1) for p in range(1, PLANES)]
    halo = lax.ppermute(lower, SEQ, halo_pairs)
    upper, own_payload, halo = hold(upper, own_payload, halo)
    payload, near_rim = pair_rows(table, lower, upper, q_a, q_b, own_payload)
    arrived = lax.all_to_all(payload, PLANE, 0, 0)
    local_sum, local_best, local_total = rim_rows(
        table, q_rows, near_rim, halo, q_a, q_b, own_sum, own_best, own_total
    )
    answer = far_branch(table, arrived)
    answers = lax.all_to_all(answer, PLANE, 0, 0)
    return finish(table, answers, local_sum, local_best, local_total, tissue)


def solution(mesh):
    devices = mesh.devices.reshape(-1, 2, 4, 4, 2)
    split = Mesh(devices, ("zlo", "core", "y", "x", "zhi"))
    slide, seq = ("zlo", "core"), ("y", "x", "zhi")
    return jax.shard_map(
        on_device,
        mesh=split,
        in_specs=(
            P(slide, seq, None),
            P(slide, seq, None),
            P(None, seq),
            P(None, seq),
            P(None, seq),
            P(slide, seq, None),
            P(slide, None),
            P(slide, None),
        ),
        out_specs=P(slide, seq, None),
        check_vma=False,
    )
```

```python
import jax
import jax.numpy as jnp
from jax import lax
from jax.experimental import pallas as pl
from jax.experimental.pallas import tpu as pltpu
from jax.sharding import Mesh, PartitionSpec as P

HEADS = 16
HEAD_DIM = 48
D = 768
D_ENC = 1536
HALF = 64
TILE_DEV = 192
CHUNK = 64
SEQ_LEN = 4096
WINDOW = 320
KEY_SLOTS = 80
SLOTS = 48
LANES = 128
W_ROWS = 48
P_ROWS = 24
PLANES = 16
PLANE = ("y", "x")
SEQ = ("y", "x", "zhi")
EVERY = ("zlo", "core", "y", "x", "zhi")
NORM_EPS = 1e-06
BIG_NEGATIVE = -1e30
SCALE = HEAD_DIM**-0.5
BF16 = jnp.bfloat16
F32 = jnp.float32
I32 = jnp.int32
VMEM_LIMIT = 24 * 1024 * 1024

CORE, HIGH, PLANE_ID, RATE, SEGMENT = range(5)
START_ME, COUNT_ME, START_OTHER, COUNT_OTHER, PAIR_START, PAIR_COUNT = range(5, 11)
ALL_STARTS = 16
ALL_COUNTS = 32


def dot_nn(a, b):
    return lax.dot_general(a, b, (((1,), (0,)), ((), ())), preferred_element_type=F32)


def dot_nt(a, b):
    return lax.dot_general(a, b, (((1,), (1,)), ((), ())), preferred_element_type=F32)


def dot_tn(a, b):
    return lax.dot_general(a, b, (((0,), (0,)), ((), ())), preferred_element_type=F32)


def iota(shape, dim):
    return lax.broadcasted_iota(I32, shape, dim)


def call(kernel, name, out_shape, specs, scratch, flops, size, exps=0):
    vmem = pl.BlockSpec(memory_space=pltpu.VMEM)
    smem = pl.BlockSpec(memory_space=pltpu.SMEM)
    hbm = pl.BlockSpec(memory_space=pl.ANY)
    kinds = {"s": smem, "v": vmem, "h": hbm}
    ins, outs = specs.split("-")
    return pl.pallas_call(
        kernel,
        out_shape=tuple(jax.ShapeDtypeStruct(shape, dtype) for shape, dtype in out_shape),
        in_specs=[kinds[c] for c in ins],
        out_specs=tuple(kinds[c] for c in outs),
        scratch_shapes=scratch,
        compiler_params=pltpu.CompilerParams(vmem_limit_bytes=VMEM_LIMIT),
        cost_estimate=pl.CostEstimate(flops=flops, bytes_accessed=size, transcendentals=exps),
        name=name,
    )


def prepare_kernel(place, counts, dilation, ctx, res, listing, own_ctx, own_res, table):
    table[CORE], table[HIGH], table[PLANE_ID] = place[0], place[1], place[2]
    table[RATE], table[SEGMENT] = dilation[0, 1], dilation[0, 0]
    high = place[1]
    start = jnp.int32(0)
    for p in range(PLANES):
        first, second = counts[0, 2 * p], counts[0, 2 * p + 1]
        table[ALL_STARTS + p] = start
        table[ALL_COUNTS + p] = first + second

        @pl.when(place[2] == p)
        def _(first=first, second=second, start=start):
            table[PAIR_START] = start
            table[PAIR_COUNT] = first + second
            table[COUNT_ME] = jnp.where(high == 0, first, second)
            table[COUNT_OTHER] = jnp.where(high == 0, second, first)
            table[START_ME] = jnp.where(high == 0, start, start + first)
            table[START_OTHER] = jnp.where(high == 0, start + first, start)

        start = start + first + second
    order = (iota((TILE_DEV, TILE_DEV), 0) == listing[0]).astype(BF16)
    own_ctx[...] = dot_tn(order, ctx[0]).astype(BF16)
    own_res[...] = dot_tn(order, res[0]).astype(BF16)


def prepare(*args):
    rows = ((TILE_DEV, D_ENC), BF16)
    shapes = (rows, rows, ((ALL_COUNTS + PLANES,), I32))
    return call(prepare_kernel, "prepare_rows", shapes, "sssvvv-vvs", [], 250_000_000, 2_400_000)(*args)


def halves(table, ref, width):
    core = table[CORE]
    first = ref[:, pl.ds(pl.multiple_of(core * width, LANES), width)]
    second = ref[:, pl.ds(pl.multiple_of((1 - core) * width, LANES), width)]
    return first, second


def embed_kernel(table, ctx, res, own, other, out, lower, upper, w, p, hidden, normed, sems):
    core = table[CORE]
    w_loads, p_loads = [], []
    for block in range(PLANES):
        turned = block % 4 * 4 + block // 4
        at_own = jnp.where(core == 0, block, turned)
        at_other = jnp.where(core == 0, turned, block)
        for n, (source, half, at) in enumerate(((own, core, at_own), (other, 1 - core, at_other))):
            w_loads.append(
                pltpu.make_async_copy(source.at[at, : 2 * W_ROWS], w.at[half, block], sems.at[0, n, block])
            )
            p_loads.append(
                pltpu.make_async_copy(source.at[at, 2 * W_ROWS :], p.at[half, block], sems.at[1, n, block])
            )
    for load in w_loads + p_loads:
        load.start()
    total = jnp.zeros((TILE_DEV, 1), F32)
    width = D // 2
    group = PLANES // 4
    for n in range(4):
        for load in w_loads[2 * group * n : 2 * group * (n + 1)]:
            load.wait()
        columns = slice(n * width, (n + 1) * width)
        part = res[:, columns].astype(F32)
        for half in range(2):
            rows = w[half, n * group : (n + 1) * group].reshape(width, D)
            part += dot_nt(ctx[:, half * D : (half + 1) * D], rows)
        hidden[:, columns] = part
        total += jnp.sum(part, axis=1, keepdims=True)
    center = hidden[...] - total / D_ENC
    spread = jnp.sum(center * center, axis=1, keepdims=True) / D_ENC
    normed[...] = (center * lax.rsqrt(spread + NORM_EPS)).astype(BF16)
    for load in p_loads:
        load.wait()
    out[...] = (dot_nt(normed[:, :D], p[0].reshape(D, D)) + dot_nt(normed[:, D:], p[1].reshape(D, D))).astype(BF16)
    pass_first = jnp.where(table[HIGH] == 0, 0, table[COUNT_ME] - CHUNK)
    pick = (iota((CHUNK, TILE_DEV), 1) == iota((CHUNK, TILE_DEV), 0) + pass_first).astype(BF16)
    lower[...] = dot_nn(pick, out[...]).astype(BF16)

    @pl.when(table[HIGH] == 0)
    def _():
        upper[...] = out[CHUNK:]

    @pl.when(table[HIGH] != 0)
    def _():
        upper[...] = out[: TILE_DEV - CHUNK]


def embed(*args):
    scratch = [
        pltpu.VMEM((2, PLANES, 2 * W_ROWS, D), BF16),
        pltpu.VMEM((2, PLANES, 2 * P_ROWS, D), BF16),
        pltpu.VMEM((TILE_DEV, D_ENC), F32),
        pltpu.VMEM((TILE_DEV, D_ENC), BF16),
        pltpu.SemaphoreType.DMA((2, 2, PLANES)),
    ]
    shapes = (((TILE_DEV, D), BF16), ((CHUNK, D), BF16), ((TILE_DEV - CHUNK, D), BF16))
    return call(embed_kernel, "embed_rows", shapes, "svvhh-vvv", scratch, 1_400_000_000, 9_000_000)(*args)


def key_picks(table, h, first, block_rows):
    rate, base = table[RATE], table[PAIR_START]
    place = iota((KEY_SLOTS, TILE_DEV), 0) * rate + ((h - base) & (rate - 1)) + (base - first)
    return (block_rows == place).astype(BF16)


def live_rows(rows, lane, count):
    return jnp.where(lane < count, rows, -SEQ_LEN)


def key_rows(kv, h):
    rest = jnp.zeros((LANES - 2 * HEAD_DIM, TILE_DEV), BF16)
    return jnp.concatenate([kv[head_rows(h)], kv[head_rows(HEADS + h)], rest], axis=0)


def head_rows(h):
    return slice(h * HEAD_DIM, (h + 1) * HEAD_DIM)


def segments(table, position):
    length = jnp.full((1, 1), table[SEGMENT], I32).astype(F32)
    return jnp.floor((position.astype(F32) + 0.5) / length)


def own_kernel(table, own, q_a, q_b, payload, q_out, kv_out, out_sum, out_best, out_total):
    rate, start_me, count_me = table[RATE], table[START_ME], table[COUNT_ME]
    first, second = halves(table, own, D // 2)
    q_out[...] = (dot_nt(q_a[:D], first) + dot_nt(q_b[:D], second)).astype(BF16)
    kv_out[...] = (dot_nt(q_a[D:], first) + dot_nt(q_b[D:], second)).astype(BF16)
    slot = iota((SLOTS, TILE_DEV), 0) * rate
    lane = iota((SLOTS, TILE_DEV), 1)
    rest = jnp.zeros((LANES - HEAD_DIM, TILE_DEV), BF16)
    wide_lane = iota((KEY_SLOTS, TILE_DEV), 1)
    block_rows = live_rows(wide_lane, wide_lane, count_me)
    for h in range(HEADS):
        payload[h, :KEY_SLOTS] = dot_nt(key_picks(table, h, start_me, block_rows), key_rows(kv_out, h)).astype(BF16)
        pick = (lane == slot + ((h - start_me) & (rate - 1))).astype(BF16)
        ask = jnp.concatenate([q_out[head_rows(h)], rest], axis=0)
        payload[h, KEY_SLOTS:] = dot_nt(pick, ask).astype(BF16)
    key_at = iota((TILE_DEV, 1), 0)
    key_seg = jnp.where(key_at < count_me, segments(table, start_me + key_at), -1.0)
    allowed = key_seg == segments(table, start_me + iota((1, TILE_DEV), 1))
    for h in range(HEADS):
        rows = head_rows(h)
        scores = jnp.where(allowed, dot_tn(kv_out[rows], q_out[rows]) * SCALE, BIG_NEGATIVE)
        best = jnp.max(scores, axis=0, keepdims=True)
        weights = jnp.exp(scores - best)
        out_best[h : h + 1] = best
        out_total[h : h + 1] = jnp.sum(weights, axis=0, keepdims=True)
        out_sum[rows] = dot_nn(kv_out[head_rows(HEADS + h)], weights.astype(BF16))


def own_rows(*args):
    stat = ((HEADS, TILE_DEV), F32)
    pay = ((HEADS, KEY_SLOTS + SLOTS, LANES), BF16)
    shapes = (pay, ((D, TILE_DEV), BF16), ((2 * D, TILE_DEV), BF16), ((D, TILE_DEV), F32), stat, stat)
    return call(own_kernel, "own_rows", shapes, "svvv-vvvvvv", [], 1_000_000_000, 5_000_000, 600_000)(*args)


def pair_kernel(table, lower, upper, halo, q_a, q_b, own_payload, payload, rim, far_rim, kv, partner):
    partner[:CHUNK] = lower[...]
    partner[CHUNK:] = upper[...]
    first, second = halves(table, partner, D // 2)
    kv[...] = (dot_nt(q_a[D:], first) + dot_nt(q_b[D:], second)).astype(BF16)
    count, upward = table[COUNT_OTHER], table[HIGH] == 0
    lane = iota((KEY_SLOTS, TILE_DEV), 1)
    turned = jnp.where(lane < CHUNK, lane + (count - CHUNK), lane - CHUNK)
    block_rows = live_rows(jnp.where(upward, turned, lane), lane, count)
    for h in range(HEADS):
        picks = key_picks(table, h, table[START_OTHER], block_rows)
        both = dot_nt(picks, key_rows(kv, h)) + own_payload[h, :KEY_SLOTS].astype(F32)
        payload[h, :KEY_SLOTS] = both.astype(BF16)
        payload[h, KEY_SLOTS:] = own_payload[h, KEY_SLOTS:]
    rim_first = jnp.where(upward, CHUNK, count - HALF)
    pick = (iota((TILE_DEV, HALF), 0) == iota((TILE_DEV, HALF), 1) + rim_first).astype(BF16)
    rim[...] = dot_nn(kv[...], pick).astype(BF16)
    first, second = halves(table, halo, D // 2)
    far_rim[...] = (dot_nt(q_a[D:], first) + dot_nt(q_b[D:], second)).astype(BF16)


def pair_rows(*args):
    rim = ((2 * D, HALF), BF16)
    shapes = (((HEADS, KEY_SLOTS + SLOTS, LANES), BF16), rim, rim)
    scratch = [pltpu.VMEM((2 * D, TILE_DEV), BF16), pltpu.VMEM((TILE_DEV, D), BF16)]
    return call(pair_kernel, "pair_rows", shapes, "svvvvvv-vvv", scratch, 700_000_000, 4_000_000)(*args)


def rim_kernel(table, q, near_rim, far_rim, own_sum, own_best, own_total, out_sum, out_best, out_total):
    start_me, end_me = table[START_ME], table[START_ME] + table[COUNT_ME]
    query_seg = segments(table, start_me + iota((1, TILE_DEV), 1))

    def allowed(begin):
        at = begin + iota((HALF, 1), 0)
        return jnp.where((at >= 0) & (at < SEQ_LEN), segments(table, at), -1.0) == query_seg

    upper = table[HIGH] == 0
    near_ok = allowed(jnp.where(upper, end_me, start_me - HALF))
    far_ok = allowed(jnp.where(upper, start_me - HALF, end_me))
    for h in range(HEADS):
        rows, v_rows = head_rows(h), head_rows(HEADS + h)
        near = jnp.where(near_ok, dot_tn(near_rim[rows], q[rows]) * SCALE, BIG_NEGATIVE)
        far = jnp.where(far_ok, dot_tn(far_rim[rows], q[rows]) * SCALE, BIG_NEGATIVE)
        best_o = own_best[h : h + 1]
        best = jnp.maximum(jnp.max(jnp.maximum(near, far), axis=0, keepdims=True), best_o)
        near, far, scale = jnp.exp(near - best), jnp.exp(far - best), jnp.exp(best_o - best)
        out_best[h : h + 1] = best
        out_total[h : h + 1] = jnp.sum(near + far, axis=0, keepdims=True) + scale * own_total[h : h + 1]
        summed = dot_nn(near_rim[v_rows], near.astype(BF16)) + dot_nn(far_rim[v_rows], far.astype(BF16))
        out_sum[rows] = summed + scale * own_sum[rows]


def rim_rows(*args):
    stat = ((HEADS, TILE_DEV), F32)
    shapes = (((D, TILE_DEV), F32), stat, stat)
    return call(rim_kernel, "rim_rows", shapes, "svvvvvv-vvv", [], 200_000_000, 2_500_000, 400_000)(*args)


def far_kernel(table, arrived, answer, scores):
    rate = table[RATE]
    kv = arrived[:, :KEY_SLOTS].reshape(PLANES * KEY_SLOTS, LANES)
    group = 8
    width = group * SLOTS
    slot = iota((KEY_SLOTS, width), 0) * rate
    for n in range(PLANES // group):
        asks = arrived[n * group : (n + 1) * group, KEY_SLOTS:].reshape(width, LANES)
        best = jnp.full((1, width), BIG_NEGATIVE, F32)
        for p in range(PLANES):
            phase = (table[PLANE_ID] - table[ALL_STARTS + p]) & (rate - 1)
            piece = dot_nt(arrived[p, :KEY_SLOTS], asks) * SCALE
            piece = jnp.where(slot + phase < table[ALL_COUNTS + p], piece, BIG_NEGATIVE)
            scores[p * KEY_SLOTS : (p + 1) * KEY_SLOTS] = piece
            best = jnp.maximum(best, jnp.max(piece, axis=0, keepdims=True))
        weights = jnp.exp(scores[...] - best)
        total = jnp.sum(weights, axis=0, keepdims=True)
        summed = dot_tn(kv, weights.astype(BF16))
        shared = summed[HEAD_DIM : 2 * HEAD_DIM] / total
        log_all = best + jnp.log(total)
        log_a = log_all.astype(BF16).astype(F32)
        log_b = (log_all - log_a).astype(BF16).astype(F32)
        log_c = log_all - log_a - log_b
        row = iota((LANES - HEAD_DIM, width), 0)
        tail = jnp.where(row == 0, log_a, jnp.where(row == 1, log_b, jnp.where(row == 2, log_c, 0.0)))
        block = jnp.concatenate([shared, tail], axis=0)
        answer[n * group : (n + 1) * group] = block.T.astype(BF16).reshape(group, SLOTS, LANES)


def far_branch(*args):
    shapes = (((PLANES, SLOTS, LANES), BF16),)
    scratch = [pltpu.VMEM((PLANES * KEY_SLOTS, PLANES // 2 * SLOTS), F32)]
    return call(far_kernel, "far_branch", shapes, "sv-v", scratch, 500_000_000, 1_000_000, 1_000_000)(*args)[0]


def finish_kernel(table, answers, local_sum, local_best, local_total, listing, out, attended):
    rate = table[RATE]
    slot = iota((SLOTS, TILE_DEV), 0) * rate
    lane = iota((SLOTS, TILE_DEV), 1)
    row = iota((1, TILE_DEV), 1)
    live = row < table[COUNT_ME]
    for h in range(HEADS):
        rows = slice(h * HEAD_DIM, (h + 1) * HEAD_DIM)
        phase = (h - table[START_ME]) & (rate - 1)
        pick = (lane == slot + phase).astype(BF16)
        wide = dot_tn(answers[h], pick)
        log_all = wide[HEAD_DIM : HEAD_DIM + 1] + wide[HEAD_DIM + 1 : HEAD_DIM + 2] + wide[HEAD_DIM + 2 : HEAD_DIM + 3]
        log_all = jnp.where((row & (rate - 1)) == phase, log_all, BIG_NEGATIVE)
        best = local_best[h : h + 1]
        joint = jnp.maximum(best, log_all)
        near = jnp.exp(best - joint)
        far = jnp.exp(log_all - joint)
        below = jnp.where(live, near * local_total[h : h + 1] + far, 1.0)
        mixed = (near * local_sum[rows] + far * wide[:HEAD_DIM]) / below
        attended[rows] = jnp.where(live, mixed, 0.0).astype(BF16)
    back = (listing[0] == iota((TILE_DEV, TILE_DEV), 0)).astype(BF16)
    out[0] = dot_nt(back, attended[...]).astype(BF16)


def finish(*args):
    shapes = (((1, TILE_DEV, D), BF16),)
    scratch = [pltpu.VMEM((D, TILE_DEV), BF16)]
    return call(finish_kernel, "finish_rows", shapes, "svvvvv-v", scratch, 100_000_000, 1_500_000, 10_000)(*args)[0]


def mirrored(x):
    z_low = lax.axis_size("zlo")
    pairs = [
        (low * 2 + high, (z_low - 1 - low) * 2 + (1 - high))
        for low in range(z_low)
        for high in range(2)
    ]
    return lax.ppermute(x, ("zlo", "zhi"), pairs)


def along_z(x, part):
    z_low = lax.axis_size("zlo")

    def rank(z, core):
        return (z % z_low * 2 + core) * 2 + z // z_low

    half = z_low // 2 if part == 0 else z_low - z_low // 2
    pairs = []
    for z in range(2 * z_low):
        for core in range(2):
            step = half if core == 0 else -half
            pairs.append((rank(z, core), rank((z + step) % (2 * z_low), core)))
    return lax.ppermute(x, ("zlo", "core", "zhi"), pairs)


def other_core(x):
    return lax.ppermute(x, "core", [(0, 1), (1, 0)])


def over_plane(x):
    return lax.all_to_all(x, PLANE, 0, 0)


def hold(*values):
    return lax.optimization_barrier(values)


def copies(x):
    return jnp.broadcast_to(x[None], (PLANES,) + x.shape)


def along_lines(x, stage):
    groups = []
    for low in range(lax.axis_size("zlo")):
        for core in range(2):
            for high in range(2):
                for line in range(4):
                    across_x = (core == 0) == (stage == 0)
                    plane = [line * 4 + k if across_x else k * 4 + line for k in range(4)]
                    groups.append([((low * 2 + core) * PLANES + p) * 2 + high for p in plane])
    spread = jnp.broadcast_to(x[None], (4,) + x.shape)
    return lax.all_to_all(spread, EVERY, 0, 0, axis_index_groups=groups)


def in_order(own, other, high):
    return jnp.where(high == 0, jnp.concatenate([own, other]), jnp.concatenate([other, own]))


def on_device(ctx_in, resid, enc_out_w, slide_proj, qkv_w, tissue, kept_count, dilation):
    core = lax.axis_index("core")
    high = lax.axis_index("zhi")
    plane_id = lax.axis_index("y") * lax.axis_size("x") + lax.axis_index("x")

    w_own = lax.dynamic_slice_in_dim(enc_out_w, core * D, D, 0).T
    p_own = lax.dynamic_slice_in_dim(slide_proj, core * D, D, 0).T
    q_own = lax.dynamic_slice_in_dim(qkv_w, core * (D // 2), D // 2, 0).T
    other_wp = mirrored(jnp.concatenate([w_own, p_own]))
    q_other = mirrored(q_own)
    place = jnp.stack([core, high, plane_id]).astype(I32)
    own_ctx, own_res, table = prepare(place, kept_count, dilation, ctx_in, resid, tissue)
    wp = jnp.concatenate(
        [in_order(w_own, other_wp[:W_ROWS], high), in_order(p_own, other_wp[W_ROWS:], high)]
    )
    wp = along_lines(along_lines(wp, 0).reshape(-1, D), 1).reshape(PLANES, -1, D)
    q_both = copies(in_order(q_own, q_other, high))
    wp, q_both = hold(wp, q_both)
    q_a = over_plane(q_both)
    embedded, lower, upper = embed(table, own_ctx, own_res, wp, other_core(wp))
    lower = along_z(along_z(lower, 0), 1)
    upper = along_z(upper, 0)
    q_a, embedded, lower, upper = hold(q_a, embedded, lower, upper)
    q_a = q_a.reshape(3 * D, D // 2)
    q_b = other_core(q_a)
    upper = along_z(upper, 1)
    own_payload, q_rows, _, own_sum, own_best, own_total = own_rows(table, embedded, q_a, q_b)
    halo_pairs = [(p * 2, p * 2 + 2) for p in range(PLANES - 1)]
    halo_pairs += [(p * 2 + 1, p * 2 - 1) for p in range(1, PLANES)]
    halo = lax.ppermute(lower, SEQ, halo_pairs)
    upper, own_payload, halo = hold(upper, own_payload, halo)
    payload, near_rim, far_rim = pair_rows(table, lower, upper, halo, q_a, q_b, own_payload)
    arrived = lax.all_to_all(payload, PLANE, 0, 0)
    local_sum, local_best, local_total = rim_rows(
        table, q_rows, near_rim, far_rim, own_sum, own_best, own_total
    )
    answer = far_branch(table, arrived)
    answers = lax.all_to_all(answer, PLANE, 0, 0)
    return finish(table, answers, local_sum, local_best, local_total, tissue)


def solution(mesh):
    devices = mesh.devices.reshape(-1, 2, 4, 4, 2)
    split = Mesh(devices, ("zlo", "core", "y", "x", "zhi"))
    slide, seq = ("zlo", "core"), ("y", "x", "zhi")
    return jax.shard_map(
        on_device,
        mesh=split,
        in_specs=(
            P(slide, seq, None),
            P(slide, seq, None),
            P(None, seq),
            P(None, seq),
            P(None, seq),
            P(slide, seq, None),
            P(slide, None),
            P(slide, None),
        ),
        out_specs=P(slide, seq, None),
        check_vma=False,
    )
```
